32 devices in a mesh: seq: 2 (over x), mp: 4 (over y, core), dp: 4 (over z).
Axes of the slice: x: 2, y: 2, z: 4, core: 2. Of those that a mesh axis runs over, the one named last changes fastest.
Arguments:
- block_input: bfloat16 [4, 2048, 1280], P('dp', 'seq', 'mp'), may hold values from -6 to 6
- conv_weight: bfloat16 [5, 1280, 1536], P(None, None, 'mp'), as said below
- norm_gain: float32 [1536], P('mp'), may hold values from 0.1 to 1.9
- qkv_weight: bfloat16 [1536, 2560], P(None, 'mp'), may hold values from -0.15625 to 0.15625
- encoder_grad: bfloat16 [4, 1024, 1536], P('dp', 'seq', 'mp'), may hold values from -6 to 6
Outputs:
- qkv: bfloat16 [4, 1024, 2560], P('dp', 'seq', 'mp')
- conv_grad: float32 [1280, 5, 1536], P('seq', None, 'mp')
The draws below stay inside these ranges and needn't reach their ends.
Inputs may be any that keep to these rules, and one draw needn't show every extreme that they name: `conv_weight`: output channel o's kernel column carries a scale factor that varies with o; input channels differ in scale.
All inputs are finite; a program needn't handle non-finite values.
Results may differ from the reference program's by a relative error of at most 0.019.
Values may be sent and summed in bfloat16 or wider, within the bound.
No kernel may reach another device: no remote copies, remote signals or barrier semaphores. Data moves between devices by JAX's collectives and lax.ppermute only.
A program may use at most 64 MiB of HBM per device.

```python
import jax
import jax.numpy as jnp
from jax import lax

CIN = 1280
COUT = 1536
KW = 5
QKVW = 2560
ROWS = 1024
LIN = 2048
BATCH = 4


def draw_conv_weight(key, part):
    k_base, k_rows, k_cols = jax.random.split(key, 3)
    base = jax.random.normal(k_base, (KW, CIN, COUT), jnp.float32)
    rows = jnp.exp(jax.random.uniform(k_rows, (1, CIN, 1), jnp.float32, 0.0, 2.302585))
    ramp = 3.0 ** (jnp.arange(COUT, dtype=jnp.float32) / COUT)
    cols = ramp.reshape(1, 1, COUT) * jnp.exp(jax.random.uniform(k_cols, (1, 1, COUT), jnp.float32, 0.0, 1.0986))
    weight = base * rows * cols / (5.0 * jnp.sqrt(jnp.float32(KW * CIN)))
    return weight.astype(jnp.bfloat16)


def shard_levels(rng, extent, pieces, least, high):
    gain, own = 1.0, jax.random.fold_in(rng, 6)
    for dim, parts in pieces:
        draws = jnp.exp(jax.random.uniform(jax.random.fold_in(own, dim), (parts,), jnp.float32, least / len(pieces), high / len(pieces)))
        gain = gain * jnp.repeat(draws, extent[dim] // parts).reshape([-1 if axis == dim else 1 for axis in range(len(extent))])
    return gain


def bell_draw(key, shape, scale, limit, cuts=(), held_as=jnp.bfloat16):
    values = scale * jax.random.normal(key, shape, jnp.float32)
    if cuts:
        values = values * shard_levels(key, shape, cuts, -0.22, 0.18)
    return jnp.clip(values, -limit, limit).astype(held_as)


def setup_inputs(seed: int = 0) -> dict:
    arg_keys = jax.random.split(jax.random.key(seed), 6)
    return {
        "block_input": bell_draw(arg_keys[0], (BATCH, LIN, CIN), 1.0, 6.0, ((0, 4), (1, 2), (2, 4))),
        "conv_weight": draw_conv_weight(jax.random.fold_in(arg_keys[5], 71), 0),
        "norm_gain": jnp.clip(1.0 + 0.18 * jax.random.normal(arg_keys[2], (COUT,), jnp.float32), 0.1, 1.9),
        "qkv_weight": bell_draw(arg_keys[3], (COUT, QKVW), COUT ** -0.5, 0.15625, ((1, 4),)),
        "encoder_grad": bell_draw(arg_keys[4], (BATCH, ROWS, COUT), 1.0, 6.0, ((0, 4), (1, 2), (2, 4))),
    }


def gelu_value(v):
    u = 0.7978845608 * (v + 0.044715 * v * v * v)
    return 0.5 * v * (1.0 + jnp.tanh(u))

def gelu_slope(v):
    u = 0.7978845608 * (v + 0.044715 * v * v * v)
    th = jnp.tanh(u)
    return 0.5 * (1.0 + th) + 0.5 * v * (1.0 - th * th) * 0.7978845608 * (1.0 + 0.134145 * v * v)

def one_sequence(inputs):
    seq_input, seq_grad, conv_weight, norm_gain, qkv_weight = inputs
    padded = jnp.pad(seq_input, ((2, 2), (0, 0)))
    length = seq_input.shape[0]
    pre = jnp.zeros((length, conv_weight.shape[2]), jnp.float32)
    for k in range(KW):
        pre = pre + jnp.dot(padded[k:k + length], conv_weight[k], preferred_element_type=jnp.float32)
    act = gelu_value(pre)
    encoded = (0.5 * (act[0::2] + act[1::2])).astype(jnp.bfloat16)
    values = encoded.astype(jnp.float32)
    mean = lax.optimization_barrier(jnp.sum(values, axis=1, keepdims=True)) / COUT
    meansq = lax.optimization_barrier(jnp.sum(values * values, axis=1, keepdims=True)) / COUT
    var = meansq - mean * mean
    normalized = ((values - mean) * lax.rsqrt(var + 1e-05) * norm_gain).astype(jnp.bfloat16)
    qkv = jnp.dot(normalized, qkv_weight, preferred_element_type=jnp.float32).astype(jnp.bfloat16)
    spread = jnp.repeat(seq_grad.astype(jnp.float32), 2, axis=0)
    pre_grad = (gelu_slope(pre) * 0.5 * spread).astype(jnp.bfloat16)
    terms = [lax.dot_general(padded[k:k + length], pre_grad, (((0,), (0,)), ((), ())), preferred_element_type=jnp.float32) for k in range(KW)]
    return (qkv, jnp.stack(terms, axis=1))

def reference(block_input, conv_weight, norm_gain, qkv_weight, encoder_grad):

    def step(carry, index):
        qkv, grad = one_sequence((block_input[index], encoder_grad[index], conv_weight, norm_gain, qkv_weight))
        return (carry + grad, qkv)
    start = jnp.zeros((CIN, KW, COUT), jnp.float32)
    conv_grad, qkv = lax.scan(step, start, jnp.arange(BATCH, dtype=jnp.int32))
    return (qkv, conv_grad)
```

```python
import functools

import jax
import jax.numpy as jnp
from jax import lax
from jax.experimental import pallas as pl
from jax.experimental.pallas import tpu as pltpu
from jax.sharding import PartitionSpec as P

EDGE = 8
LANES = 128
VMEM_BYTES = 56 * 1024 * 1024
F32 = jnp.float32
BF16 = jnp.bfloat16


def gelu_parts(v):
    u = 0.7978845608 * (v + 0.044715 * v * v * v)
    th = jnp.tanh(u)
    value = 0.5 * v * (1.0 + th)
    slope = 0.5 * (1.0 + th) + 0.5 * v * (1.0 - th * th) * 0.7978845608 * (1.0 + 0.134145 * v * v)
    return value, slope


def swap(value, axis, bit):
    peers = lax.axis_size(axis)
    return lax.ppermute(value, axis, [(i, i ^ bit) for i in range(peers)])


def conv_rows(offsets, me, x_refs, halo_refs, w_ref, rows_scr, y_scr):
    taps, width = w_ref.shape[0], w_ref.shape[2]
    depth, length = x_refs[0].shape
    x = jnp.concatenate([ref[...] for ref in x_refs], axis=0)
    halo = jnp.concatenate([ref[...] for ref in halo_refs], axis=0)
    rows_scr[0:length, :] = x.T
    rows_scr[length : length + 16, :] = halo.T[0:16]
    starts = [pl.multiple_of((me ^ off) * depth, 16) for off in offsets]
    for first in range(0, taps, 2):
        group = range(first, min(first + 2, taps))
        w = jnp.concatenate(
            [
                jnp.concatenate([w_ref[k, pl.ds(s, depth), :] for s in starts], axis=0)
                for k in group
            ],
            axis=1,
        )
        y = jnp.dot(rows_scr[...], w, preferred_element_type=F32)
        for c in range(w.shape[1] // LANES):
            part = y[:, c * LANES : (c + 1) * LANES]
            at = first * width // LANES + c
            y_scr[at, EDGE : EDGE + length, :] = part[0:length]
            y_scr[at, EDGE - 2 : EDGE, :] = part[length : length + 2]
            y_scr[at, EDGE + length : EDGE + length + 2, :] = part[length + 2 : length + 4]


def tap_sum(y_scr, start, count, phase, taps, c):
    total = None
    for k in range(taps):
        at = k * (y_scr.shape[0] // taps) + c
        part = y_scr[at, pl.ds(EDGE + 2 * start + phase + k - 2, count, stride=2), :]
        total = part if total is None else total + part
    return total


def first_kernel(offsets, idx_ref, *refs):
    n = len(offsets)
    x_refs, halo_refs, (w_ref, even_ref, odd_ref, rows_scr, y_scr) = refs[:n], refs[n : 2 * n], refs[2 * n :]
    conv_rows(offsets, idx_ref[0], x_refs, halo_refs, w_ref, rows_scr, y_scr)
    taps, width = w_ref.shape[0], w_ref.shape[2]
    half = even_ref.shape[0]
    step = min(64, half)
    for start in range(0, half, step):
        rows = slice(start, start + step)
        for c in range(width // LANES):
            lanes = slice(c * LANES, (c + 1) * LANES)
            even_ref[rows, lanes] = tap_sum(y_scr, start, step, 0, taps, c)
            odd_ref[rows, lanes] = tap_sum(y_scr, start, step, 1, taps, c)


def second_kernel(offsets, idx_ref, *refs):
    n = len(offsets)
    x_refs, halo_refs = refs[:n], refs[n : 2 * n]
    w_ref, even_ref, odd_ref, grad_ref, enc_ref, pre_ref, rows_scr, y_scr, p_scr = refs[2 * n :]
    conv_rows(offsets, idx_ref[0], x_refs, halo_refs, w_ref, rows_scr, y_scr)
    taps, width = w_ref.shape[0], w_ref.shape[2]
    half = even_ref.shape[0]
    step = min(64, half)
    length = 2 * half
    zero = jnp.zeros((EDGE, width), F32)
    pre_ref[0:EDGE, :] = zero
    pre_ref[EDGE + length : 2 * EDGE + length, :] = zero
    for start in range(0, half, step):
        rows = slice(start, start + step)
        for c in range(width // LANES):
            lanes = slice(c * LANES, (c + 1) * LANES)
            even = even_ref[rows, lanes] + tap_sum(y_scr, start, step, 0, taps, c)
            odd = odd_ref[rows, lanes] + tap_sum(y_scr, start, step, 1, taps, c)
            act_even, slope_even = gelu_parts(even)
            act_odd, slope_odd = gelu_parts(odd)
            enc_ref[rows, lanes] = (0.5 * (act_even + act_odd)).astype(BF16)
            spread = grad_ref[rows, lanes].astype(F32)
            p_scr[c, pl.ds(2 * start, step, stride=2), :] = slope_even * 0.5 * spread
            p_scr[c, pl.ds(2 * start + 1, step, stride=2), :] = slope_odd * 0.5 * spread
    for c in range(width // LANES):
        lanes = slice(c * LANES, (c + 1) * LANES)
        pre_ref[EDGE : EDGE + length, lanes] = p_scr[c].astype(BF16).astype(F32)


def grad_kernel(offsets, tap, shards, idx_ref, *refs):
    n = len(offsets)
    x_refs, halo_refs, (p_ref, *out_refs, edge_scr) = refs[:n], refs[n : 2 * n], refs[2 * n :]
    depth, length = x_refs[0].shape
    edge_scr[...] = jnp.zeros_like(edge_scr)
    edge_scr[0:2, :] = p_ref[EDGE - tap : EDGE - tap + 2, :]
    edge_scr[2:4, :] = p_ref[EDGE + length + 2 - tap : EDGE + length + 4 - tap, :]
    p = p_ref[EDGE + 2 - tap : EDGE + 2 - tap + length, :].astype(BF16)
    edge = edge_scr[...].astype(BF16)
    me = idx_ref[0]
    x = jnp.concatenate([ref[...] for ref in x_refs], axis=0)
    halo = jnp.concatenate([ref[...] for ref in halo_refs], axis=0)
    res = jnp.dot(x, p, preferred_element_type=F32) + jnp.dot(halo, edge, preferred_element_type=F32)
    res = res.astype(BF16)
    for j, off in enumerate(offsets):
        part = res[j * depth : (j + 1) * depth]
        at = me ^ off
        if len(out_refs) == 1:
            out_refs[0][pl.ds(pl.multiple_of(at * depth, 16), depth), :] = part
            continue
        per = n // shards
        row = pl.multiple_of(lax.rem(at, per) * depth, 16)
        mine = lax.div(at, per) == idx_ref[1]

        @pl.when(mine)
        def _():
            out_refs[0][pl.ds(row, depth), :] = part

        @pl.when(jnp.logical_not(mine))
        def _():
            out_refs[1][pl.ds(row, depth), :] = part


def qkv_kernel(offsets, idx_ref, *refs):
    n = len(offsets)
    enc_refs, gain_refs, (w_ref, out_ref) = refs[:n], refs[n : 2 * n], refs[2 * n :]
    depth = enc_refs[0].shape[1]
    values = [ref[...].astype(F32) for ref in enc_refs]
    channels = n * depth
    sums = sum(jnp.sum(v, axis=1, keepdims=True) for v in values)
    squares = sum(jnp.sum(v * v, axis=1, keepdims=True) for v in values)
    mean = sums / channels
    var = squares / channels - mean * mean
    scale = lax.rsqrt(var + 1e-05)
    total = None
    for off, v, gain_ref in zip(offsets, values, gain_refs):
        normal = ((v - mean) * scale * gain_ref[...]).astype(BF16)
        w = w_ref[pl.ds(pl.multiple_of((idx_ref[0] ^ off) * depth, 16), depth), :]
        part = jnp.dot(normal, w, preferred_element_type=F32)
        total = part if total is None else total + part
    out_ref[...] = total.astype(BF16)


def call(kernel, out, scratch, idx, *arrays):
    vmem = pl.BlockSpec(memory_space=pltpu.VMEM)
    return pl.pallas_call(
        kernel,
        out_shape=out,
        in_specs=[pl.BlockSpec(memory_space=pltpu.SMEM)] + [vmem] * len(arrays),
        out_specs=jax.tree.map(lambda _: vmem, out),
        scratch_shapes=scratch,
        compiler_params=pltpu.CompilerParams(vmem_limit_bytes=VMEM_BYTES),
    )(idx, *arrays)


def edge_columns(x):
    peers = lax.axis_size("seq")
    up = [(i, (i + 1) % peers) for i in range(peers - 1)]
    down = [(j, i) for i, j in up]
    length = x.shape[1]
    before = lax.ppermute(x[:, length - 2 :], "seq", up)
    after = lax.ppermute(x[:, :2], "seq", down)
    return jnp.concatenate([before, after], axis=1)


def gathered(value, axis, bits):
    blocks, offsets = [value], [0]
    for bit in bits:
        blocks = blocks + [swap(b, axis, bit) for b in blocks]
        offsets = offsets + [o ^ bit for o in offsets]
    return blocks, offsets


def chain_sum(part, axis):
    peers = lax.axis_size(axis)
    if peers % 2:
        return lax.psum(part, axis)
    me = lax.axis_index(axis)
    half = peers // 2
    total = part
    for i in range(half - 1):
        got = lax.ppermute(total, axis, [(i, i + 1), (peers - 1 - i, peers - 2 - i)])
        total = (total.astype(F32) + got.astype(F32)).astype(BF16)
    got = lax.ppermute(total, axis, [(half - 1, half), (half, half - 1)])
    total = (total.astype(F32) + got.astype(F32)).astype(BF16)
    for i in reversed(range(half - 1)):
        got = lax.ppermute(total, axis, [(i + 1, i), (peers - 2 - i, peers - 1 - i)])
        total = jnp.where(jnp.logical_or(me == i, me == peers - 1 - i), got, total)
    return total


def on_device(block_input, conv_weight, norm_gain, qkv_weight, encoder_grad):
    x = jnp.swapaxes(block_input[0], 0, 1)
    depth, length = x.shape
    taps, _, width = conv_weight.shape
    peers, shards = lax.axis_size("mp"), lax.axis_size("seq")
    bits = [1 << b for b in reversed(range(peers.bit_length() - 1))]
    idx = jnp.stack([lax.axis_index("mp"), lax.axis_index("seq")]).astype(jnp.int32)

    blocks, offsets = gathered(x, "mp", bits)
    edges, _ = gathered(edge_columns(x), "mp", bits)
    halos = [jnp.pad(e, ((0, 0), (0, LANES - e.shape[1]))) for e in edges]
    gains, _ = gathered(norm_gain.reshape(1, -1), "mp", bits)

    near = [j for j, o in enumerate(offsets) if o < 2]
    far = [j for j, o in enumerate(offsets) if o >= 2]
    half = length // 2
    pick = lambda items, at: [items[j] for j in at]
    scratch = lambda at: [
        pltpu.VMEM((length + 16, len(at) * depth), BF16),
        pltpu.VMEM((taps * width // LANES, length + 2 * EDGE, LANES), F32),
    ]
    part = jax.ShapeDtypeStruct((half, width), F32)
    even, odd = call(
        functools.partial(first_kernel, pick(offsets, near)),
        (part, part),
        scratch(near),
        idx, *pick(blocks, near), *pick(halos, near), conv_weight,
    )
    encoded, pre_grad = call(
        functools.partial(second_kernel, pick(offsets, far)),
        (jax.ShapeDtypeStruct((half, width), BF16), jax.ShapeDtypeStruct((length + 2 * EDGE, width), F32)),
        scratch(far) + [pltpu.VMEM((width // LANES, length, LANES), F32)],
        idx, *pick(blocks, far), *pick(halos, far), conv_weight, even, odd, encoder_grad[0],
    )

    total = peers * depth
    pair = shards == 2 and peers % shards == 0
    rows = total // shards if pair else total
    sums = []
    for k in range(taps):
        outs = call(
            functools.partial(grad_kernel, offsets, k, shards),
            (jax.ShapeDtypeStruct((rows, width), BF16),) * (2 if pair else 1),
            [pltpu.VMEM((LANES, width), F32)],
            idx, *blocks, *halos, pre_grad,
        )
        if pair:
            got = swap(outs[1], "seq", 1)
            share = (outs[0].astype(F32) + got.astype(F32)).astype(BF16)
        else:
            share = lax.psum_scatter(outs[0], "seq", scatter_dimension=0, tiled=True)
        sums.append(chain_sum(share, "dp"))
    conv_grad = jnp.stack([s.astype(F32) for s in sums], axis=1)

    encs, _ = gathered(encoded, "mp", bits)
    qkv = call(
        functools.partial(qkv_kernel, offsets),
        jax.ShapeDtypeStruct((half, qkv_weight.shape[1]), BF16),
        [],
        idx, *encs, *gains, qkv_weight,
    )
    return (qkv[None], conv_grad)


def solution(mesh):
    return jax.shard_map(
        on_device,
        mesh=mesh,
        in_specs=(
            P("dp", "seq", "mp"),
            P(None, None, "mp"),
            P("mp"),
            P(None, "mp"),
            P("dp", "seq", "mp"),
        ),
        out_specs=(P("dp", "seq", "mp"), P("seq", None, "mp")),
        check_vma=False,
    )
```

```python
import functools

import jax
import jax.numpy as jnp
from jax import lax
from jax.experimental import pallas as pl
from jax.experimental.pallas import tpu as pltpu
from jax.sharding import PartitionSpec as P

EDGE = 8
LANES = 128
F32 = jnp.float32
BF16 = jnp.bfloat16


def gelu_parts(v):
    u = 0.7978845608 * (v + 0.044715 * v * v * v)
    th = jnp.tanh(u)
    value = 0.5 * v * (1.0 + th)
    slope = 0.5 * (1.0 + th) + 0.5 * v * (1.0 - th * th) * 0.7978845608 * (1.0 + 0.134145 * v * v)
    return value, slope


def swap(value, axis, bit):
    peers = lax.axis_size(axis)
    return lax.ppermute(value, axis, [(i, i ^ bit) for i in range(peers)])


def conv_rows(offsets, me, x_refs, halo_refs, w_ref, rows_scr, y_scr):
    taps, width = w_ref.shape[0], w_ref.shape[2]
    depth, length = x_refs[0].shape
    x = jnp.concatenate([ref[...] for ref in x_refs], axis=0)
    halo = jnp.concatenate([ref[...] for ref in halo_refs], axis=0)
    rows_scr[0:length, :] = x.T
    rows_scr[length : length + 16, :] = halo.T[0:16]
    starts = [pl.multiple_of((me ^ off) * depth, 16) for off in offsets]
    for first in range(0, taps, 2):
        group = range(first, min(first + 2, taps))
        w = jnp.concatenate(
            [
                jnp.concatenate([w_ref[k, pl.ds(s, depth), :] for s in starts], axis=0)
                for k in group
            ],
            axis=1,
        )
        y = jnp.dot(rows_scr[...], w, preferred_element_type=F32)
        for c in range(w.shape[1] // LANES):
            part = y[:, c * LANES : (c + 1) * LANES]
            at = first * width // LANES + c
            y_scr[at, EDGE : EDGE + length, :] = part[0:length]
            y_scr[at, EDGE - 2 : EDGE, :] = part[length : length + 2]
            y_scr[at, EDGE + length : EDGE + length + 2, :] = part[length + 2 : length + 4]


def tap_sum(y_scr, start, count, phase, taps, c):
    total = None
    for k in range(taps):
        at = k * (y_scr.shape[0] // taps) + c
        part = y_scr[at, pl.ds(EDGE + 2 * start + phase + k - 2, count, stride=2), :]
        total = part if total is None else total + part
    return total


def first_kernel(offsets, idx_ref, *refs):
    n = len(offsets)
    x_refs, halo_refs, (w_ref, even_ref, odd_ref, rows_scr, y_scr) = refs[:n], refs[n : 2 * n], refs[2 * n :]
    conv_rows(offsets, idx_ref[0], x_refs, halo_refs, w_ref, rows_scr, y_scr)
    taps, width = w_ref.shape[0], w_ref.shape[2]
    half = even_ref.shape[0]
    step = min(64, half)
    for start in range(0, half, step):
        rows = slice(start, start + step)
        for c in range(width // LANES):
            lanes = slice(c * LANES, (c + 1) * LANES)
            even_ref[rows, lanes] = tap_sum(y_scr, start, step, 0, taps, c)
            odd_ref[rows, lanes] = tap_sum(y_scr, start, step, 1, taps, c)


def second_kernel(offsets, idx_ref, *refs):
    n = len(offsets)
    x_refs, halo_refs = refs[:n], refs[n : 2 * n]
    w_ref, even_ref, odd_ref, grad_ref, enc_ref, pre_ref, rows_scr, y_scr, p_scr = refs[2 * n :]
    conv_rows(offsets, idx_ref[0], x_refs, halo_refs, w_ref, rows_scr, y_scr)
    taps, width = w_ref.shape[0], w_ref.shape[2]
    half = even_ref.shape[0]
    step = min(64, half)
    length = 2 * half
    zero = jnp.zeros((EDGE, width), F32)
    pre_ref[0:EDGE, :] = zero
    pre_ref[EDGE + length : 2 * EDGE + length, :] = zero
    for start in range(0, half, step):
        rows = slice(start, start + step)
        for c in range(width // LANES):
            lanes = slice(c * LANES, (c + 1) * LANES)
            even = even_ref[rows, lanes] + tap_sum(y_scr, start, step, 0, taps, c)
            odd = odd_ref[rows, lanes] + tap_sum(y_scr, start, step, 1, taps, c)
            act_even, slope_even = gelu_parts(even)
            act_odd, slope_odd = gelu_parts(odd)
            enc_ref[rows, lanes] = (0.5 * (act_even + act_odd)).astype(BF16)
            spread = grad_ref[rows, lanes].astype(F32)
            p_scr[c, pl.ds(2 * start, step, stride=2), :] = slope_even * 0.5 * spread
            p_scr[c, pl.ds(2 * start + 1, step, stride=2), :] = slope_odd * 0.5 * spread
    for c in range(width // LANES):
        lanes = slice(c * LANES, (c + 1) * LANES)
        pre_ref[EDGE : EDGE + length, lanes] = p_scr[c].astype(BF16).astype(F32)


def grad_kernel(offsets, group, shards, idx_ref, *refs):
    n = len(offsets)
    x_refs, halo_refs, (p_ref, *out_refs, edge_scr) = refs[:n], refs[n : 2 * n], refs[2 * n :]
    depth, length = x_refs[0].shape
    width = p_ref.shape[1]
    edge_scr[...] = jnp.zeros_like(edge_scr)
    shifted = []
    for i, tap in enumerate(group):
        cols = slice(i * width, (i + 1) * width)
        edge_scr[0:2, cols] = p_ref[EDGE - tap : EDGE - tap + 2, :]
        edge_scr[2:4, cols] = p_ref[EDGE + length + 2 - tap : EDGE + length + 4 - tap, :]
        shifted.append(p_ref[EDGE + 2 - tap : EDGE + 2 - tap + length, :].astype(BF16))
    p = jnp.concatenate(shifted, axis=1)
    edge = edge_scr[...].astype(BF16)
    me = idx_ref[0]
    x = jnp.concatenate([ref[...] for ref in x_refs], axis=0)
    halo = jnp.concatenate([ref[...] for ref in halo_refs], axis=0)
    res = jnp.dot(x, p, preferred_element_type=F32) + jnp.dot(halo, edge, preferred_element_type=F32)
    res = res.astype(BF16)
    per = n // shards
    for i in range(len(group)):
        for j, off in enumerate(offsets):
            part = res[j * depth : (j + 1) * depth, i * width : (i + 1) * width]
            at = me ^ off
            if per == 0:
                out_refs[i][pl.ds(pl.multiple_of(at * depth, 16), depth), :] = part
                continue
            shard = lax.div(at, per)
            for d in range(shards):
                for r in range(per):
                    hit = jnp.logical_and(shard == lax.rem(idx_ref[1] + d, shards), lax.rem(at, per) == r)
                    ref = out_refs[(i * shards + d) * per + r]

                    @pl.when(hit)
                    def _(ref=ref, part=part):
                        ref[...] = part


def qkv_kernel(offsets, idx_ref, *refs):
    n = len(offsets)
    enc_refs, gain_refs, (w_ref, out_ref) = refs[:n], refs[n : 2 * n], refs[2 * n :]
    depth = enc_refs[0].shape[1]
    values = [ref[...].astype(F32) for ref in enc_refs]
    channels = n * depth
    sums = sum(jnp.sum(v, axis=1, keepdims=True) for v in values)
    squares = sum(jnp.sum(v * v, axis=1, keepdims=True) for v in values)
    mean = sums / channels
    var = squares / channels - mean * mean
    scale = lax.rsqrt(var + 1e-05)
    total = None
    for off, v, gain_ref in zip(offsets, values, gain_refs):
        normal = ((v - mean) * scale * gain_ref[...]).astype(BF16)
        w = w_ref[pl.ds(pl.multiple_of((idx_ref[0] ^ off) * depth, 16), depth), :]
        part = jnp.dot(normal, w, preferred_element_type=F32)
        total = part if total is None else total + part
    out_ref[...] = total.astype(BF16)


def call(kernel, out, scratch, mib, idx, *arrays):
    vmem = pl.BlockSpec(memory_space=pltpu.VMEM)
    return pl.pallas_call(
        kernel,
        out_shape=out,
        in_specs=[pl.BlockSpec(memory_space=pltpu.SMEM)] + [vmem] * len(arrays),
        out_specs=jax.tree.map(lambda _: vmem, out),
        scratch_shapes=scratch,
        compiler_params=pltpu.CompilerParams(vmem_limit_bytes=mib * 1024 * 1024),
    )(idx, *arrays)


def after(value, *others):
    return lax.optimization_barrier((value, *others))[0]


def edge_columns(x):
    peers = lax.axis_size("seq")
    up = [(i, (i + 1) % peers) for i in range(peers - 1)]
    down = [(j, i) for i, j in up]
    length = x.shape[1]
    before = lax.ppermute(x[:, length - 2 :], "seq", up)
    after = lax.ppermute(x[:, :2], "seq", down)
    return jnp.concatenate([before, after], axis=1)


def gathered(value, axis, bits):
    blocks = [value]
    for bit in bits:
        blocks = blocks + [swap(b, axis, bit) for b in blocks]
    return blocks


def added(a, b):
    return (a.astype(F32) + b.astype(F32)).astype(BF16)


def chain_stages(axis):
    peers = lax.axis_size(axis)
    me = lax.axis_index(axis)
    half = peers // 2
    stages = []
    for i in range(half - 1):
        stages.append((axis, [(i, i + 1), (peers - 1 - i, peers - 2 - i)], added))
    stages.append((axis, [(half - 1, half), (half, half - 1)], added))
    for i in reversed(range(half - 1)):
        outer = jnp.logical_or(me == i, me == peers - 1 - i)
        choose = lambda a, b, outer=outer: jnp.where(outer, b, a)
        stages.append((axis, [(i + 1, i), (peers - 2 - i, peers - 1 - i)], choose))
    return stages


def pipelined(parts, stages, sent=None):
    n, depth = len(parts), len(stages)
    state, flying, last = list(parts), [None] * n, None
    late = None

    def launch(c, i, value):
        axis, pairs, _ = stages[i]
        flying[c] = lax.ppermute(value, axis, pairs)

    first = list(parts if sent is None else sent)
    launch(0, 0, first[0])
    for step in range(n + depth - 1):
        if step + 1 < n:
            launch(step + 1, 0, first[step + 1] if last is None else after(first[step + 1], last))
        for i in range(depth):
            c = step - i
            if not 0 <= c < n:
                continue
            got = flying[c] if last is None else after(flying[c], last)
            state[c] = stages[i][2](state[c], got)
            last = state[c]
            if i + 1 < depth:
                launch(c, i + 1, state[c])
                late = last
    return state, late


def on_device(block_input, conv_weight, norm_gain, qkv_weight, encoder_grad):
    x = jnp.swapaxes(block_input[0], 0, 1)
    depth, length = x.shape
    taps, _, width = conv_weight.shape
    peers, shards = lax.axis_size("mp"), lax.axis_size("seq")
    bits = [1 << b for b in reversed(range(peers.bit_length() - 1))]
    idx = jnp.stack([lax.axis_index("mp"), lax.axis_index("seq")]).astype(jnp.int32)

    offsets = [0]
    for bit in bits:
        offsets = offsets + [o ^ bit for o in offsets]
    near = [j for j, o in enumerate(offsets) if o < 2]
    far = [j for j, o in enumerate(offsets) if o >= 2]
    half = length // 2
    pick = lambda items, at: [items[j] for j in at]
    scratch = lambda at: [
        pltpu.VMEM((length + 16, len(at) * depth), BF16),
        pltpu.VMEM((taps * width // LANES, length + 2 * EDGE, LANES), F32),
    ]

    blocks = [x]
    for bit in bits[:-1]:
        blocks = blocks + [swap(b, "mp", bit) for b in blocks]
    own = swap(x, "mp", bits[-1])
    edges = gathered(edge_columns(x), "mp", bits)
    gains = gathered(norm_gain.reshape(1, -1), "mp", bits)
    halos = [jnp.pad(e, ((0, 0), (0, LANES - e.shape[1]))) for e in edges]
    part = jax.ShapeDtypeStruct((half, width), F32)
    even, odd = call(
        functools.partial(first_kernel, pick(offsets, near)),
        (part, part),
        scratch(near),
        40,
        after(idx, *gains), x, own, *pick(halos, near), conv_weight,
    )
    blocks = blocks + [own] + [swap(after(b, even), "mp", bits[-1]) for b in blocks[1:]]
    encoded, pre_grad = call(
        functools.partial(second_kernel, pick(offsets, far)),
        (jax.ShapeDtypeStruct((half, width), BF16), jax.ShapeDtypeStruct((length + 2 * EDGE, width), F32)),
        scratch(far) + [pltpu.VMEM((width // LANES, length, LANES), F32)],
        40,
        idx, *pick(blocks, far), *pick(halos, far), conv_weight, even, odd, encoder_grad[0],
    )

    pair = shards == 2 and peers % shards == 0
    per = peers // shards if pair else 0
    out = (depth, width) if pair else (peers * depth, width)
    count = shards * per if pair else 1
    keep, send = [], []
    done = idx
    encs = [encoded]
    for bit in bits[:-1]:
        encs = encs + [swap(e, "mp", bit) for e in encs]
    encs_own = swap(encoded, "mp", bits[-1])
    for group in [(0,)] + [tuple(range(k, min(k + 2, taps))) for k in range(1, taps, 2)]:
        outs = call(
            functools.partial(grad_kernel, offsets, group, shards if pair else peers + 1),
            (jax.ShapeDtypeStruct(out, BF16),) * (count * len(group)),
            [pltpu.VMEM((LANES, width * len(group)), F32)],
            28,
            done, *blocks, *halos, pre_grad,
        )
        done = after(idx, outs[0], *(encs[1:] if group[0] else ()))
        if not pair:
            keep += [lax.psum_scatter(o, "seq", scatter_dimension=0, tiled=True) for o in outs]
            continue
        for i in range(len(group)):
            keep += outs[i * count : i * count + per]
            send += outs[i * count + per : (i + 1) * count]
    encs = encs + [encs_own] + [swap(e, "mp", bits[-1]) for e in encs[1:]]
    keep[1] = after(keep[1], *encs)
    stages = chain_stages("dp") if lax.axis_size("dp") % 2 == 0 else []
    if pair:
        stages = [("seq", [(0, 1), (1, 0)], added)] + stages
    sums, late = pipelined(keep, stages, send if pair else None)
    if lax.axis_size("dp") % 2:
        sums = [lax.psum(s, "dp") for s in sums]
    lines = max(per, 1)
    sums = [jnp.concatenate(sums[k * lines : (k + 1) * lines], axis=0) for k in range(taps)]
    conv_grad = jnp.stack([s.astype(F32) for s in sums], axis=1)

    qkv = call(
        functools.partial(qkv_kernel, offsets),
        jax.ShapeDtypeStruct((half, qkv_weight.shape[1]), BF16),
        [],
        20,
        idx if late is None else after(idx, late), *encs, *gains, qkv_weight,
    )
    return (qkv[None], conv_grad)


def solution(mesh):
    return jax.shard_map(
        on_device,
        mesh=mesh,
        in_specs=(
            P("dp", "seq", "mp"),
            P(None, None, "mp"),
            P("mp"),
            P(None, "mp"),
            P("dp", "seq", "mp"),
        ),
        out_specs=(P("dp", "seq", "mp"), P("seq", None, "mp")),
        check_vma=False,
    )
```

```python
import functools

import jax
import jax.numpy as jnp
from jax import lax
from jax.experimental import pallas as pl
from jax.experimental.pallas import tpu as pltpu
from jax.sharding import PartitionSpec as P

EDGE = 8
LANES = 128
F32 = jnp.float32
BF16 = jnp.bfloat16


def gelu_parts(v):
    u = 0.7978845608 * (v + 0.044715 * v * v * v)
    th = jnp.tanh(u)
    value = 0.5 * v * (1.0 + th)
    slope = 0.5 * (1.0 + th) + 0.5 * v * (1.0 - th * th) * 0.7978845608 * (1.0 + 0.134145 * v * v)
    return value, slope


def swap(value, axis, bit):
    peers = lax.axis_size(axis)
    return lax.ppermute(value, axis, [(i, i ^ bit) for i in range(peers)])


def edge_block(ref, depth):
    rows = jnp.concatenate([ref[0:8, :], jnp.zeros((LANES - 8, ref.shape[1]), F32)], axis=0)
    keep = lax.broadcasted_iota(jnp.int32, rows.shape, 0) < 4
    return jnp.where(keep, rows, 0.0).T[0:depth, :].astype(BF16)


def conv_rows(offsets, me, x_refs, halo_refs, w_ref, rows_scr, y_scr):
    taps, width = w_ref.shape[0], w_ref.shape[2]
    length = x_refs[0].shape[1]
    x = jnp.concatenate([ref[...] for ref in x_refs], axis=0)
    depth = x.shape[0] // len(offsets)
    halo = jnp.concatenate([edge_block(ref, depth) for ref in halo_refs], axis=0)
    rows_scr[0:length, :] = x.T
    rows_scr[length : length + 16, :] = halo.T[0:16]
    starts = [pl.multiple_of((me ^ off) * depth, 16) for off in offsets]
    for first in range(0, taps, 2):
        group = range(first, min(first + 2, taps))
        w = jnp.concatenate(
            [
                jnp.concatenate([w_ref[k, pl.ds(s, depth), :] for s in starts], axis=0)
                for k in group
            ],
            axis=1,
        )
        y = jnp.dot(rows_scr[...], w, preferred_element_type=F32)
        for c in range(w.shape[1] // LANES):
            part = y[:, c * LANES : (c + 1) * LANES]
            at = first * width // LANES + c
            y_scr[at, EDGE : EDGE + length, :] = part[0:length]
            y_scr[at, EDGE - 2 : EDGE, :] = part[length : length + 2]
            y_scr[at, EDGE + length : EDGE + length + 2, :] = part[length + 2 : length + 4]


def tap_sum(y_scr, start, count, phase, taps, c):
    total = None
    for k in range(taps):
        at = k * (y_scr.shape[0] // taps) + c
        part = y_scr[at, pl.ds(EDGE + 2 * start + phase + k - 2, count, stride=2), :]
        total = part if total is None else total + part
    return total


def first_kernel(offsets, idx_ref, *refs):
    n = len(offsets)
    *x_refs, w_ref, even_ref, odd_ref, rows_scr, y_scr = refs
    x_refs, halo_refs = x_refs[:-n], x_refs[-n:]
    conv_rows(offsets, idx_ref[0], x_refs, halo_refs, w_ref, rows_scr, y_scr)
    taps, width = w_ref.shape[0], w_ref.shape[2]
    half = even_ref.shape[0]
    step = min(64, half)
    for start in range(0, half, step):
        rows = slice(start, start + step)
        for c in range(width // LANES):
            lanes = slice(c * LANES, (c + 1) * LANES)
            even_ref[rows, lanes] = tap_sum(y_scr, start, step, 0, taps, c)
            odd_ref[rows, lanes] = tap_sum(y_scr, start, step, 1, taps, c)


def second_kernel(offsets, idx_ref, *refs):
    n = len(offsets)
    *x_refs, w_ref, even_ref, odd_ref, grad_ref, enc_ref, pre_ref, rows_scr, y_scr, p_scr = refs
    x_refs, halo_refs = x_refs[:-n], x_refs[-n:]
    conv_rows(offsets, idx_ref[0], x_refs, halo_refs, w_ref, rows_scr, y_scr)
    taps, width = w_ref.shape[0], w_ref.shape[2]
    half = even_ref.shape[0]
    step = min(64, half)
    length = 2 * half
    zero = jnp.zeros((EDGE, width), F32)
    pre_ref[0:EDGE, :] = zero
    pre_ref[EDGE + length : 2 * EDGE + length, :] = zero
    for start in range(0, half, step):
        rows = slice(start, start + step)
        for c in range(width // LANES):
            lanes = slice(c * LANES, (c + 1) * LANES)
            even = even_ref[rows, lanes] + tap_sum(y_scr, start, step, 0, taps, c)
            odd = odd_ref[rows, lanes] + tap_sum(y_scr, start, step, 1, taps, c)
            act_even, slope_even = gelu_parts(even)
            act_odd, slope_odd = gelu_parts(odd)
            enc_ref[rows, lanes] = (0.5 * (act_even + act_odd)).astype(BF16)
            spread = grad_ref[rows, lanes].astype(F32)
            p_scr[c, pl.ds(2 * start, step, stride=2), :] = slope_even * 0.5 * spread
            p_scr[c, pl.ds(2 * start + 1, step, stride=2), :] = slope_odd * 0.5 * spread
    for c in range(width // LANES):
        lanes = slice(c * LANES, (c + 1) * LANES)
        pre_ref[EDGE : EDGE + length, lanes] = p_scr[c].astype(BF16).astype(F32)


def grad_kernel(offsets, group, shards, split, idx_ref, *refs):
    n = len(offsets)
    *x_refs, p_ref = refs[: -1 - len(group) * split[1]]
    out_refs, edge_scr = refs[len(x_refs) + 1 : -1], refs[-1]
    x_refs, halo_refs = x_refs[:-n], x_refs[-n:]
    length = x_refs[0].shape[1]
    width = p_ref.shape[1]
    edge_scr[...] = jnp.zeros_like(edge_scr)
    shifted = []
    for i, tap in enumerate(group):
        cols = slice(i * width, (i + 1) * width)
        edge_scr[0:2, cols] = p_ref[EDGE - tap : EDGE - tap + 2, :]
        edge_scr[2:4, cols] = p_ref[EDGE + length + 2 - tap : EDGE + length + 4 - tap, :]
        shifted.append(p_ref[EDGE + 2 - tap : EDGE + 2 - tap + length, :].astype(BF16))
    p = jnp.concatenate(shifted, axis=1)
    edge = edge_scr[...].astype(BF16)
    me = idx_ref[0]
    x = jnp.concatenate([ref[...] for ref in x_refs], axis=0)
    depth = x.shape[0] // n
    halo = jnp.concatenate([edge_block(ref, depth) for ref in halo_refs], axis=0)
    res = jnp.dot(x, p, preferred_element_type=F32) + jnp.dot(halo, edge, preferred_element_type=F32)
    res = res.astype(BF16)
    per, each = split
    for i in range(len(group)):
        outs = out_refs[i * each : (i + 1) * each]
        for j, off in enumerate(offsets):
            part = res[j * depth : (j + 1) * depth, i * width : (i + 1) * width]
            at = me ^ off
            if not per:
                outs[0][pl.ds(pl.multiple_of(at * depth, 16), depth), :] = part
                continue
            mine = lax.div(at, per) == idx_ref[1]
            row = lax.rem(at, per)
            for r in range(per):

                @pl.when(jnp.logical_and(mine, row == r))
                def _(ref=outs[r], part=part):
                    ref[...] = part

                if each == 2 * per:

                    @pl.when(jnp.logical_and(jnp.logical_not(mine), row == r))
                    def _(ref=outs[per + r], part=part):
                        ref[...] = part

            if each == per + 1:

                @pl.when(jnp.logical_not(mine))
                def _(ref=outs[per], part=part):
                    ref[pl.ds(pl.multiple_of(row * depth, 16), depth), :] = part


def qkv_kernel(offsets, idx_ref, *refs):
    n = len(offsets)
    enc_refs, gain_refs, (w_ref, out_ref) = refs[:n], refs[n : 2 * n], refs[2 * n :]
    depth = enc_refs[0].shape[1]
    values = [ref[...].astype(F32) for ref in enc_refs]
    channels = n * depth
    sums = sum(jnp.sum(v, axis=1, keepdims=True) for v in values)
    squares = sum(jnp.sum(v * v, axis=1, keepdims=True) for v in values)
    mean = sums / channels
    var = squares / channels - mean * mean
    scale = lax.rsqrt(var + 1e-05)
    total = None
    for off, v, gain_ref in zip(offsets, values, gain_refs):
        normal = ((v - mean) * scale * gain_ref[4:5, 0:depth]).astype(BF16)
        w = w_ref[pl.ds(pl.multiple_of((idx_ref[0] ^ off) * depth, 16), depth), :]
        part = jnp.dot(normal, w, preferred_element_type=F32)
        total = part if total is None else total + part
    out_ref[...] = total.astype(BF16)


def call(kernel, out, scratch, mib, idx, *arrays):
    vmem = pl.BlockSpec(memory_space=pltpu.VMEM)
    return pl.pallas_call(
        kernel,
        out_shape=out,
        in_specs=[pl.BlockSpec(memory_space=pltpu.SMEM)] + [vmem] * len(arrays),
        out_specs=jax.tree.map(lambda _: vmem, out),
        scratch_shapes=scratch,
        compiler_params=pltpu.CompilerParams(vmem_limit_bytes=mib * 1024 * 1024),
    )(idx, *arrays)


def after(value, *others):
    return lax.optimization_barrier((value, *others))[0]


def edge_rows(x):
    peers = lax.axis_size("seq")
    me = lax.axis_index("seq")
    length = x.shape[1]
    head, tail = x[:, :2], x[:, length - 2 :]
    if peers == 2:
        got = swap(jnp.where(me == 0, tail, head), "seq", 1)
        zero = jnp.zeros_like(got)
        before, behind = jnp.where(me == 0, zero, got), jnp.where(me == 0, got, zero)
    else:
        up = [(i, (i + 1) % peers) for i in range(peers - 1)]
        down = [(j, i) for i, j in up]
        before, behind = lax.ppermute(tail, "seq", up), lax.ppermute(head, "seq", down)
    return lax.optimization_barrier(jnp.concatenate([before, behind], axis=1)).T


def added(a, b):
    return (a.astype(F32) + b.astype(F32)).astype(BF16)


def chain_sums(count, part, sent):
    me = lax.axis_index("dp")
    last, late = None, None
    h, sums = {}, {}
    ways = [
        dict(order=(0, 1, 2, 3), step=1, got=None, p={}, s={}, out={}),
        dict(order=(3, 2, 1, 0), step=-1, got=None, p={}, s={}, out={}),
    ]
    for r in range(count + 3):
        if r < count:
            h[r] = part(r, last)
            last = h[r]
            sent(r, last)
        for way, other in (ways, ways[::-1]):
            first, second, third, _ = way["order"]
            if way["got"] is not None:
                got = after(way["got"], last)
                if r - 1 < count:
                    way["p"][r - 1] = added(h[r - 1], got)
                if 0 <= r - 2 < count:
                    way["s"][r - 2] = added(other["p"][r - 2], got)
                if 0 <= r - 3 < count:
                    way["out"][r - 3] = got
                last = got
            options = [(first, h.get(r)), (second, way["p"].get(r - 1)), (third, way["s"].get(r - 2))]
            options = [o for o in options if o[1] is not None]
            way["got"] = None
            if not options:
                continue
            value = options[-1][1]
            for peer, choice in options[:-1]:
                value = jnp.where(me == peer, choice, value)
            if r - 1 in way["p"] and way is ways[1]:
                value, way["p"][r - 1] = lax.optimization_barrier((value, way["p"][r - 1]))
                late = value
            else:
                value = lax.optimization_barrier(value)
            last = value
            way["got"] = lax.ppermute(value, "dp", [(peer, peer + way["step"]) for peer, _ in options])
        c = r - 3
        if c >= 0:
            lower = jnp.where(me == 0, ways[1]["out"][c], ways[1]["s"][c])
            upper = jnp.where(me == 3, ways[0]["out"][c], ways[0]["s"][c])
            sums[c] = jnp.where(me < 2, lower, upper).astype(F32)
    return [sums[c] for c in range(count)], late


def on_device(block_input, conv_weight, norm_gain, qkv_weight, encoder_grad):
    x = jnp.swapaxes(block_input[0], 0, 1)
    depth, length = x.shape
    taps, _, width = conv_weight.shape
    peers, shards = lax.axis_size("mp"), lax.axis_size("seq")
    bits = [1 << b for b in reversed(range(peers.bit_length() - 1))]
    idx = jnp.stack([lax.axis_index("mp"), lax.axis_index("seq")]).astype(jnp.int32)

    offsets = [0]
    for bit in bits:
        offsets = offsets + [o ^ bit for o in offsets]
    near = [j for j, o in enumerate(offsets) if o < 2]
    far = [j for j, o in enumerate(offsets) if o >= 2]
    half = length // 2
    pick = lambda items, at: [items[j] for j in at]
    scratch = lambda at: [
        pltpu.VMEM((length + 16, len(at) * depth), BF16),
        pltpu.VMEM((taps * width // LANES, length + 2 * EDGE, LANES), F32),
    ]

    blocks = [x]
    for bit in bits[:-1]:
        blocks = blocks + [swap(b, "mp", bit) for b in blocks]
    own = swap(x, "mp", bits[-1])
    edges = edge_rows(x).astype(F32)
    edges = jnp.pad(edges, ((0, 0), (0, width - depth)))
    payload = jnp.concatenate([edges, norm_gain.reshape(1, -1), jnp.zeros((3, width), F32)], axis=0)
    pay_blocks = [payload]
    for bit in bits[:-1]:
        pay_blocks = pay_blocks + [swap(b, "mp", bit) for b in pay_blocks]
    pay_own = swap(payload, "mp", bits[-1])
    part = jax.ShapeDtypeStruct((half, width), F32)
    even, odd = call(
        functools.partial(first_kernel, pick(offsets, near)),
        (part, part),
        scratch(near),
        40,
        idx, x, own, payload, pay_own, conv_weight,
    )
    relay = lambda blocks: [swap(after(b, even), "mp", bits[-1]) for b in blocks[1:]]
    payloads = pay_blocks + [pay_own] + relay(pay_blocks)
    blocks = blocks + [own] + relay(blocks)
    encoded, pre_grad = call(
        functools.partial(second_kernel, pick(offsets, far)),
        (jax.ShapeDtypeStruct((half, width), BF16), jax.ShapeDtypeStruct((length + 2 * EDGE, width), F32)),
        scratch(far) + [pltpu.VMEM((width // LANES, length, LANES), F32)],
        40,
        idx, *pick(blocks, far), *pick(payloads, far), conv_weight, even, odd, encoder_grad[0],
    )

    pair = shards == 2 and peers % shards == 0 and lax.axis_size("dp") == 4
    per = peers // shards if pair else 0
    piece = jax.ShapeDtypeStruct((depth, width), BF16)
    keep, send = [], []
    done = idx
    encs = [encoded]
    for bit in bits[:-1]:
        encs = encs + [swap(e, "mp", bit) for e in encs]
    encs_own = swap(encoded, "mp", bits[-1])
    for group in [(0,)] + [tuple(range(k, min(k + 2, taps))) for k in range(1, taps, 2)]:
        if not pair:
            outs = (jax.ShapeDtypeStruct((peers * depth, width), BF16),)
        elif group[0] == 0:
            outs = (piece,) * (2 * per)
        else:
            outs = (piece,) * per + (jax.ShapeDtypeStruct((per * depth, width), BF16),)
        each = len(outs)
        outs = call(
            functools.partial(grad_kernel, offsets, group, shards, (per, each)),
            outs * len(group),
            [pltpu.VMEM((LANES, width * len(group)), F32)],
            28,
            done, *blocks, *payloads, pre_grad,
        )
        done = after(idx, outs[0], *(encs[1:] if group[0] else ()))
        for i in range(len(group)):
            mine = outs[i * each : (i + 1) * each]
            keep += mine[: max(per, 1)]
            send.append(mine[per:])
    encs = encs + [encs_own] + [swap(e, "mp", bits[-1]) for e in encs[1:]]

    late = encs[-1]
    if pair:
        got = {0: [swap(v, "seq", 1) for v in send[0]]}

        def share(c, last):
            tap, row = c // per, c % per
            value = got[tap][row] if tap == 0 else got[tap][0][row * depth : (row + 1) * depth]
            hold = [] if last is None else [last]
            if c == 1:
                hold = hold + encs
            if hold:
                value = after(value, *hold)
            return added(keep[c], value)

        def sent(c, last):
            tap = c // per + 1
            if c % per == 0 and tap < taps:
                got[tap] = [swap(after(v, last), "seq", 1) for v in send[tap]]

        sums, late = chain_sums(taps * per, share, sent)
        sums = [jnp.concatenate(sums[k * per : (k + 1) * per], axis=0) for k in range(taps)]
    else:
        sums = [lax.psum_scatter(v, "seq", scatter_dimension=0, tiled=True) for v in keep]
        sums = [lax.psum(v, "dp").astype(F32) for v in sums]
    conv_grad = jnp.stack(sums, axis=1)

    qkv = call(
        functools.partial(qkv_kernel, offsets),
        jax.ShapeDtypeStruct((half, qkv_weight.shape[1]), BF16),
        [],
        20,
        after(idx, late), *encs, *payloads, qkv_weight,
    )
    return (qkv[None], conv_grad)


def solution(mesh):
    return jax.shard_map(
        on_device,
        mesh=mesh,
        in_specs=(
            P("dp", "seq", "mp"),
            P(None, None, "mp"),
            P("mp"),
            P(None, "mp"),
            P("dp", "seq", "mp"),
        ),
        out_specs=(P("dp", "seq", "mp"), P("seq", None, "mp")),
        check_vma=False,
    )
```

```python
import functools

import jax
import jax.numpy as jnp
from jax import lax
from jax.experimental import pallas as pl
from jax.experimental.pallas import tpu as pltpu
from jax.sharding import PartitionSpec as P

EDGE = 8
LANES = 128
F32 = jnp.float32
BF16 = jnp.bfloat16


def gelu_parts(v):
    u = 0.7978845608 * (v + 0.044715 * v * v * v)
    th = jnp.tanh(u)
    value = 0.5 * v * (1.0 + th)
    slope = 0.5 * (1.0 + th) + 0.5 * v * (1.0 - th * th) * 0.7978845608 * (1.0 + 0.134145 * v * v)
    return value, slope


def swap(value, axis, bit):
    peers = lax.axis_size(axis)
    return lax.ppermute(value, axis, [(i, i ^ bit) for i in range(peers)])


def edge_block(ref, depth):
    rows = jnp.concatenate([ref[0:8, :], jnp.zeros((LANES - 8, ref.shape[1]), F32)], axis=0)
    keep = lax.broadcasted_iota(jnp.int32, rows.shape, 0) < 4
    return jnp.where(keep, rows, 0.0).T[0:depth, :].astype(BF16)


def conv_rows(offsets, me, x_refs, halo_refs, w_ref, rows_scr, y_scr):
    taps, width = w_ref.shape[0], w_ref.shape[2]
    length = x_refs[0].shape[1]
    x = jnp.concatenate([ref[...] for ref in x_refs], axis=0)
    depth = x.shape[0] // len(offsets)
    halo = jnp.concatenate([edge_block(ref, depth) for ref in halo_refs], axis=0)
    rows_scr[0:length, :] = x.T
    rows_scr[length : length + 16, :] = halo.T[0:16]
    starts = [pl.multiple_of((me ^ off) * depth, 16) for off in offsets]
    for first in range(0, taps, 2):
        group = range(first, min(first + 2, taps))
        w = jnp.concatenate(
            [
                jnp.concatenate([w_ref[k, pl.ds(s, depth), :] for s in starts], axis=0)
                for k in group
            ],
            axis=1,
        )
        y = jnp.dot(rows_scr[...], w, preferred_element_type=F32)
        for c in range(w.shape[1] // LANES):
            part = y[:, c * LANES : (c + 1) * LANES]
            at = first * width // LANES + c
            y_scr[at, EDGE : EDGE + length, :] = part[0:length]
            y_scr[at, EDGE - 2 : EDGE, :] = part[length : length + 2]
            y_scr[at, EDGE + length : EDGE + length + 2, :] = part[length + 2 : length + 4]


def tap_sum(y_scr, start, count, phase, taps, c):
    total = None
    for k in range(taps):
        at = k * (y_scr.shape[0] // taps) + c
        part = y_scr[at, pl.ds(EDGE + 2 * start + phase + k - 2, count, stride=2), :]
        total = part if total is None else total + part
    return total


def first_kernel(offsets, idx_ref, *refs):
    n = len(offsets)
    *x_refs, w_ref, even_ref, odd_ref, rows_scr, y_scr = refs
    x_refs, halo_refs = x_refs[:-n], x_refs[-n:]
    conv_rows(offsets, idx_ref[0], x_refs, halo_refs, w_ref, rows_scr, y_scr)
    taps, width = w_ref.shape[0], w_ref.shape[2]
    half = even_ref.shape[0]
    step = min(64, half)
    for start in range(0, half, step):
        rows = slice(start, start + step)
        for c in range(width // LANES):
            lanes = slice(c * LANES, (c + 1) * LANES)
            even_ref[rows, lanes] = tap_sum(y_scr, start, step, 0, taps, c)
            odd_ref[rows, lanes] = tap_sum(y_scr, start, step, 1, taps, c)


def second_kernel(offsets, idx_ref, *refs):
    n = len(offsets)
    *x_refs, w_ref, even_ref, odd_ref, grad_ref, enc_ref, pre_ref, rows_scr, y_scr, p_scr = refs
    x_refs, halo_refs = x_refs[:-n], x_refs[-n:]
    conv_rows(offsets, idx_ref[0], x_refs, halo_refs, w_ref, rows_scr, y_scr)
    taps, width = w_ref.shape[0], w_ref.shape[2]
    half = even_ref.shape[0]
    step = min(64, half)
    length = 2 * half
    zero = jnp.zeros((EDGE, width), F32)
    pre_ref[0:EDGE, :] = zero
    pre_ref[EDGE + length : 2 * EDGE + length, :] = zero
    for start in range(0, half, step):
        rows = slice(start, start + step)
        for c in range(width // LANES):
            lanes = slice(c * LANES, (c + 1) * LANES)
            even = even_ref[rows, lanes] + tap_sum(y_scr, start, step, 0, taps, c)
            odd = odd_ref[rows, lanes] + tap_sum(y_scr, start, step, 1, taps, c)
            act_even, slope_even = gelu_parts(even)
            act_odd, slope_odd = gelu_parts(odd)
            enc_ref[rows, lanes] = (0.5 * (act_even + act_odd)).astype(BF16)
            spread = grad_ref[rows, lanes].astype(F32)
            p_scr[c, pl.ds(2 * start, step, stride=2), :] = slope_even * 0.5 * spread
            p_scr[c, pl.ds(2 * start + 1, step, stride=2), :] = slope_odd * 0.5 * spread
    for c in range(width // LANES):
        lanes = slice(c * LANES, (c + 1) * LANES)
        pre_ref[EDGE : EDGE + length, lanes] = p_scr[c].astype(BF16).astype(F32)


def grad_kernel(offsets, group, shards, split, idx_ref, *refs):
    n = len(offsets)
    *x_refs, p_ref = refs[: -1 - len(group) * split[1]]
    out_refs, edge_scr = refs[len(x_refs) + 1 : -1], refs[-1]
    x_refs, halo_refs = x_refs[:-n], x_refs[-n:]
    length = x_refs[0].shape[1]
    width = p_ref.shape[1]
    edge_scr[...] = jnp.zeros_like(edge_scr)
    shifted = []
    for i, tap in enumerate(group):
        cols = slice(i * width, (i + 1) * width)
        edge_scr[0:2, cols] = p_ref[EDGE - tap : EDGE - tap + 2, :]
        edge_scr[2:4, cols] = p_ref[EDGE + length + 2 - tap : EDGE + length + 4 - tap, :]
        shifted.append(p_ref[EDGE + 2 - tap : EDGE + 2 - tap + length, :].astype(BF16))
    p = jnp.concatenate(shifted, axis=1)
    edge = edge_scr[...].astype(BF16)
    me = idx_ref[0]
    x = jnp.concatenate([ref[...] for ref in x_refs], axis=0)
    depth = x.shape[0] // n
    halo = jnp.concatenate([edge_block(ref, depth) for ref in halo_refs], axis=0)
    res = jnp.dot(x, p, preferred_element_type=F32) + jnp.dot(halo, edge, preferred_element_type=F32)
    res = res.astype(BF16)
    per, each = split
    for i in range(len(group)):
        outs = out_refs[i * each : (i + 1) * each]
        for j, off in enumerate(offsets):
            part = res[j * depth : (j + 1) * depth, i * width : (i + 1) * width]
            at = me ^ off
            if not per:
                outs[0][pl.ds(pl.multiple_of(at * depth, 16), depth), :] = part
                continue
            mine = lax.div(at, per) == idx_ref[1]
            row = lax.rem(at, per)
            for r in range(per):

                @pl.when(jnp.logical_and(mine, row == r))
                def _(ref=outs[r], part=part):
                    ref[...] = part

                if each == 2 * per:

                    @pl.when(jnp.logical_and(jnp.logical_not(mine), row == r))
                    def _(ref=outs[per + r], part=part):
                        ref[...] = part

            if each == per + 1:

                @pl.when(jnp.logical_not(mine))
                def _(ref=outs[per], part=part):
                    ref[pl.ds(pl.multiple_of(row * depth, 16), depth), :] = part


def qkv_kernel(offsets, idx_ref, *refs):
    n = len(offsets)
    enc_refs, gain_refs, (w_ref, out_ref) = refs[:n], refs[n : 2 * n], refs[2 * n :]
    depth = enc_refs[0].shape[1]
    values = [ref[...].astype(F32) for ref in enc_refs]
    channels = n * depth
    sums = sum(jnp.sum(v, axis=1, keepdims=True) for v in values)
    squares = sum(jnp.sum(v * v, axis=1, keepdims=True) for v in values)
    mean = sums / channels
    var = squares / channels - mean * mean
    scale = lax.rsqrt(var + 1e-05)
    total = None
    for off, v, gain_ref in zip(offsets, values, gain_refs):
        normal = ((v - mean) * scale * gain_ref[4:5, 0:depth]).astype(BF16)
        w = w_ref[pl.ds(pl.multiple_of((idx_ref[0] ^ off) * depth, 16), depth), :]
        part = jnp.dot(normal, w, preferred_element_type=F32)
        total = part if total is None else total + part
    out_ref[...] = total.astype(BF16)


def call(kernel, out, scratch, mib, idx, *arrays):
    vmem = pl.BlockSpec(memory_space=pltpu.VMEM)
    return pl.pallas_call(
        kernel,
        out_shape=out,
        in_specs=[pl.BlockSpec(memory_space=pltpu.SMEM)] + [vmem] * len(arrays),
        out_specs=jax.tree.map(lambda _: vmem, out),
        scratch_shapes=scratch,
        compiler_params=pltpu.CompilerParams(vmem_limit_bytes=mib * 1024 * 1024),
    )(idx, *arrays)


def after(value, *others):
    return lax.optimization_barrier((value, *others))[0]


def edge_kernel(head_ref, tail_ref, out_ref):
    depth = head_ref.shape[0]
    extra = jnp.zeros((out_ref.shape[1] - depth, LANES), F32)
    head = jnp.concatenate([head_ref[...].astype(F32), extra], axis=0).T
    tail = jnp.concatenate([tail_ref[...].astype(F32), extra], axis=0).T
    out_ref[...] = jnp.zeros_like(out_ref)
    out_ref[0:2, :] = head[0:2]
    out_ref[2:4, :] = tail[LANES - 2 : LANES]


def edge_rows(x, width):
    peers = lax.axis_size("seq")
    me = lax.axis_index("seq")
    depth, length = x.shape
    ends = pl.pallas_call(
        edge_kernel,
        out_shape=jax.ShapeDtypeStruct((8, width), F32),
        grid=(1,),
        in_specs=[
            pl.BlockSpec((depth, LANES), lambda i: (0, 0)),
            pl.BlockSpec((depth, LANES), lambda i: (0, length // LANES - 1)),
        ],
        out_specs=pl.BlockSpec((8, width), lambda i: (0, 0)),
    )(x, x)
    if peers == 2:
        before = behind = swap(ends, "seq", 1)
    else:
        up = [(i, (i + 1) % peers) for i in range(peers - 1)]
        down = [(j, i) for i, j in up]
        before, behind = lax.ppermute(ends, "seq", up), lax.ppermute(ends, "seq", down)
    before = jnp.where(me == 0, 0.0, before[2:4])
    behind = jnp.where(me == peers - 1, 0.0, behind[0:2])
    return jnp.concatenate([before, behind], axis=0)


def added(a, b):
    return (a.astype(F32) + b.astype(F32)).astype(BF16)


def chain_sums(count, part, sent):
    me = lax.axis_index("dp")
    end = jnp.logical_or(me == 0, me == 3)
    outer_pairs = [(0, 1), (1, 0), (2, 3), (3, 2)]
    middle_pairs = [(0, 0), (1, 2), (2, 1), (3, 3)]
    last, late = None, None
    h, p, s, outer, middle, sums = {}, {}, {}, {}, {}, {}
    for r in range(count + 5):
        if r < count:
            h[r] = part(r, last)
            last = h[r]
            sent(r, last)
        if r < count + 3:
            value = h.get(r, s.get(r - 3))
            if r in h and r - 3 in s:
                value = jnp.where(end, h[r], s[r - 3])
            last = value = lax.optimization_barrier(value)
            outer[r] = lax.ppermute(value, "dp", outer_pairs)
        if r - 1 in outer:
            got = after(outer.pop(r - 1), last)
            if r - 1 < count:
                last = p[r - 1] = lax.optimization_barrier(added(h[r - 1], got))
                late = last
                middle[r - 1] = lax.ppermute(last, "dp", middle_pairs)
            if r - 4 >= 0:
                sums[r - 4] = lax.optimization_barrier(jnp.where(end, got, s[r - 4]))
                if r - 1 >= count:
                    last = sums[r - 4]
        if r - 2 in middle:
            got = after(middle.pop(r - 2), last)
            last = s[r - 2] = lax.optimization_barrier(added(p[r - 2], got))
    return [sums[c].astype(F32) for c in range(count)], late


def on_device(block_input, conv_weight, norm_gain, qkv_weight, encoder_grad):
    x = jnp.swapaxes(block_input[0], 0, 1)
    depth, length = x.shape
    taps, _, width = conv_weight.shape
    peers, shards = lax.axis_size("mp"), lax.axis_size("seq")
    bits = [1 << b for b in reversed(range(peers.bit_length() - 1))]
    idx = jnp.stack([lax.axis_index("mp"), lax.axis_index("seq")]).astype(jnp.int32)

    offsets = [0]
    for bit in bits:
        offsets = offsets + [o ^ bit for o in offsets]
    near = [j for j, o in enumerate(offsets) if o < 2]
    far = [j for j, o in enumerate(offsets) if o >= 2]
    half = length // 2
    pick = lambda items, at: [items[j] for j in at]
    scratch = lambda at: [
        pltpu.VMEM((length + 16, len(at) * depth), BF16),
        pltpu.VMEM((taps * width // LANES, length + 2 * EDGE, LANES), F32),
    ]

    blocks = [x]
    for bit in bits[:-1]:
        blocks = blocks + [swap(b, "mp", bit) for b in blocks]
    own = swap(x, "mp", bits[-1])
    edges = edge_rows(x, width)
    payload = jnp.concatenate([edges, norm_gain.reshape(1, -1), jnp.zeros((3, width), F32)], axis=0)
    payloads = [payload] + [swap(payload, "mp", o) for o in offsets[1:]]

    part = jax.ShapeDtypeStruct((half, width), F32)
    even, odd = call(
        functools.partial(first_kernel, pick(offsets, near)),
        (part, part),
        scratch(near),
        24,
        idx, x, own, *pick(payloads, near), conv_weight,
    )
    hold = [even] + pick(payloads, far)
    blocks = blocks + [own] + [swap(after(b, *hold), "mp", bits[-1]) for b in blocks[1:]]
    encoded, pre_grad = call(
        functools.partial(second_kernel, pick(offsets, far)),
        (jax.ShapeDtypeStruct((half, width), BF16), jax.ShapeDtypeStruct((length + 2 * EDGE, width), F32)),
        scratch(far) + [pltpu.VMEM((width // LANES, length, LANES), F32)],
        24,
        idx, *pick(blocks, far), *pick(payloads, far), conv_weight, even, odd, encoder_grad[0],
    )

    pair = shards == 2 and peers % shards == 0 and lax.axis_size("dp") == 4
    per = peers // shards if pair else 0
    piece = jax.ShapeDtypeStruct((depth, width), BF16)
    keep, send = [], []
    done = idx
    encs = [encoded]
    for bit in bits[:-1]:
        encs = encs + [swap(e, "mp", bit) for e in encs]
    encs_own = swap(encoded, "mp", bits[-1])
    for group in [(0,)] + [tuple(range(k, min(k + 2, taps))) for k in range(1, taps, 2)]:
        if not pair:
            outs = (jax.ShapeDtypeStruct((peers * depth, width), BF16),)
        elif group[0] == 0:
            outs = (piece,) * (2 * per)
        else:
            outs = (piece,) * per + (jax.ShapeDtypeStruct((per * depth, width), BF16),)
        each = len(outs)
        outs = call(
            functools.partial(grad_kernel, offsets, group, shards, (per, each)),
            outs * len(group),
            [pltpu.VMEM((LANES, width * len(group)), F32)],
            14,
            done, *blocks, *payloads, pre_grad,
        )
        done = after(idx, outs[0], *(encs[1:] if group[0] else ()))
        for i in range(len(group)):
            mine = outs[i * each : (i + 1) * each]
            keep += mine[: max(per, 1)]
            send.append(mine[per:])
    encs = encs + [encs_own] + [swap(e, "mp", bits[-1]) for e in encs[1:]]

    late = encs[-1]
    if pair:
        got = {0: [swap(v, "seq", 1) for v in send[0]]}

        def share(c, last):
            tap, row = c // per, c % per
            value = got[tap][row] if tap == 0 else got[tap][0][row * depth : (row + 1) * depth]
            hold = [] if last is None else [last]
            if c == 1:
                hold = hold + encs
            if hold:
                value = after(value, *hold)
            return added(keep[c], value)

        def sent(c, last):
            tap = c // per + 1
            if c % per == 0 and tap < taps:
                got[tap] = [swap(after(v, last), "seq", 1) for v in send[tap]]

        sums, late = chain_sums(taps * per, share, sent)
        sums = [jnp.concatenate(sums[k * per : (k + 1) * per], axis=0) for k in range(taps)]
    else:
        sums = [lax.psum_scatter(v, "seq", scatter_dimension=0, tiled=True) for v in keep]
        sums = [lax.psum(v, "dp").astype(F32) for v in sums]
    conv_grad = jnp.stack(sums, axis=1)

    qkv = call(
        functools.partial(qkv_kernel, offsets),
        jax.ShapeDtypeStruct((half, qkv_weight.shape[1]), BF16),
        [],
        8,
        after(idx, late), *encs, *payloads, qkv_weight,
    )
    return (qkv[None], conv_grad)


def solution(mesh):
    return jax.shard_map(
        on_device,
        mesh=mesh,
        in_specs=(
            P("dp", "seq", "mp"),
            P(None, None, "mp"),
            P("mp"),
            P(None, "mp"),
            P("dp", "seq", "mp"),
        ),
        out_specs=(P("dp", "seq", "mp"), P("seq", None, "mp")),
        check_vma=False,
    )
```

```python
import functools

import jax
import jax.numpy as jnp
from jax import lax
from jax.experimental import pallas as pl
from jax.experimental.pallas import tpu as pltpu
from jax.sharding import PartitionSpec as P

EDGE = 8
LANES = 128
F32 = jnp.float32
BF16 = jnp.bfloat16


def gelu_parts(v):
    u = 0.7978845608 * (v + 0.044715 * v * v * v)
    th = jnp.tanh(u)
    value = 0.5 * v * (1.0 + th)
    slope = 0.5 * (1.0 + th) + 0.5 * v * (1.0 - th * th) * 0.7978845608 * (1.0 + 0.134145 * v * v)
    return value, slope


def swap(value, axis, bit):
    peers = lax.axis_size(axis)
    return lax.ppermute(value, axis, [(i, i ^ bit) for i in range(peers)])


def edge_block(ref, depth):
    rows = jnp.concatenate([ref[0:8, :], jnp.zeros((LANES - 8, ref.shape[1]), F32)], axis=0)
    keep = lax.broadcasted_iota(jnp.int32, rows.shape, 0) < 4
    return jnp.where(keep, rows, 0.0).T[0:depth, :].astype(BF16)


def conv_rows(offsets, me, x_refs, halo_refs, w_ref, rows_scr, y_scr):
    taps, width = w_ref.shape[0], w_ref.shape[2]
    length = x_refs[0].shape[1]
    x = jnp.concatenate([ref[...] for ref in x_refs], axis=0)
    depth = x.shape[0] // len(offsets)
    halo = jnp.concatenate([edge_block(ref, depth) for ref in halo_refs], axis=0)
    rows_scr[0:length, :] = x.T
    rows_scr[length : length + 16, :] = halo.T[0:16]
    starts = [pl.multiple_of((me ^ off) * depth, 16) for off in offsets]
    for first in range(0, taps, 2):
        group = range(first, min(first + 2, taps))
        w = jnp.concatenate(
            [
                jnp.concatenate([w_ref[k, pl.ds(s, depth), :] for s in starts], axis=0)
                for k in group
            ],
            axis=1,
        )
        y = jnp.dot(rows_scr[...], w, preferred_element_type=F32)
        for c in range(w.shape[1] // LANES):
            part = y[:, c * LANES : (c + 1) * LANES]
            at = first * width // LANES + c
            y_scr[at, EDGE : EDGE + length, :] = part[0:length]
            y_scr[at, EDGE - 2 : EDGE, :] = part[length : length + 2]
            y_scr[at, EDGE + length : EDGE + length + 2, :] = part[length + 2 : length + 4]


def tap_sum(y_scr, start, count, phase, taps, c):
    total = None
    for k in range(taps):
        at = k * (y_scr.shape[0] // taps) + c
        part = y_scr[at, pl.ds(EDGE + 2 * start + phase + k - 2, count, stride=2), :]
        total = part if total is None else total + part
    return total


def first_kernel(offsets, idx_ref, *refs):
    n = len(offsets)
    *x_refs, w_ref, even_ref, odd_ref, rows_scr, y_scr = refs
    x_refs, halo_refs = x_refs[:-n], x_refs[-n:]
    conv_rows(offsets, idx_ref[0], x_refs, halo_refs, w_ref, rows_scr, y_scr)
    taps, width = w_ref.shape[0], w_ref.shape[2]
    half = even_ref.shape[0]
    step = min(64, half)
    for start in range(0, half, step):
        rows = slice(start, start + step)
        for c in range(width // LANES):
            lanes = slice(c * LANES, (c + 1) * LANES)
            even_ref[rows, lanes] = tap_sum(y_scr, start, step, 0, taps, c)
            odd_ref[rows, lanes] = tap_sum(y_scr, start, step, 1, taps, c)


def second_kernel(offsets, far, per, idx_ref, *refs):
    n = len(offsets)
    blocks, pays, refs = refs[:n], refs[n : 2 * n], refs[2 * n :]
    w_ref, even_ref, odd_ref, grad_ref, enc_ref, pre_ref, *sent_refs, rows_scr, y_scr, p_scr, x_scr, edge_scr = refs
    me = idx_ref[0]
    pick = lambda items: [items[j] for j in far]
    conv_rows(pick(offsets), me, pick(blocks), pick(pays), w_ref, rows_scr, y_scr)
    taps, width = w_ref.shape[0], w_ref.shape[2]
    half = even_ref.shape[0]
    step = min(64, half)
    length = 2 * half
    zero = jnp.zeros((EDGE, width), F32)
    pre_ref[0:EDGE, :] = zero
    pre_ref[EDGE + length : 2 * EDGE + length, :] = zero
    for start in range(0, half, step):
        rows = slice(start, start + step)
        for c in range(width // LANES):
            lanes = slice(c * LANES, (c + 1) * LANES)
            even = even_ref[rows, lanes] + tap_sum(y_scr, start, step, 0, taps, c)
            odd = odd_ref[rows, lanes] + tap_sum(y_scr, start, step, 1, taps, c)
            act_even, slope_even = gelu_parts(even)
            act_odd, slope_odd = gelu_parts(odd)
            enc_ref[rows, lanes] = (0.5 * (act_even + act_odd)).astype(BF16)
            spread = grad_ref[rows, lanes].astype(F32)
            p_scr[c, pl.ds(2 * start, step, stride=2), :] = slope_even * 0.5 * spread
            p_scr[c, pl.ds(2 * start + 1, step, stride=2), :] = slope_odd * 0.5 * spread
    for c in range(width // LANES):
        lanes = slice(c * LANES, (c + 1) * LANES)
        pre_ref[EDGE : EDGE + length, lanes] = p_scr[c].astype(BF16).astype(F32)
    if not sent_refs:
        return
    wanted = (1 - idx_ref[1]) * per
    depth = blocks[0].shape[0]
    for off, block, pay in zip(offsets, blocks, pays):

        @pl.when(me ^ off == wanted)
        def _(block=block, pay=pay):
            x_scr[:, 0:length] = block[...]
            x_scr[:, length : length + LANES] = edge_block(pay, depth)

    p, edge = shifted_rows(pre_ref, edge_scr, (0,))
    res = jnp.dot(x_scr[:, 0:length], p, preferred_element_type=F32)
    res = res + jnp.dot(x_scr[:, length : length + LANES], edge, preferred_element_type=F32)
    sent_refs[0][...] = res.astype(BF16)


def shifted_rows(p_ref, edge_scr, group):
    length, width = p_ref.shape[0] - 2 * EDGE, p_ref.shape[1]
    edge_scr[...] = jnp.zeros_like(edge_scr)
    shifted = []
    for i, tap in enumerate(group):
        cols = slice(i * width, (i + 1) * width)
        edge_scr[0:2, cols] = p_ref[EDGE - tap : EDGE - tap + 2, :]
        edge_scr[2:4, cols] = p_ref[EDGE + length + 2 - tap : EDGE + length + 4 - tap, :]
        shifted.append(p_ref[EDGE + 2 - tap : EDGE + 2 - tap + length, :].astype(BF16))
    return jnp.concatenate(shifted, axis=1), edge_scr[...].astype(BF16)


def grad_kernel(offsets, group, per, pieces, idx_ref, *refs):
    n = len(offsets)
    blocks, pays, p_ref = refs[:n], refs[n : 2 * n], refs[2 * n]
    out_refs, edge_scr = refs[2 * n + 1 : -1], refs[-1]
    width = p_ref.shape[1]
    p, edge = shifted_rows(p_ref, edge_scr, group)
    me = idx_ref[0]
    x = jnp.concatenate([ref[...] for ref in blocks], axis=0)
    depth = x.shape[0] // n
    halo = jnp.concatenate([edge_block(ref, depth) for ref in pays], axis=0)
    res = jnp.dot(x, p, preferred_element_type=F32) + jnp.dot(halo, edge, preferred_element_type=F32)
    res = res.astype(BF16)
    each = len(out_refs) // len(group)
    for i in range(len(group)):
        outs = out_refs[i * each : (i + 1) * each]
        for j, off in enumerate(offsets):
            part = res[j * depth : (j + 1) * depth, i * width : (i + 1) * width]
            at = me ^ off
            if not per:
                outs[0][pl.ds(pl.multiple_of(at * depth, 16), depth), :] = part
                continue
            mine = lax.div(at, per) == idx_ref[1]
            other = jnp.logical_not(mine)
            row = lax.rem(at, per)
            hits = [(outs[r], jnp.logical_and(mine, row == r)) for r in range(per)]
            hits += [(outs[per + k], jnp.logical_and(other, row == r)) for k, r in enumerate(pieces)]
            for ref, hit in hits:

                @pl.when(hit)
                def _(ref=ref, part=part):
                    ref[...] = part

            if not pieces:

                @pl.when(other)
                def _(ref=outs[per], part=part, row=row):
                    ref[pl.ds(pl.multiple_of(row * depth, 16), depth), :] = part


def qkv_kernel(offsets, idx_ref, *refs):
    n = len(offsets)
    enc_refs, gain_refs, (w_ref, out_ref) = refs[:n], refs[n : 2 * n], refs[2 * n :]
    depth = enc_refs[0].shape[1]
    values = [ref[...].astype(F32) for ref in enc_refs]
    channels = n * depth
    sums = sum(jnp.sum(v, axis=1, keepdims=True) for v in values)
    squares = sum(jnp.sum(v * v, axis=1, keepdims=True) for v in values)
    mean = sums / channels
    var = squares / channels - mean * mean
    scale = lax.rsqrt(var + 1e-05)
    total = None
    for off, v, gain_ref in zip(offsets, values, gain_refs):
        normal = ((v - mean) * scale * gain_ref[4:5, 0:depth]).astype(BF16)
        w = w_ref[pl.ds(pl.multiple_of((idx_ref[0] ^ off) * depth, 16), depth), :]
        part = jnp.dot(normal, w, preferred_element_type=F32)
        total = part if total is None else total + part
    out_ref[...] = total.astype(BF16)


def call(kernel, out, scratch, mib, idx, *arrays):
    vmem = pl.BlockSpec(memory_space=pltpu.VMEM)
    return pl.pallas_call(
        kernel,
        out_shape=out,
        in_specs=[pl.BlockSpec(memory_space=pltpu.SMEM)] + [vmem] * len(arrays),
        out_specs=jax.tree.map(lambda _: vmem, out),
        scratch_shapes=scratch,
        compiler_params=pltpu.CompilerParams(vmem_limit_bytes=mib * 1024 * 1024),
    )(idx, *arrays)


def after(value, *others):
    return lax.optimization_barrier((value, *others))[0]


def edge_kernel(head_ref, tail_ref, out_ref):
    depth = head_ref.shape[0]
    extra = jnp.zeros((out_ref.shape[1] - depth, LANES), F32)
    head = jnp.concatenate([head_ref[...].astype(F32), extra], axis=0).T
    tail = jnp.concatenate([tail_ref[...].astype(F32), extra], axis=0).T
    out_ref[...] = jnp.zeros_like(out_ref)
    out_ref[0:2, :] = head[0:2]
    out_ref[2:4, :] = tail[LANES - 2 : LANES]


def edge_rows(x, width):
    peers = lax.axis_size("seq")
    me = lax.axis_index("seq")
    depth, length = x.shape
    ends = pl.pallas_call(
        edge_kernel,
        out_shape=jax.ShapeDtypeStruct((8, width), F32),
        grid=(1,),
        in_specs=[
            pl.BlockSpec((depth, LANES), lambda i: (0, 0)),
            pl.BlockSpec((depth, LANES), lambda i: (0, length // LANES - 1)),
        ],
        out_specs=pl.BlockSpec((8, width), lambda i: (0, 0)),
        compiler_params=pltpu.CompilerParams(vmem_limit_bytes=2 * 1024 * 1024),
    )(x, x)
    if peers == 2:
        before = behind = swap(ends, "seq", 1)
    else:
        up = [(i, (i + 1) % peers) for i in range(peers - 1)]
        down = [(j, i) for i, j in up]
        before, behind = lax.ppermute(ends, "seq", up), lax.ppermute(ends, "seq", down)
    before = jnp.where(me == 0, 0.0, before[2:4])
    behind = jnp.where(me == peers - 1, 0.0, behind[0:2])
    return jnp.concatenate([before, behind], axis=0)


def added(a, b):
    return (a.astype(F32) + b.astype(F32)).astype(BF16)


def chain_sums(count, part, sent):
    me = lax.axis_index("dp")
    end = jnp.logical_or(me == 0, me == 3)
    outer_pairs = [(0, 1), (1, 0), (2, 3), (3, 2)]
    middle_pairs = [(0, 0), (1, 2), (2, 1), (3, 3)]
    last, late = None, None
    h, p, s, outer, middle, sums = {}, {}, {}, {}, {}, {}
    for r in range(count + 5):
        if r < count:
            h[r] = part(r, last)
            last = h[r]
            sent(r, last)
        if r < count + 3:
            value = h.get(r, s.get(r - 3))
            if r in h and r - 3 in s:
                value = jnp.where(end, h[r], s[r - 3])
            last = value = lax.optimization_barrier(value)
            outer[r] = lax.ppermute(value, "dp", outer_pairs)
        if r - 1 in outer:
            got = after(outer.pop(r - 1), last)
            if r - 1 < count:
                last = p[r - 1] = lax.optimization_barrier(added(h[r - 1], got))
                late = last
                middle[r - 1] = lax.ppermute(last, "dp", middle_pairs)
            if r - 4 >= 0:
                sums[r - 4] = lax.optimization_barrier(jnp.where(end, got, s[r - 4]))
                if r - 1 >= count:
                    last = sums[r - 4]
        if r - 2 in middle:
            got = after(middle.pop(r - 2), last)
            last = s[r - 2] = lax.optimization_barrier(added(p[r - 2], got))
    return [sums[c].astype(F32) for c in range(count)], late


def on_device(block_input, conv_weight, norm_gain, qkv_weight, encoder_grad):
    x = jnp.swapaxes(block_input[0], 0, 1)
    depth, length = x.shape
    taps, _, width = conv_weight.shape
    peers, shards = lax.axis_size("mp"), lax.axis_size("seq")
    bits = [1 << b for b in reversed(range(peers.bit_length() - 1))]
    idx = jnp.stack([lax.axis_index("mp"), lax.axis_index("seq")]).astype(jnp.int32)

    offsets = [0]
    for bit in bits:
        offsets = offsets + [o ^ bit for o in offsets]
    near = [j for j, o in enumerate(offsets) if o < 2]
    far = [j for j, o in enumerate(offsets) if o >= 2]
    half = length // 2
    pick = lambda items, at: [items[j] for j in at]
    scratch = lambda at: [
        pltpu.VMEM((length + 16, len(at) * depth), BF16),
        pltpu.VMEM((taps * width // LANES, length + 2 * EDGE, LANES), F32),
    ]

    blocks = [x]
    for bit in bits[:-1]:
        blocks = blocks + [swap(b, "mp", bit) for b in blocks]
    own = swap(x, "mp", bits[-1])
    edges = edge_rows(x, width)
    payload = jnp.concatenate([edges, norm_gain.reshape(1, -1), jnp.zeros((3, width), F32)], axis=0)
    payloads = [payload] + [swap(payload, "mp", o) for o in offsets[1:]]

    part = jax.ShapeDtypeStruct((half, width), F32)
    even, odd = call(
        functools.partial(first_kernel, pick(offsets, near)),
        (part, part),
        scratch(near),
        24,
        idx, x, own, *pick(payloads, near), conv_weight,
    )
    hold = [even] + pick(payloads, far)
    blocks = blocks + [own] + [swap(after(b, *hold), "mp", bits[-1]) for b in blocks[1:]]
    pair = shards == 2 and peers % shards == 0 and lax.axis_size("dp") == 4
    per = peers // shards if pair else 0
    piece = jax.ShapeDtypeStruct((depth, width), BF16)
    encoded, pre_grad, *first = call(
        functools.partial(second_kernel, offsets, far, per),
        (
            jax.ShapeDtypeStruct((half, width), BF16),
            jax.ShapeDtypeStruct((length + 2 * EDGE, width), F32),
            *([piece] if pair else []),
        ),
        scratch(far)
        + [
            pltpu.VMEM((width // LANES, length, LANES), F32),
            pltpu.VMEM((depth, length + LANES), BF16),
            pltpu.VMEM((LANES, width), F32),
        ],
        26,
        idx, *blocks, *payloads, conv_weight, even, odd, encoder_grad[0],
    )
    encs = [encoded]
    for bit in bits[:-1]:
        encs = encs + [swap(e, "mp", bit) for e in encs]

    everything = tuple(range(per))
    pieces_of = lambda k: everything[1:] if k == 0 else (everything if k == taps - 1 else ())

    def gradient(group, hold):
        pieces = pieces_of(group[0])
        if not pair:
            outs = (jax.ShapeDtypeStruct((peers * depth, width), BF16),)
        else:
            whole = (jax.ShapeDtypeStruct((per * depth, width), BF16),)
            outs = (piece,) * per + ((piece,) * len(pieces) if pieces else whole)
        each = len(outs)
        outs = call(
            functools.partial(grad_kernel, offsets, group, per, pieces),
            outs * len(group),
            [pltpu.VMEM((LANES, width * len(group)), F32)],
            14,
            after(idx, *hold) if hold else idx, *blocks, *payloads, pre_grad,
        )
        outs = [outs[i * each : (i + 1) * each] for i in range(len(group))]
        return [list(o[:per]) for o in outs], [list(o[per:]) for o in outs]

    if pair:
        groups = [(0,)] + [tuple(range(k, min(k + 2, taps - 1))) for k in range(1, taps - 1, 2)] + [(taps - 1,)]
        keep, send, got = [], [], {}
        relays = []

        def work(hold):
            if not groups:
                return
            mine, other = gradient(groups.pop(0), hold)
            for m, o in zip(mine, other):
                keep.append(m)
                send.append((list(first) + o) if len(send) == 0 else o)

        def launch(tap, hold):
            while len(send) <= tap:
                work(hold)
            got[tap] = [swap(after(v, *hold) if hold else v, "seq", 1) for v in send[tap]]

        work([])
        launch(0, [])
        launch(1, [])

        def share(c, last):
            tap, row = c // per, c % per
            value = got[tap][row] if len(got[tap]) > 1 else got[tap][0][row * depth : (row + 1) * depth]
            hold = [] if last is None else [last]
            if c == per:
                relays.extend([swap(after(e, last), "mp", bits[-1]) for e in encs])
            if c == 2 * per:
                hold = hold + relays
            if hold:
                value = after(value, *hold)
            return added(keep[tap][row], value)

        def sent(c, last):
            if c == per - 1:
                work([last] + encs[1:])
                work([last])
            if c % per == per - 1 and c // per + 2 < taps:
                launch(c // per + 2, [last])

        sums, late = chain_sums(taps * per, share, sent)
        encs = encs + relays
        sums = [jnp.concatenate(sums[k * per : (k + 1) * per], axis=0) for k in range(taps)]
    else:
        sums = [gradient((k,), [])[1][0][0] for k in range(taps)]
        sums = [lax.psum_scatter(v, "seq", scatter_dimension=0, tiled=True) for v in sums]
        sums = [lax.psum(v, "dp").astype(F32) for v in sums]
        encs = encs + [swap(e, "mp", bits[-1]) for e in encs]
        late = encs[-1]
    conv_grad = jnp.stack(sums, axis=1)

    qkv = call(
        functools.partial(qkv_kernel, offsets),
        jax.ShapeDtypeStruct((half, qkv_weight.shape[1]), BF16),
        [],
        8,
        after(idx, late), *encs, *payloads, qkv_weight,
    )
    return (qkv[None], conv_grad)


def solution(mesh):
    return jax.shard_map(
        on_device,
        mesh=mesh,
        in_specs=(
            P("dp", "seq", "mp"),
            P(None, None, "mp"),
            P("mp"),
            P(None, "mp"),
            P("dp", "seq", "mp"),
        ),
        out_specs=(P("dp", "seq", "mp"), P("seq", None, "mp")),
        check_vma=False,
    )
```

```python
import functools

import jax
import jax.numpy as jnp
from jax import lax
from jax.experimental import pallas as pl
from jax.experimental.pallas import tpu as pltpu
from jax.sharding import PartitionSpec as P

EDGE = 8
LANES = 128
F32 = jnp.float32
BF16 = jnp.bfloat16


def gelu_parts(v):
    u = 0.7978845608 * (v + 0.044715 * v * v * v)
    th = jnp.tanh(u)
    value = 0.5 * v * (1.0 + th)
    slope = 0.5 * (1.0 + th) + 0.5 * v * (1.0 - th * th) * 0.7978845608 * (1.0 + 0.134145 * v * v)
    return value, slope


def swap(value, axis, bit):
    peers = lax.axis_size(axis)
    return lax.ppermute(value, axis, [(i, i ^ bit) for i in range(peers)])


def edge_block(ref, depth):
    rows = jnp.concatenate([ref[0:8, :], jnp.zeros((LANES - 8, ref.shape[1]), F32)], axis=0)
    keep = lax.broadcasted_iota(jnp.int32, rows.shape, 0) < 4
    return jnp.where(keep, rows, 0.0).T[0:depth, :].astype(BF16)


def conv_rows(offsets, me, x_refs, halo_refs, w_ref, rows_scr, y_scr, w_scr, sems):
    taps, width = w_ref.shape[0], w_ref.shape[2]
    length = x_refs[0].shape[1]
    depth = w_scr.shape[1] // len(offsets)

    def copies(k):
        return [
            pltpu.make_async_copy(
                w_ref.at[k, pl.ds(pl.multiple_of((me ^ off) * depth, 16), depth), :],
                w_scr.at[k, j * depth : (j + 1) * depth, :],
                sems.at[k, j],
            )
            for j, off in enumerate(offsets)
        ]

    for k in range(taps):
        for copy in copies(k):
            copy.start()
    x = jnp.concatenate([ref[...] for ref in x_refs], axis=0)
    halo = jnp.concatenate([edge_block(ref, depth) for ref in halo_refs], axis=0)
    rows_scr[0:length, :] = x.T
    rows_scr[length : length + 16, :] = halo.T[0:16]
    for first in range(0, taps, 2):
        group = range(first, min(first + 2, taps))
        for k in group:
            for copy in copies(k):
                copy.wait()
        w = jnp.concatenate([w_scr[k] for k in group], axis=1)
        y = jnp.dot(rows_scr[...], w, preferred_element_type=F32)
        for c in range(w.shape[1] // LANES):
            part = y[:, c * LANES : (c + 1) * LANES]
            at = first * width // LANES + c
            y_scr[at, EDGE : EDGE + length, :] = part[0:length]
            y_scr[at, EDGE - 2 : EDGE, :] = part[length : length + 2]
            y_scr[at, EDGE + length : EDGE + length + 2, :] = part[length + 2 : length + 4]


def tap_sum(y_scr, start, count, phase, taps, c):
    total = None
    for k in range(taps):
        at = k * (y_scr.shape[0] // taps) + c
        part = y_scr[at, pl.ds(EDGE + 2 * start + phase + k - 2, count, stride=2), :]
        total = part if total is None else total + part
    return total


def first_kernel(offsets, idx_ref, *refs):
    n = len(offsets)
    *x_refs, w_ref, even_ref, odd_ref, rows_scr, y_scr, w_scr, sems = refs
    x_refs, halo_refs = x_refs[:-n], x_refs[-n:]
    conv_rows(offsets, idx_ref[0], x_refs, halo_refs, w_ref, rows_scr, y_scr, w_scr, sems)
    taps, width = w_ref.shape[0], w_ref.shape[2]
    half = even_ref.shape[0]
    step = min(64, half)
    for start in range(0, half, step):
        rows = slice(start, start + step)
        for c in range(width // LANES):
            lanes = slice(c * LANES, (c + 1) * LANES)
            even_ref[rows, lanes] = tap_sum(y_scr, start, step, 0, taps, c)
            odd_ref[rows, lanes] = tap_sum(y_scr, start, step, 1, taps, c)


def second_kernel(offsets, far, per, idx_ref, *refs):
    n = len(offsets)
    blocks, pays, refs = refs[:n], refs[n : 2 * n], refs[2 * n :]
    w_ref, even_ref, odd_ref, grad_ref, enc_ref, pre_ref, *sent_refs = refs[:-7]
    rows_scr, y_scr, w_scr, sems, p_scr, x_scr, edge_scr = refs[-7:]
    me = idx_ref[0]
    pick = lambda items: [items[j] for j in far]
    conv_rows(pick(offsets), me, pick(blocks), pick(pays), w_ref, rows_scr, y_scr, w_scr, sems)
    taps, width = w_ref.shape[0], w_ref.shape[2]
    half = even_ref.shape[0]
    step = min(64, half)
    length = 2 * half
    zero = jnp.zeros((EDGE, width), F32)
    pre_ref[0:EDGE, :] = zero
    pre_ref[EDGE + length : 2 * EDGE + length, :] = zero
    for start in range(0, half, step):
        rows = slice(start, start + step)
        for c in range(width // LANES):
            lanes = slice(c * LANES, (c + 1) * LANES)
            even = even_ref[rows, lanes] + tap_sum(y_scr, start, step, 0, taps, c)
            odd = odd_ref[rows, lanes] + tap_sum(y_scr, start, step, 1, taps, c)
            act_even, slope_even = gelu_parts(even)
            act_odd, slope_odd = gelu_parts(odd)
            enc_ref[rows, lanes] = (0.5 * (act_even + act_odd)).astype(BF16)
            spread = grad_ref[rows, lanes].astype(F32)
            p_scr[c, pl.ds(2 * start, step, stride=2), :] = slope_even * 0.5 * spread
            p_scr[c, pl.ds(2 * start + 1, step, stride=2), :] = slope_odd * 0.5 * spread
    for c in range(width // LANES):
        lanes = slice(c * LANES, (c + 1) * LANES)
        pre_ref[EDGE : EDGE + length, lanes] = p_scr[c].astype(BF16).astype(F32)
    if not sent_refs:
        return
    wanted = (1 - idx_ref[1]) * per
    depth = blocks[0].shape[0]
    for off, block, pay in zip(offsets, blocks, pays):

        @pl.when(me ^ off == wanted)
        def _(block=block, pay=pay):
            x_scr[:, 0:length] = block[...]
            x_scr[:, length : length + LANES] = edge_block(pay, depth)

    p, edge = shifted_rows(pre_ref, edge_scr, (0,))
    res = jnp.dot(x_scr[:, 0:length], p, preferred_element_type=F32)
    res = res + jnp.dot(x_scr[:, length : length + LANES], edge, preferred_element_type=F32)
    sent_refs[0][...] = res.astype(BF16)


def shifted_rows(p_ref, edge_scr, group):
    length, width = p_ref.shape[0] - 2 * EDGE, p_ref.shape[1]
    edge_scr[...] = jnp.zeros_like(edge_scr)
    shifted = []
    for i, tap in enumerate(group):
        cols = slice(i * width, (i + 1) * width)
        edge_scr[0:2, cols] = p_ref[EDGE - tap : EDGE - tap + 2, :]
        edge_scr[2:4, cols] = p_ref[EDGE + length + 2 - tap : EDGE + length + 4 - tap, :]
        shifted.append(p_ref[EDGE + 2 - tap : EDGE + 2 - tap + length, :].astype(BF16))
    return jnp.concatenate(shifted, axis=1), edge_scr[...].astype(BF16)


def grad_kernel(offsets, group, per, pieces, idx_ref, *refs):
    n = len(offsets)
    blocks, pays, p_ref = refs[:n], refs[n : 2 * n], refs[2 * n]
    out_refs, edge_scr = list(refs[2 * n + 1 : -1]), refs[-1]
    width = p_ref.shape[1]
    p, edge = shifted_rows(p_ref, edge_scr, group)
    me = idx_ref[0]
    x = jnp.concatenate([ref[...] for ref in blocks], axis=0)
    depth = x.shape[0] // n
    halo = jnp.concatenate([edge_block(ref, depth) for ref in pays], axis=0)
    res = jnp.dot(x, p, preferred_element_type=F32) + jnp.dot(halo, edge, preferred_element_type=F32)
    res = res.astype(BF16)
    for i in range(len(group)):
        own_ref = out_refs.pop(0)
        other_refs = [out_refs.pop(0) for _ in range(len(pieces[i]) or min(per, 1))]
        for j, off in enumerate(offsets):
            part = res[j * depth : (j + 1) * depth, i * width : (i + 1) * width]
            at = me ^ off
            if not per:
                own_ref[pl.ds(pl.multiple_of(at * depth, 16), depth), :] = part
                continue
            mine = lax.div(at, per) == idx_ref[1]
            other = jnp.logical_not(mine)
            row = lax.rem(at, per)
            hits = [(own_ref, mine)]
            if not pieces[i]:
                hits.append((other_refs[0], other))
            for ref, hit in hits:

                @pl.when(hit)
                def _(ref=ref, part=part, row=row):
                    ref[pl.ds(pl.multiple_of(row * depth, 16), depth), :] = part

            for r, ref in zip(pieces[i], other_refs):

                @pl.when(jnp.logical_and(other, row == r))
                def _(ref=ref, part=part):
                    ref[...] = part


def qkv_kernel(offsets, idx_ref, *refs):
    n = len(offsets)
    enc_refs, gain_refs, (w_ref, out_ref) = refs[:n], refs[n : 2 * n], refs[2 * n :]
    depth = enc_refs[0].shape[1]
    values = [ref[...].astype(F32) for ref in enc_refs]
    channels = n * depth
    sums = sum(jnp.sum(v, axis=1, keepdims=True) for v in values)
    squares = sum(jnp.sum(v * v, axis=1, keepdims=True) for v in values)
    mean = sums / channels
    var = squares / channels - mean * mean
    scale = lax.rsqrt(var + 1e-05)
    total = None
    for off, v, gain_ref in zip(offsets, values, gain_refs):
        normal = ((v - mean) * scale * gain_ref[4:5, 0:depth]).astype(BF16)
        w = w_ref[pl.ds(pl.multiple_of((idx_ref[0] ^ off) * depth, 16), depth), :]
        part = jnp.dot(normal, w, preferred_element_type=F32)
        total = part if total is None else total + part
    out_ref[...] = total.astype(BF16)


def call(kernel, out, scratch, mib, idx, *arrays, far_off=()):
    vmem = pl.BlockSpec(memory_space=pltpu.VMEM)
    held = [j for j, a in enumerate(arrays) if any(v is a for v in far_off)]
    arrays = [pltpu.with_memory_space_constraint(a, pltpu.HBM) if j in held else a for j, a in enumerate(arrays)]
    specs = [pl.BlockSpec(memory_space=pltpu.HBM) if j in held else vmem for j in range(len(arrays))]
    return pl.pallas_call(
        kernel,
        out_shape=out,
        in_specs=[pl.BlockSpec(memory_space=pltpu.SMEM)] + specs,
        out_specs=jax.tree.map(lambda _: vmem, out),
        scratch_shapes=scratch,
        compiler_params=pltpu.CompilerParams(vmem_limit_bytes=mib * 1024 * 1024),
    )(idx, *arrays)


def after(value, *others):
    return lax.optimization_barrier((value, *others))[0]


def write_kernel(*refs):
    *part_refs, out_ref = refs
    pieces = len(part_refs) // out_ref.shape[0]
    rows = part_refs[0].shape[0]
    for i, ref in enumerate(part_refs):
        tap, r = i // pieces, i % pieces
        out_ref[tap, r * rows : (r + 1) * rows, :] = ref[...].astype(F32)


def written(parts, taps, at, buffer, shape):
    rows, width = parts[0].shape
    extra = [] if buffer is None else [buffer]
    kernel = write_kernel if buffer is None else lambda b, *refs: write_kernel(*refs)
    return pl.pallas_call(
        kernel,
        out_shape=jax.ShapeDtypeStruct(shape, F32),
        grid=(1,),
        in_specs=[pl.BlockSpec(memory_space=pl.ANY)] * len(extra)
        + [pl.BlockSpec((rows, width), lambda i: (0, 0))] * len(parts),
        out_specs=pl.BlockSpec((taps, shape[1], width), lambda i: (at // taps, 0, 0)),
        input_output_aliases={0: 0} if extra else {},
        compiler_params=pltpu.CompilerParams(vmem_limit_bytes=16 * 1024 * 1024),
    )(*extra, *parts)


def edge_kernel(head_ref, tail_ref, out_ref):
    depth = head_ref.shape[0]
    extra = jnp.zeros((out_ref.shape[1] - depth, LANES), F32)
    head = jnp.concatenate([head_ref[...].astype(F32), extra], axis=0).T
    tail = jnp.concatenate([tail_ref[...].astype(F32), extra], axis=0).T
    out_ref[...] = jnp.zeros_like(out_ref)
    out_ref[0:2, :] = head[0:2]
    out_ref[2:4, :] = tail[LANES - 2 : LANES]


def edge_rows(x, width):
    peers = lax.axis_size("seq")
    me = lax.axis_index("seq")
    depth, length = x.shape
    ends = pl.pallas_call(
        edge_kernel,
        out_shape=jax.ShapeDtypeStruct((8, width), F32),
        grid=(1,),
        in_specs=[
            pl.BlockSpec((depth, LANES), lambda i: (0, 0)),
            pl.BlockSpec((depth, LANES), lambda i: (0, length // LANES - 1)),
        ],
        out_specs=pl.BlockSpec((8, width), lambda i: (0, 0)),
        compiler_params=pltpu.CompilerParams(vmem_limit_bytes=2 * 1024 * 1024),
    )(x, x)
    if peers == 2:
        before = behind = swap(ends, "seq", 1)
    else:
        up = [(i, (i + 1) % peers) for i in range(peers - 1)]
        down = [(j, i) for i, j in up]
        before, behind = lax.ppermute(ends, "seq", up), lax.ppermute(ends, "seq", down)
    before = jnp.where(me == 0, 0.0, before[2:4])
    behind = jnp.where(me == peers - 1, 0.0, behind[0:2])
    return jnp.concatenate([before, behind], axis=0)


def added(a, b):
    return (a.astype(F32) + b.astype(F32)).astype(BF16)


def chain_sums(count, part, sent, idle):
    me = lax.axis_index("dp")
    end = jnp.logical_or(me == 0, me == 3)
    outer_pairs = [(0, 1), (1, 0), (2, 3), (3, 2)]
    middle_pairs = [(0, 0), (1, 2), (2, 1), (3, 3)]
    last = None
    h, p, s, outer, middle, sums = {}, {}, {}, {}, {}, {}
    for r in range(count + 3):
        if r - 2 in middle:
            got = after(middle.pop(r - 2), last)
            last = s[r - 2] = lax.optimization_barrier(added(p[r - 2], got))
        if r < count:
            last = h[r] = part(r, last)
        if r < count + 2:
            value = h.get(r, s.get(r - 2))
            if r in h and r - 2 in s:
                value = jnp.where(end, h[r], s[r - 2])
            last = value = lax.optimization_barrier(value)
            outer[r] = lax.ppermute(value, "dp", outer_pairs)
            last = sent(r, last)
        if r - 1 in outer:
            got = after(outer.pop(r - 1), last)
            if r - 1 < count:
                last = p[r - 1] = lax.optimization_barrier(added(h[r - 1], got))
                middle[r - 1] = lax.ppermute(last, "dp", middle_pairs)
            if r >= 3:
                sums[r - 3] = jnp.where(end, got, s[r - 3])
            if r - 1 < count:
                last = idle(r - 1, last, sums)
    return [sums[c] for c in range(count)]


def on_device(block_input, conv_weight, norm_gain, qkv_weight, encoder_grad):
    x = jnp.swapaxes(block_input[0], 0, 1)
    depth, length = x.shape
    taps, _, width = conv_weight.shape
    peers, shards = lax.axis_size("mp"), lax.axis_size("seq")
    bits = [1 << b for b in reversed(range(peers.bit_length() - 1))]
    idx = jnp.stack([lax.axis_index("mp"), lax.axis_index("seq")]).astype(jnp.int32)

    offsets = [0]
    for bit in bits:
        offsets = offsets + [o ^ bit for o in offsets]
    near = [j for j, o in enumerate(offsets) if o < 2]
    far = [j for j, o in enumerate(offsets) if o >= 2]
    half = length // 2
    pick = lambda items, at: [items[j] for j in at]
    scratch = lambda at: [
        pltpu.VMEM((length + 16, len(at) * depth), BF16),
        pltpu.VMEM((taps * width // LANES, length + 2 * EDGE, LANES), F32),
        pltpu.VMEM((taps, len(at) * depth, width), BF16),
        pltpu.SemaphoreType.DMA((taps, len(at))),
    ]

    blocks = [x]
    for bit in bits[:-1]:
        blocks = blocks + [swap(b, "mp", bit) for b in blocks]
    own = swap(x, "mp", bits[-1])
    edges = edge_rows(x, width)
    payload = jnp.concatenate([edges, norm_gain.reshape(1, -1), jnp.zeros((3, width), F32)], axis=0)
    payloads = [payload] + [swap(payload, "mp", o) for o in offsets[1:]]

    part = jax.ShapeDtypeStruct((half, width), F32)
    even, odd = call(
        functools.partial(first_kernel, pick(offsets, near)),
        (part, part),
        scratch(near),
        24,
        idx, x, own, *pick(payloads, near), conv_weight,
        far_off=(conv_weight,),
    )
    hold = [even] + pick(payloads, far)
    blocks = blocks + [own] + [swap(after(b, *hold), "mp", bits[-1]) for b in blocks[1:]]
    pair = shards == 2 and peers % shards == 0 and lax.axis_size("dp") == 4
    per = peers // shards if pair else 0
    piece = jax.ShapeDtypeStruct((depth, width), BF16)
    encoded, pre_grad, *first = call(
        functools.partial(second_kernel, offsets, far, per),
        (
            jax.ShapeDtypeStruct((half, width), BF16),
            jax.ShapeDtypeStruct((length + 2 * EDGE, width), F32),
            *([piece] if pair else []),
        ),
        scratch(far)
        + [
            pltpu.VMEM((width // LANES, length, LANES), F32),
            pltpu.VMEM((depth, length + LANES), BF16),
            pltpu.VMEM((LANES, width), F32),
        ],
        26,
        idx, *blocks, *payloads, conv_weight, even, odd, encoder_grad[0],
        far_off=(conv_weight,),
    )
    encs = [encoded]
    for bit in bits[:-1]:
        encs = encs + [swap(e, "mp", bit) for e in encs]

    everything = tuple(range(per))
    pieces_of = lambda k: (everything[1:], everything)[k] if k < 2 else ()

    def gradient(group, hold):
        pieces = [pieces_of(k) for k in group]
        outs = []
        for q in pieces:
            if not pair:
                outs.append([jax.ShapeDtypeStruct((peers * depth, width), BF16)])
                continue
            whole = jax.ShapeDtypeStruct((per * depth, width), BF16)
            outs.append([whole] + ([piece] * len(q) if q else [whole]))
        flat = call(
            functools.partial(grad_kernel, offsets, group, per, pieces),
            tuple(o for tap in outs for o in tap),
            [pltpu.VMEM((LANES, width * len(group)), F32)],
            16,
            after(idx, *hold) if hold else idx, *blocks, *payloads, pre_grad,
        )
        flat = list(flat)
        taken = [[flat.pop(0) for _ in tap] for tap in outs]
        return [t[0] for t in taken], [t[1:] for t in taken]

    qkv_call = lambda idx, encs: call(
        functools.partial(qkv_kernel, offsets),
        jax.ShapeDtypeStruct((half, qkv_weight.shape[1]), BF16),
        [],
        8,
        idx, *encs, *payloads, qkv_weight,
    )
    if not pair:
        sums = [gradient((k,), [])[0][0] for k in range(taps)]
        sums = [lax.psum_scatter(v, "seq", scatter_dimension=0, tiled=True) for v in sums]
        sums = [lax.psum(v, "dp").astype(F32) for v in sums]
        encs = encs + [swap(e, "mp", bits[-1]) for e in encs]
        return (qkv_call(idx, encs)[None], jnp.stack(sums, axis=1))

    chunks = taps * per
    keep, send, got, relays, done = [], [], {}, [], {}

    def work(group, hold):
        if not group:
            return
        mine, other = gradient(group, hold)
        keep.extend(mine)
        send.extend(other if send else [list(first) + other[0]] + other[1:])

    def launch(tap, hold):
        if tap < taps:
            got[tap] = [swap(after(v, *hold) if hold else v, "seq", 1) for v in send[tap]]

    work((0,), [])
    launch(0, [])

    def share(c, last):
        tap, row = c // per, c % per
        rows = slice(row * depth, (row + 1) * depth)
        value = got[tap][row] if len(got[tap]) > 1 else got[tap][0][rows]
        return added(keep[tap][rows], value if last is None else after(value, last))

    def sent(r, last):
        if r == 0:
            work(tuple(range(1, min(3, taps))), [last])
            launch(1, [])
            last = keep[-1]
        return last

    def idle(c, last, sums):
        if c == 0:
            work(tuple(range(3, taps)), [last] + encs[1:])
            last = keep[-1]
        if c == 1:
            relays.extend([swap(after(e, last), "mp", bits[-1]) for e in encs])
        if c % per == 0 and c // per + 2 < taps:
            launch(c // per + 2, [last])
        if c == chunks - 4:
            last = done["qkv"] = qkv_call(after(idx, last, *relays), encs + relays)
        if c == chunks - 1:
            early = (len(sums) // per) if len(sums) >= per * (taps - 1) else 0
            if early:
                parts = [sums[i] for i in range(early * per)]
                parts[0] = after(parts[0], last)
                last = done["early"] = written(parts, early, 0, None, (taps, per * depth, width))
        return last

    sums = chain_sums(chunks, share, sent, idle)
    shape = (taps, per * depth, width)
    if "early" in done:
        conv_grad = written(sums[(taps - 1) * per :], 1, taps - 1, done["early"], shape)
    else:
        conv_grad = written(sums, taps, 0, None, shape)
    return (done["qkv"][None], jnp.swapaxes(conv_grad, 0, 1))


def solution(mesh):
    return jax.shard_map(
        on_device,
        mesh=mesh,
        in_specs=(
            P("dp", "seq", "mp"),
            P(None, None, "mp"),
            P("mp"),
            P(None, "mp"),
            P("dp", "seq", "mp"),
        ),
        out_specs=(P("dp", "seq", "mp"), P("seq", None, "mp")),
        check_vma=False,
    )
```

```python
import functools

import jax
import jax.numpy as jnp
from jax import lax
from jax.experimental import pallas as pl
from jax.experimental.pallas import tpu as pltpu
from jax.sharding import PartitionSpec as P

EDGE = 8
LANES = 128
F32 = jnp.float32
BF16 = jnp.bfloat16


def gelu_parts(v):
    u = 0.7978845608 * (v + 0.044715 * v * v * v)
    th = jnp.tanh(u)
    value = 0.5 * v * (1.0 + th)
    slope = 0.5 * (1.0 + th) + 0.5 * v * (1.0 - th * th) * 0.7978845608 * (1.0 + 0.134145 * v * v)
    return value, slope


def swap(value, axis, bit):
    peers = lax.axis_size(axis)
    return lax.ppermute(value, axis, [(i, i ^ bit) for i in range(peers)])


def edge_block(ref, depth):
    rows = jnp.concatenate([ref[0:8, :], jnp.zeros((LANES - 8, ref.shape[1]), F32)], axis=0)
    keep = lax.broadcasted_iota(jnp.int32, rows.shape, 0) < 4
    return jnp.where(keep, rows, 0.0).T[0:depth, :].astype(BF16)


def conv_rows(offsets, me, x_refs, halo_refs, w_ref, rows_scr, y_scr):
    taps, width = w_ref.shape[0], w_ref.shape[2]
    length = x_refs[0].shape[1]
    x = jnp.concatenate([ref[...] for ref in x_refs], axis=0)
    depth = x.shape[0] // len(offsets)
    halo = jnp.concatenate([edge_block(ref, depth) for ref in halo_refs], axis=0)
    rows_scr[0:length, :] = x.T
    rows_scr[length : length + 16, :] = halo.T[0:16]
    starts = [pl.multiple_of((me ^ off) * depth, 16) for off in offsets]
    for first in range(0, taps, 2):
        group = range(first, min(first + 2, taps))
        w = jnp.concatenate(
            [
                jnp.concatenate([w_ref[k, pl.ds(s, depth), :] for s in starts], axis=0)
                for k in group
            ],
            axis=1,
        )
        y = jnp.dot(rows_scr[...], w, preferred_element_type=F32)
        for c in range(w.shape[1] // LANES):
            part = y[:, c * LANES : (c + 1) * LANES]
            at = first * width // LANES + c
            y_scr[at, EDGE : EDGE + length, :] = part[0:length]
            y_scr[at, EDGE - 2 : EDGE, :] = part[length : length + 2]
            y_scr[at, EDGE + length : EDGE + length + 2, :] = part[length + 2 : length + 4]


def tap_sum(y_scr, start, count, phase, taps, c):
    total = None
    for k in range(taps):
        at = k * (y_scr.shape[0] // taps) + c
        part = y_scr[at, pl.ds(EDGE + 2 * start + phase + k - 2, count, stride=2), :]
        total = part if total is None else total + part
    return total


def first_kernel(offsets, idx_ref, *refs):
    n = len(offsets)
    *x_refs, w_ref, even_ref, odd_ref, rows_scr, y_scr = refs
    x_refs, halo_refs = x_refs[:-n], x_refs[-n:]
    conv_rows(offsets, idx_ref[0], x_refs, halo_refs, w_ref, rows_scr, y_scr)
    taps, width = w_ref.shape[0], w_ref.shape[2]
    half = even_ref.shape[0]
    step = min(64, half)
    for start in range(0, half, step):
        rows = slice(start, start + step)
        for c in range(width // LANES):
            lanes = slice(c * LANES, (c + 1) * LANES)
            even_ref[rows, lanes] = tap_sum(y_scr, start, step, 0, taps, c)
            odd_ref[rows, lanes] = tap_sum(y_scr, start, step, 1, taps, c)


def second_kernel(offsets, far, per, idx_ref, *refs):
    n = len(offsets)
    blocks, pays, refs = refs[:n], refs[n : 2 * n], refs[2 * n :]
    w_ref, even_ref, odd_ref, grad_ref, enc_ref, pre_ref, *sent_refs = refs[:-5]
    rows_scr, y_scr, p_scr, x_scr, edge_scr = refs[-5:]
    me = idx_ref[0]
    pick = lambda items: [items[j] for j in far]
    conv_rows(pick(offsets), me, pick(blocks), pick(pays), w_ref, rows_scr, y_scr)
    taps, width = w_ref.shape[0], w_ref.shape[2]
    half = even_ref.shape[0]
    step = min(64, half)
    length = 2 * half
    zero = jnp.zeros((EDGE, width), F32)
    pre_ref[0:EDGE, :] = zero
    pre_ref[EDGE + length : 2 * EDGE + length, :] = zero
    for start in range(0, half, step):
        rows = slice(start, start + step)
        for c in range(width // LANES):
            lanes = slice(c * LANES, (c + 1) * LANES)
            even = even_ref[rows, lanes] + tap_sum(y_scr, start, step, 0, taps, c)
            odd = odd_ref[rows, lanes] + tap_sum(y_scr, start, step, 1, taps, c)
            act_even, slope_even = gelu_parts(even)
            act_odd, slope_odd = gelu_parts(odd)
            enc_ref[rows, lanes] = (0.5 * (act_even + act_odd)).astype(BF16)
            spread = grad_ref[rows, lanes].astype(F32)
            p_scr[c, pl.ds(2 * start, step, stride=2), :] = slope_even * 0.5 * spread
            p_scr[c, pl.ds(2 * start + 1, step, stride=2), :] = slope_odd * 0.5 * spread
    for c in range(width // LANES):
        lanes = slice(c * LANES, (c + 1) * LANES)
        pre_ref[EDGE : EDGE + length, lanes] = p_scr[c].astype(BF16).astype(F32)
    if not sent_refs:
        return
    wanted = (1 - idx_ref[1]) * per
    depth = blocks[0].shape[0]
    for off, block, pay in zip(offsets, blocks, pays):

        @pl.when(me ^ off == wanted)
        def _(block=block, pay=pay):
            x_scr[:, 0:length] = block[...]
            x_scr[:, length : length + LANES] = edge_block(pay, depth)

    p, edge = shifted_rows(pre_ref, edge_scr, (0,))
    res = jnp.dot(x_scr[:, 0:length], p, preferred_element_type=F32)
    res = res + jnp.dot(x_scr[:, length : length + LANES], edge, preferred_element_type=F32)
    sent_refs[0][...] = res.astype(BF16)


def shifted_rows(p_ref, edge_scr, group):
    length, width = p_ref.shape[0] - 2 * EDGE, p_ref.shape[1]
    edge_scr[...] = jnp.zeros_like(edge_scr)
    shifted = []
    for i, tap in enumerate(group):
        cols = slice(i * width, (i + 1) * width)
        edge_scr[0:2, cols] = p_ref[EDGE - tap : EDGE - tap + 2, :]
        edge_scr[2:4, cols] = p_ref[EDGE + length + 2 - tap : EDGE + length + 4 - tap, :]
        shifted.append(p_ref[EDGE + 2 - tap : EDGE + 2 - tap + length, :].astype(BF16))
    return jnp.concatenate(shifted, axis=1), edge_scr[...].astype(BF16)


def grad_kernel(offsets, group, per, pieces, idx_ref, *refs):
    n = len(offsets)
    blocks, pays, p_ref = refs[:n], refs[n : 2 * n], refs[2 * n]
    out_refs, edge_scr = list(refs[2 * n + 1 : -1]), refs[-1]
    width = p_ref.shape[1]
    p, edge = shifted_rows(p_ref, edge_scr, group)
    me = idx_ref[0]
    x = jnp.concatenate([ref[...] for ref in blocks], axis=0)
    depth = x.shape[0] // n
    halo = jnp.concatenate([edge_block(ref, depth) for ref in pays], axis=0)
    res = jnp.dot(x, p, preferred_element_type=F32) + jnp.dot(halo, edge, preferred_element_type=F32)
    res = res.astype(BF16)
    for i in range(len(group)):
        own_ref = out_refs.pop(0)
        other_refs = [out_refs.pop(0) for _ in range(len(pieces[i]) or min(per, 1))]
        for j, off in enumerate(offsets):
            part = res[j * depth : (j + 1) * depth, i * width : (i + 1) * width]
            at = me ^ off
            if not per:
                own_ref[pl.ds(pl.multiple_of(at * depth, 16), depth), :] = part
                continue
            mine = lax.div(at, per) == idx_ref[1]
            other = jnp.logical_not(mine)
            row = lax.rem(at, per)
            hits = [(own_ref, mine)]
            if not pieces[i]:
                hits.append((other_refs[0], other))
            for ref, hit in hits:

                @pl.when(hit)
                def _(ref=ref, part=part, row=row):
                    ref[pl.ds(pl.multiple_of(row * depth, 16), depth), :] = part

            for r, ref in zip(pieces[i], other_refs):

                @pl.when(jnp.logical_and(other, row == r))
                def _(ref=ref, part=part):
                    ref[...] = part


def qkv_kernel(offsets, idx_ref, *refs):
    n = len(offsets)
    enc_refs, gain_refs, (w_ref, out_ref) = refs[:n], refs[n : 2 * n], refs[2 * n :]
    depth = enc_refs[0].shape[1]
    values = [ref[...].astype(F32) for ref in enc_refs]
    channels = n * depth
    sums = sum(jnp.sum(v, axis=1, keepdims=True) for v in values)
    squares = sum(jnp.sum(v * v, axis=1, keepdims=True) for v in values)
    mean = sums / channels
    var = squares / channels - mean * mean
    scale = lax.rsqrt(var + 1e-05)
    total = None
    for off, v, gain_ref in zip(offsets, values, gain_refs):
        normal = ((v - mean) * scale * gain_ref[4:5, 0:depth]).astype(BF16)
        w = w_ref[pl.ds(pl.multiple_of((idx_ref[0] ^ off) * depth, 16), depth), :]
        part = jnp.dot(normal, w, preferred_element_type=F32)
        total = part if total is None else total + part
    out_ref[...] = total.astype(BF16)


def call(kernel, out, scratch, mib, idx, *arrays):
    vmem = pl.BlockSpec(memory_space=pltpu.VMEM)
    return pl.pallas_call(
        kernel,
        out_shape=out,
        in_specs=[pl.BlockSpec(memory_space=pltpu.SMEM)] + [vmem] * len(arrays),
        out_specs=jax.tree.map(lambda _: vmem, out),
        scratch_shapes=scratch,
        compiler_params=pltpu.CompilerParams(vmem_limit_bytes=mib * 1024 * 1024),
    )(idx, *arrays)


def pinned(value):
    return pltpu.with_memory_space_constraint(value, pltpu.VMEM)


def after(value, *others):
    return lax.optimization_barrier((value, *others))[0]


def write_kernel(*refs):
    *part_refs, out_ref = refs
    pieces = len(part_refs) // out_ref.shape[0]
    rows = part_refs[0].shape[0]
    for i, ref in enumerate(part_refs):
        tap, r = i // pieces, i % pieces
        out_ref[tap, r * rows : (r + 1) * rows, :] = ref[...].astype(F32)


def written(parts, taps, at, buffer, shape):
    rows, width = parts[0].shape
    extra = [] if buffer is None else [buffer]
    kernel = write_kernel if buffer is None else lambda b, *refs: write_kernel(*refs)
    return pl.pallas_call(
        kernel,
        out_shape=jax.ShapeDtypeStruct(shape, F32),
        grid=(1,),
        in_specs=[pl.BlockSpec(memory_space=pl.ANY)] * len(extra)
        + [pl.BlockSpec((rows, width), lambda i: (0, 0))] * len(parts),
        out_specs=pl.BlockSpec((taps, shape[1], width), lambda i: (at // taps, 0, 0)),
        input_output_aliases={0: 0} if extra else {},
        compiler_params=pltpu.CompilerParams(vmem_limit_bytes=16 * 1024 * 1024),
    )(*extra, *parts)


def edge_kernel(head_ref, tail_ref, out_ref):
    depth = head_ref.shape[0]
    extra = jnp.zeros((out_ref.shape[1] - depth, LANES), F32)
    head = jnp.concatenate([head_ref[...].astype(F32), extra], axis=0).T
    tail = jnp.concatenate([tail_ref[...].astype(F32), extra], axis=0).T
    out_ref[...] = jnp.zeros_like(out_ref)
    out_ref[0:2, :] = head[0:2]
    out_ref[2:4, :] = tail[LANES - 2 : LANES]


def edge_rows(x, width):
    peers = lax.axis_size("seq")
    me = lax.axis_index("seq")
    depth, length = x.shape
    ends = pl.pallas_call(
        edge_kernel,
        out_shape=jax.ShapeDtypeStruct((8, width), F32),
        grid=(1,),
        in_specs=[
            pl.BlockSpec((depth, LANES), lambda i: (0, 0)),
            pl.BlockSpec((depth, LANES), lambda i: (0, length // LANES - 1)),
        ],
        out_specs=pl.BlockSpec((8, width), lambda i: (0, 0)),
        compiler_params=pltpu.CompilerParams(vmem_limit_bytes=2 * 1024 * 1024),
    )(x, x)
    if peers == 2:
        before = behind = swap(ends, "seq", 1)
    else:
        up = [(i, (i + 1) % peers) for i in range(peers - 1)]
        down = [(j, i) for i, j in up]
        before, behind = lax.ppermute(ends, "seq", up), lax.ppermute(ends, "seq", down)
    before = jnp.where(me == 0, 0.0, before[2:4])
    behind = jnp.where(me == peers - 1, 0.0, behind[0:2])
    return jnp.concatenate([before, behind], axis=0)


def added(a, b):
    return (a.astype(F32) + b.astype(F32)).astype(BF16)


def chain_sums(count, part, sent, idle):
    me = lax.axis_index("dp")
    end = jnp.logical_or(me == 0, me == 3)
    outer_pairs = [(0, 1), (1, 0), (2, 3), (3, 2)]
    middle_pairs = [(0, 0), (1, 2), (2, 1), (3, 3)]
    last = None
    h, p, s, outer, middle, sums = {}, {}, {}, {}, {}, {}
    for r in range(count + 5):
        if r < count:
            last = h[r] = part(r, last)
        if r < count + 3:
            value = h.get(r, s.get(r - 3))
            if r in h and r - 3 in s:
                value = jnp.where(end, h[r], s[r - 3])
            last = value = lax.optimization_barrier(value)
            outer[r] = lax.ppermute(value, "dp", outer_pairs)
            last = sent(r, last)
        if r - 1 in outer:
            got = after(outer.pop(r - 1), last)
            if r - 1 < count:
                last = p[r - 1] = lax.optimization_barrier(added(h[r - 1], got))
                middle[r - 1] = lax.ppermute(last, "dp", middle_pairs)
            if r >= 4:
                sums[r - 4] = lax.optimization_barrier(jnp.where(end, got, s[r - 4]))
                if r - 1 >= count:
                    last = sums[r - 4]
            last = idle(r - 1, last, sums)
        if r - 2 in middle:
            got = after(middle.pop(r - 2), last)
            last = s[r - 2] = lax.optimization_barrier(added(p[r - 2], got))
    return [sums[c] for c in range(count)]


def on_device(block_input, conv_weight, norm_gain, qkv_weight, encoder_grad):
    x = jnp.swapaxes(block_input[0], 0, 1)
    depth, length = x.shape
    taps, _, width = conv_weight.shape
    peers, shards = lax.axis_size("mp"), lax.axis_size("seq")
    bits = [1 << b for b in reversed(range(peers.bit_length() - 1))]
    idx = jnp.stack([lax.axis_index("mp"), lax.axis_index("seq")]).astype(jnp.int32)

    offsets = [0]
    for bit in bits:
        offsets = offsets + [o ^ bit for o in offsets]
    near = [j for j, o in enumerate(offsets) if o < 2]
    far = [j for j, o in enumerate(offsets) if o >= 2]
    half = length // 2
    pick = lambda items, at: [items[j] for j in at]
    scratch = lambda at: [
        pltpu.VMEM((length + 16, len(at) * depth), BF16),
        pltpu.VMEM((taps * width // LANES, length + 2 * EDGE, LANES), F32),
    ]

    blocks = [x]
    for bit in bits[:-1]:
        blocks = blocks + [pinned(swap(b, "mp", bit)) for b in blocks]
    own = pinned(swap(x, "mp", bits[-1]))
    weight = pinned(conv_weight)
    near_x = pinned(x)
    edges = edge_rows(x, width)
    payload = jnp.concatenate([edges, norm_gain.reshape(1, -1), jnp.zeros((3, width), F32)], axis=0)
    payloads = [payload] + [swap(payload, "mp", o) for o in offsets[1:]]

    part = jax.ShapeDtypeStruct((half, width), F32)
    even, odd = call(
        functools.partial(first_kernel, pick(offsets, near)),
        (part, part),
        scratch(near),
        24,
        idx, near_x, own, *pick(payloads, near), weight,
    )
    hold = [even] + pick(payloads, far)
    blocks = blocks + [own] + [pinned(swap(after(b, *hold), "mp", bits[-1])) for b in blocks[1:]]
    blocks[0] = near_x
    pair = shards == 2 and peers % shards == 0 and lax.axis_size("dp") == 4
    per = peers // shards if pair else 0
    piece = jax.ShapeDtypeStruct((depth, width), BF16)
    encoded, pre_grad, *first = call(
        functools.partial(second_kernel, offsets, far, per),
        (
            jax.ShapeDtypeStruct((half, width), BF16),
            jax.ShapeDtypeStruct((length + 2 * EDGE, width), F32),
            *([piece] if pair else []),
        ),
        scratch(far)
        + [
            pltpu.VMEM((width // LANES, length, LANES), F32),
            pltpu.VMEM((depth, length + LANES), BF16),
            pltpu.VMEM((LANES, width), F32),
        ],
        26,
        idx, *blocks, *payloads, weight, even, odd, encoder_grad[0],
    )
    encs = [encoded]
    for bit in bits[:-1]:
        encs = encs + [swap(e, "mp", bit) for e in encs]

    everything = tuple(range(per))
    pieces_of = lambda k: (everything[1:], everything)[k] if k < 2 else ()

    def gradient(group, hold):
        pieces = [pieces_of(k) for k in group]
        outs = []
        for q in pieces:
            if not pair:
                outs.append([jax.ShapeDtypeStruct((peers * depth, width), BF16)])
                continue
            whole = jax.ShapeDtypeStruct((per * depth, width), BF16)
            outs.append([whole] + ([piece] * len(q) if q else [whole]))
        flat = call(
            functools.partial(grad_kernel, offsets, group, per, pieces),
            tuple(o for tap in outs for o in tap),
            [pltpu.VMEM((LANES, width * len(group)), F32)],
            16,
            after(idx, *hold) if hold else idx, *blocks, *payloads, pre_grad,
        )
        flat = list(flat)
        taken = [[flat.pop(0) for _ in tap] for tap in outs]
        return [t[0] for t in taken], [t[1:] for t in taken]

    qkv_call = lambda idx, encs: call(
        functools.partial(qkv_kernel, offsets),
        jax.ShapeDtypeStruct((half, qkv_weight.shape[1]), BF16),
        [],
        8,
        idx, *encs, *payloads, qkv_weight,
    )
    if not pair:
        sums = [gradient((k,), [])[0][0] for k in range(taps)]
        sums = [lax.psum_scatter(v, "seq", scatter_dimension=0, tiled=True) for v in sums]
        sums = [lax.psum(v, "dp").astype(F32) for v in sums]
        encs = encs + [swap(e, "mp", bits[-1]) for e in encs]
        return (qkv_call(idx, encs)[None], jnp.stack(sums, axis=1))

    chunks = taps * per
    keep, send, got, relays, done = [], [], {}, [], {}

    def work(group, hold):
        if not group:
            return
        mine, other = gradient(group, hold)
        keep.extend(mine)
        send.extend(other if send else [list(first) + other[0]] + other[1:])

    def launch(tap, hold):
        if tap < taps:
            got[tap] = [swap(after(v, *hold) if hold else v, "seq", 1) for v in send[tap]]

    work((0,), [])
    launch(0, [])
    work((1,), [keep[-1]])
    launch(1, [])

    def share(c, last):
        tap, row = c // per, c % per
        rows = slice(row * depth, (row + 1) * depth)
        value = got[tap][row] if len(got[tap]) > 1 else got[tap][0][rows]
        return added(keep[tap][rows], value if last is None else after(value, last))

    def sent(r, last):
        return last

    def idle(c, last, sums):
        if c % per == 0 and c // per + 2 < taps:
            tap = c // per + 2
            work((tap,), [last] + (encs[1:] if tap == 2 else []))
            launch(tap, [])
            last = keep[-1]
        if c == per - 1:
            relays.extend([swap(after(e, last), "mp", bits[-1]) for e in encs])
        if c == chunks - 2:
            last = done["qkv"] = qkv_call(after(idx, last, *relays), encs + relays)
        if c == chunks:
            early = len(sums) // per
            parts = [sums[i] for i in range(early * per)]
            parts[0] = after(parts[0], last)
            last = done["early"] = written(parts, early, 0, None, (taps, per * depth, width))
            done["at"] = early
        return last

    sums = chain_sums(chunks, share, sent, idle)
    shape = (taps, per * depth, width)
    conv_grad, early = done["early"], done["at"]
    for k in range(early, taps):
        conv_grad = written(sums[k * per : (k + 1) * per], 1, k, conv_grad, shape)
    return (done["qkv"][None], jnp.swapaxes(conv_grad, 0, 1))


def solution(mesh):
    return jax.shard_map(
        on_device,
        mesh=mesh,
        in_specs=(
            P("dp", "seq", "mp"),
            P(None, None, "mp"),
            P("mp"),
            P(None, "mp"),
            P("dp", "seq", "mp"),
        ),
        out_specs=(P("dp", "seq", "mp"), P("seq", None, "mp")),
        check_vma=False,
    )
```

```python
import functools

import jax
import jax.numpy as jnp
from jax import lax
from jax.experimental import pallas as pl
from jax.experimental.pallas import tpu as pltpu
from jax.sharding import PartitionSpec as P

EDGE = 8
LANES = 128
F32 = jnp.float32
BF16 = jnp.bfloat16


def gelu_parts(v):
    u = 0.7978845608 * (v + 0.044715 * v * v * v)
    th = jnp.tanh(u)
    value = 0.5 * v * (1.0 + th)
    slope = 0.5 * (1.0 + th) + 0.5 * v * (1.0 - th * th) * 0.7978845608 * (1.0 + 0.134145 * v * v)
    return value, slope


def swap(value, axis, bit):
    peers = lax.axis_size(axis)
    return lax.ppermute(value, axis, [(i, i ^ bit) for i in range(peers)])


def edge_block(ref, depth):
    rows = jnp.concatenate([ref[0:8, :], jnp.zeros((LANES - 8, ref.shape[1]), F32)], axis=0)
    keep = lax.broadcasted_iota(jnp.int32, rows.shape, 0) < 4
    return jnp.where(keep, rows, 0.0).T[0:depth, :].astype(BF16)


def conv_rows(offsets, me, x_refs, halo_refs, w_ref, rows_scr, y_scr):
    taps, width = w_ref.shape[0], w_ref.shape[2]
    length = x_refs[0].shape[1]
    x = jnp.concatenate([ref[...] for ref in x_refs], axis=0)
    depth = x.shape[0] // len(offsets)
    halo = jnp.concatenate([edge_block(ref, depth) for ref in halo_refs], axis=0)
    rows_scr[0:length, :] = x.T
    rows_scr[length : length + 16, :] = halo.T[0:16]
    starts = [pl.multiple_of((me ^ off) * depth, 16) for off in offsets]
    for first in range(0, taps, 2):
        group = range(first, min(first + 2, taps))
        w = jnp.concatenate(
            [
                jnp.concatenate([w_ref[k, pl.ds(s, depth), :] for s in starts], axis=0)
                for k in group
            ],
            axis=1,
        )
        y = jnp.dot(rows_scr[...], w, preferred_element_type=F32)
        for c in range(w.shape[1] // LANES):
            part = y[:, c * LANES : (c + 1) * LANES]
            at = first * width // LANES + c
            y_scr[at, EDGE : EDGE + length, :] = part[0:length]
            y_scr[at, EDGE - 2 : EDGE, :] = part[length : length + 2]
            y_scr[at, EDGE + length : EDGE + length + 2, :] = part[length + 2 : length + 4]


def tap_sum(y_scr, start, count, phase, taps, c):
    total = None
    for k in range(taps):
        at = k * (y_scr.shape[0] // taps) + c
        part = y_scr[at, pl.ds(EDGE + 2 * start + phase + k - 2, count, stride=2), :]
        total = part if total is None else total + part
    return total


def first_kernel(offsets, idx_ref, *refs):
    n = len(offsets)
    *x_refs, w_ref, even_ref, odd_ref, rows_scr, y_scr = refs
    x_refs, halo_refs = x_refs[:-n], x_refs[-n:]
    conv_rows(offsets, idx_ref[0], x_refs, halo_refs, w_ref, rows_scr, y_scr)
    taps, width = w_ref.shape[0], w_ref.shape[2]
    half = even_ref.shape[0]
    step = min(64, half)
    for start in range(0, half, step):
        rows = slice(start, start + step)
        for c in range(width // LANES):
            lanes = slice(c * LANES, (c + 1) * LANES)
            even_ref[rows, lanes] = tap_sum(y_scr, start, step, 0, taps, c)
            odd_ref[rows, lanes] = tap_sum(y_scr, start, step, 1, taps, c)


def second_kernel(offsets, far, per, idx_ref, *refs):
    n = len(offsets)
    blocks, pays, refs = refs[:n], refs[n : 2 * n], refs[2 * n :]
    w_ref, even_ref, odd_ref, grad_ref, enc_ref, pre_ref, *sent_refs = refs[:-5]
    rows_scr, y_scr, p_scr, x_scr, edge_scr = refs[-5:]
    me = idx_ref[0]
    pick = lambda items: [items[j] for j in far]
    conv_rows(pick(offsets), me, pick(blocks), pick(pays), w_ref, rows_scr, y_scr)
    taps, width = w_ref.shape[0], w_ref.shape[2]
    half = even_ref.shape[0]
    step = min(64, half)
    length = 2 * half
    zero = jnp.zeros((EDGE, width), F32)
    pre_ref[0:EDGE, :] = zero
    pre_ref[EDGE + length : 2 * EDGE + length, :] = zero
    for start in range(0, half, step):
        rows = slice(start, start + step)
        for c in range(width // LANES):
            lanes = slice(c * LANES, (c + 1) * LANES)
            even = even_ref[rows, lanes] + tap_sum(y_scr, start, step, 0, taps, c)
            odd = odd_ref[rows, lanes] + tap_sum(y_scr, start, step, 1, taps, c)
            act_even, slope_even = gelu_parts(even)
            act_odd, slope_odd = gelu_parts(odd)
            enc_ref[rows, lanes] = (0.5 * (act_even + act_odd)).astype(BF16)
            spread = grad_ref[rows, lanes].astype(F32)
            p_scr[c, pl.ds(2 * start, step, stride=2), :] = slope_even * 0.5 * spread
            p_scr[c, pl.ds(2 * start + 1, step, stride=2), :] = slope_odd * 0.5 * spread
    for c in range(width // LANES):
        lanes = slice(c * LANES, (c + 1) * LANES)
        pre_ref[EDGE : EDGE + length, lanes] = p_scr[c].astype(BF16).astype(F32)
    if not sent_refs:
        return
    wanted = (1 - idx_ref[1]) * per
    depth = blocks[0].shape[0]
    for off, block, pay in zip(offsets, blocks, pays):

        @pl.when(me ^ off == wanted)
        def _(block=block, pay=pay):
            x_scr[:, 0:length] = block[...]
            x_scr[:, length : length + LANES] = edge_block(pay, depth)

    p, edge = shifted_rows(pre_ref, edge_scr, (0,))
    res = jnp.dot(x_scr[:, 0:length], p, preferred_element_type=F32)
    res = res + jnp.dot(x_scr[:, length : length + LANES], edge, preferred_element_type=F32)
    sent_refs[0][...] = res.astype(BF16)


def shifted_rows(p_ref, edge_scr, group):
    length, width = p_ref.shape[0] - 2 * EDGE, p_ref.shape[1]
    edge_scr[...] = jnp.zeros_like(edge_scr)
    shifted = []
    for i, tap in enumerate(group):
        cols = slice(i * width, (i + 1) * width)
        edge_scr[0:2, cols] = p_ref[EDGE - tap : EDGE - tap + 2, :]
        edge_scr[2:4, cols] = p_ref[EDGE + length + 2 - tap : EDGE + length + 4 - tap, :]
        shifted.append(p_ref[EDGE + 2 - tap : EDGE + 2 - tap + length, :].astype(BF16))
    return jnp.concatenate(shifted, axis=1), edge_scr[:, 0 : len(group) * width].astype(BF16)


def grad_kernel(offsets, group, per, pieces, idx_ref, *refs):
    n = len(offsets)
    blocks, pays, p_ref = refs[:n], refs[n : 2 * n], refs[2 * n]
    out_refs, edge_scr = list(refs[2 * n + 1 : -1]), refs[-1]
    width = p_ref.shape[1]
    me = idx_ref[0]
    x = jnp.concatenate([ref[...] for ref in blocks], axis=0)
    depth = x.shape[0] // n
    halo = jnp.concatenate([edge_block(ref, depth) for ref in pays], axis=0)
    for first in range(0, len(group), 2):
        some = group[first : first + 2]
        p, edge = shifted_rows(p_ref, edge_scr, some)
        res = jnp.dot(x, p, preferred_element_type=F32) + jnp.dot(halo, edge, preferred_element_type=F32)
        res = res.astype(BF16)
        for i in range(len(some)):
            own_ref = out_refs.pop(0)
            named = pieces[first + i]
            other_refs = [out_refs.pop(0) for _ in range(len(named) or min(per, 1))]
            for j, off in enumerate(offsets):
                part = res[j * depth : (j + 1) * depth, i * width : (i + 1) * width]
                at = me ^ off
                if not per:
                    own_ref[pl.ds(pl.multiple_of(at * depth, 16), depth), :] = part
                    continue
                mine = lax.div(at, per) == idx_ref[1]
                other = jnp.logical_not(mine)
                row = lax.rem(at, per)
                hits = [(own_ref, mine)]
                if not named:
                    hits.append((other_refs[0], other))
                for ref, hit in hits:

                    @pl.when(hit)
                    def _(ref=ref, part=part, row=row):
                        ref[pl.ds(pl.multiple_of(row * depth, 16), depth), :] = part

                for r, ref in zip(named, other_refs):

                    @pl.when(jnp.logical_and(other, row == r))
                    def _(ref=ref, part=part):
                        ref[...] = part


def qkv_kernel(offsets, idx_ref, *refs):
    n = len(offsets)
    enc_refs, gain_refs, (w_ref, out_ref) = refs[:n], refs[n : 2 * n], refs[2 * n :]
    depth = enc_refs[0].shape[1]
    values = [ref[...].astype(F32) for ref in enc_refs]
    channels = n * depth
    sums = sum(jnp.sum(v, axis=1, keepdims=True) for v in values)
    squares = sum(jnp.sum(v * v, axis=1, keepdims=True) for v in values)
    mean = sums / channels
    var = squares / channels - mean * mean
    scale = lax.rsqrt(var + 1e-05)
    total = None
    for off, v, gain_ref in zip(offsets, values, gain_refs):
        normal = ((v - mean) * scale * gain_ref[4:5, 0:depth]).astype(BF16)
        w = w_ref[pl.ds(pl.multiple_of((idx_ref[0] ^ off) * depth, 16), depth), :]
        part = jnp.dot(normal, w, preferred_element_type=F32)
        total = part if total is None else total + part
    out_ref[...] = total.astype(BF16)


def call(kernel, out, scratch, mib, idx, *arrays):
    vmem = pl.BlockSpec(memory_space=pltpu.VMEM)
    return pl.pallas_call(
        kernel,
        out_shape=out,
        in_specs=[pl.BlockSpec(memory_space=pltpu.SMEM)] + [vmem] * len(arrays),
        out_specs=jax.tree.map(lambda _: vmem, out),
        scratch_shapes=scratch,
        compiler_params=pltpu.CompilerParams(vmem_limit_bytes=mib * 1024 * 1024),
    )(idx, *arrays)


def after(value, *others):
    return lax.optimization_barrier((value, *others))[0]


def write_kernel(*refs):
    *part_refs, out_ref = refs
    pieces = len(part_refs) // out_ref.shape[0]
    rows = part_refs[0].shape[0]
    for i, ref in enumerate(part_refs):
        tap, r = i // pieces, i % pieces
        out_ref[tap, r * rows : (r + 1) * rows, :] = ref[...].astype(F32)


def written(parts, taps, at, buffer, shape):
    rows, width = parts[0].shape
    extra = [] if buffer is None else [buffer]
    kernel = write_kernel if buffer is None else lambda b, *refs: write_kernel(*refs)
    return pl.pallas_call(
        kernel,
        out_shape=jax.ShapeDtypeStruct(shape, F32),
        grid=(1,),
        in_specs=[pl.BlockSpec(memory_space=pl.ANY)] * len(extra)
        + [pl.BlockSpec((rows, width), lambda i: (0, 0))] * len(parts),
        out_specs=pl.BlockSpec((taps, shape[1], width), lambda i: (at // taps, 0, 0)),
        input_output_aliases={0: 0} if extra else {},
        compiler_params=pltpu.CompilerParams(vmem_limit_bytes=16 * 1024 * 1024),
    )(*extra, *parts)


def edge_kernel(head_ref, tail_ref, out_ref):
    depth = head_ref.shape[0]
    extra = jnp.zeros((out_ref.shape[1] - depth, LANES), F32)
    head = jnp.concatenate([head_ref[...].astype(F32), extra], axis=0).T
    tail = jnp.concatenate([tail_ref[...].astype(F32), extra], axis=0).T
    out_ref[...] = jnp.zeros_like(out_ref)
    out_ref[0:2, :] = head[0:2]
    out_ref[2:4, :] = tail[LANES - 2 : LANES]


def edge_rows(x, width):
    peers = lax.axis_size("seq")
    me = lax.axis_index("seq")
    depth, length = x.shape
    ends = pl.pallas_call(
        edge_kernel,
        out_shape=jax.ShapeDtypeStruct((8, width), F32),
        grid=(1,),
        in_specs=[
            pl.BlockSpec((depth, LANES), lambda i: (0, 0)),
            pl.BlockSpec((depth, LANES), lambda i: (0, length // LANES - 1)),
        ],
        out_specs=pl.BlockSpec((8, width), lambda i: (0, 0)),
        compiler_params=pltpu.CompilerParams(vmem_limit_bytes=2 * 1024 * 1024),
    )(x, x)
    if peers == 2:
        before = behind = swap(ends, "seq", 1)
    else:
        up = [(i, (i + 1) % peers) for i in range(peers - 1)]
        down = [(j, i) for i, j in up]
        before, behind = lax.ppermute(ends, "seq", up), lax.ppermute(ends, "seq", down)
    before = jnp.where(me == 0, 0.0, before[2:4])
    behind = jnp.where(me == peers - 1, 0.0, behind[0:2])
    return jnp.concatenate([before, behind], axis=0)


def added(a, b):
    return (a.astype(F32) + b.astype(F32)).astype(BF16)


def chain_sums(count, part, sent, idle):
    me = lax.axis_index("dp")
    end = jnp.logical_or(me == 0, me == 3)
    outer_pairs = [(0, 1), (1, 0), (2, 3), (3, 2)]
    middle_pairs = [(1, 2), (2, 1)]
    last = None
    h, p, s, outer, middle, sums = {}, {}, {}, {}, {}, {}
    for r in range(count + 5):
        if r < count:
            last = h[r] = part(r, last)
        if r < count + 3:
            value = h.get(r, s.get(r - 3))
            if r in h and r - 3 in s:
                value = jnp.where(end, h[r], s[r - 3])
            last = value = lax.optimization_barrier(value)
            outer[r] = lax.ppermute(value, "dp", outer_pairs)
            last = sent(r, last, sums)
        if r - 1 in outer:
            got = after(outer.pop(r - 1), last)
            if r - 1 < count:
                last = p[r - 1] = lax.optimization_barrier(added(h[r - 1], got))
                middle[r - 1] = lax.ppermute(last, "dp", middle_pairs)
            if r >= 4:
                sums[r - 4] = lax.optimization_barrier(jnp.where(end, got, s[r - 4]))
                if r - 1 >= count:
                    last = sums[r - 4]
            last = idle(r - 1, last, sums)
        if r - 2 in middle:
            got = after(middle.pop(r - 2), last)
            last = s[r - 2] = lax.optimization_barrier(added(p[r - 2], got))
    return [sums[c] for c in range(count)]


def on_device(block_input, conv_weight, norm_gain, qkv_weight, encoder_grad):
    x = jnp.swapaxes(block_input[0], 0, 1)
    depth, length = x.shape
    taps, _, width = conv_weight.shape
    peers, shards = lax.axis_size("mp"), lax.axis_size("seq")
    bits = [1 << b for b in reversed(range(peers.bit_length() - 1))]
    idx = jnp.stack([lax.axis_index("mp"), lax.axis_index("seq")]).astype(jnp.int32)

    offsets = [0]
    for bit in bits:
        offsets = offsets + [o ^ bit for o in offsets]
    near = [j for j, o in enumerate(offsets) if o < 2]
    far = [j for j, o in enumerate(offsets) if o >= 2]
    half = length // 2
    pick = lambda items, at: [items[j] for j in at]
    scratch = lambda at: [
        pltpu.VMEM((length + 16, len(at) * depth), BF16),
        pltpu.VMEM((taps * width // LANES, length + 2 * EDGE, LANES), F32),
    ]

    blocks = [x]
    for bit in bits[:-1]:
        blocks = blocks + [swap(b, "mp", bit) for b in blocks]
    own = swap(x, "mp", bits[-1])
    edges = edge_rows(x, width)
    payload = jnp.concatenate([edges, norm_gain.reshape(1, -1), jnp.zeros((3, width), F32)], axis=0)
    payloads = [payload] + [swap(payload, "mp", o) for o in offsets[1:]]

    part = jax.ShapeDtypeStruct((half, width), F32)
    even, odd = call(
        functools.partial(first_kernel, pick(offsets, near)),
        (part, part),
        scratch(near),
        24,
        idx, x, own, *pick(payloads, near), conv_weight,
    )
    hold = [even] + pick(payloads, far)
    blocks = blocks + [own] + [swap(after(b, *hold), "mp", bits[-1]) for b in blocks[1:]]
    pair = shards == 2 and peers % shards == 0 and lax.axis_size("dp") == 4
    per = peers // shards if pair else 0
    piece = jax.ShapeDtypeStruct((depth, width), BF16)
    encoded, pre_grad, *first = call(
        functools.partial(second_kernel, offsets, far, per),
        (
            jax.ShapeDtypeStruct((half, width), BF16),
            jax.ShapeDtypeStruct((length + 2 * EDGE, width), F32),
            *([piece] if pair else []),
        ),
        scratch(far)
        + [
            pltpu.VMEM((width // LANES, length, LANES), F32),
            pltpu.VMEM((depth, length + LANES), BF16),
            pltpu.VMEM((LANES, width), F32),
        ],
        26,
        idx, *blocks, *payloads, conv_weight, even, odd, encoder_grad[0],
    )
    encs = [encoded]
    for bit in bits[:-1]:
        encs = encs + [swap(e, "mp", bit) for e in encs]

    everything = tuple(range(per))
    pieces_of = lambda k: (everything[1:], everything)[k] if k < 2 else ()

    def gradient(group, hold):
        pieces = [pieces_of(k) for k in group]
        outs = []
        for q in pieces:
            if not pair:
                outs.append([jax.ShapeDtypeStruct((peers * depth, width), BF16)])
                continue
            whole = jax.ShapeDtypeStruct((per * depth, width), BF16)
            outs.append([whole] + ([piece] * len(q) if q else [whole]))
        flat = call(
            functools.partial(grad_kernel, offsets, group, per, pieces),
            tuple(o for tap in outs for o in tap),
            [pltpu.VMEM((LANES, width * min(len(group), 2)), F32)],
            24 if len(group) > 2 else 16,
            after(idx, *hold) if hold else idx, *blocks, *payloads, pre_grad,
        )
        flat = list(flat)
        taken = [[flat.pop(0) for _ in tap] for tap in outs]
        return [t[0] for t in taken], [t[1:] for t in taken]

    qkv_call = lambda idx, encs: call(
        functools.partial(qkv_kernel, offsets),
        jax.ShapeDtypeStruct((half, qkv_weight.shape[1]), BF16),
        [],
        8,
        idx, *encs, *payloads, qkv_weight,
    )
    if not pair:
        sums = [gradient((k,), [])[0][0] for k in range(taps)]
        sums = [lax.psum_scatter(v, "seq", scatter_dimension=0, tiled=True) for v in sums]
        sums = [lax.psum(v, "dp").astype(F32) for v in sums]
        encs = encs + [swap(e, "mp", bits[-1]) for e in encs]
        return (qkv_call(idx, encs)[None], jnp.stack(sums, axis=1))

    chunks = taps * per
    keep, send, got, relays, done = [], [], {}, [], {}

    def work(group, hold):
        if not group:
            return
        mine, other = gradient(group, hold)
        keep.extend(mine)
        send.extend(other if send else [list(first) + other[0]] + other[1:])

    def launch(tap, hold):
        if tap < taps:
            got[tap] = [swap(after(v, *hold) if hold else v, "seq", 1) for v in send[tap]]

    work((0,), [])
    launch(0, [])
    work(tuple(range(1, taps)), [keep[-1]])
    launch(1, [])

    def share(c, last):
        tap, row = c // per, c % per
        rows = slice(row * depth, (row + 1) * depth)
        value = got[tap][row] if len(got[tap]) > 1 else got[tap][0][rows]
        return added(keep[tap][rows], value if last is None else after(value, last))

    def sent(r, last, sums):
        if r % per == per - 1 and r // per + 2 < taps and r < chunks:
            launch(r // per + 2, [last])
        if r == chunks + 2:
            last = done["qkv"] = qkv_call(after(idx, last, *relays), encs + relays)
        return last

    def idle(c, last, sums):
        if c == per:
            held = encs[1:]
            relays.extend([swap(after(e, last, *held), "mp", bits[-1]) for e in encs])
        if c == chunks:
            early = len(sums) // per
            parts = [sums[i] for i in range(early * per)]
            parts[0] = after(parts[0], last)
            last = done["early"] = written(parts, early, 0, None, (taps, per * depth, width))
            done["at"] = early
        return last

    sums = chain_sums(chunks, share, sent, idle)
    shape = (taps, per * depth, width)
    conv_grad, early = done["early"], done["at"]
    for k in range(early, taps):
        conv_grad = written(sums[k * per : (k + 1) * per], 1, k, conv_grad, shape)
    return (done["qkv"][None], jnp.swapaxes(conv_grad, 0, 1))


def solution(mesh):
    return jax.shard_map(
        on_device,
        mesh=mesh,
        in_specs=(
            P("dp", "seq", "mp"),
            P(None, None, "mp"),
            P("mp"),
            P(None, "mp"),
            P("dp", "seq", "mp"),
        ),
        out_specs=(P("dp", "seq", "mp"), P("seq", None, "mp")),
        check_vma=False,
    )
```

```python
import functools

import jax
import jax.numpy as jnp
from jax import lax
from jax.experimental import pallas as pl
from jax.experimental.pallas import tpu as pltpu
from jax.sharding import PartitionSpec as P

EDGE = 8
LANES = 128
F32 = jnp.float32
BF16 = jnp.bfloat16


def gelu_parts(v):
    u = 0.7978845608 * (v + 0.044715 * v * v * v)
    th = jnp.tanh(u)
    value = 0.5 * v * (1.0 + th)
    slope = 0.5 * (1.0 + th) + 0.5 * v * (1.0 - th * th) * 0.7978845608 * (1.0 + 0.134145 * v * v)
    return value, slope


def swap(value, axis, bit):
    peers = lax.axis_size(axis)
    return lax.ppermute(value, axis, [(i, i ^ bit) for i in range(peers)])


def edge_block(ref, depth):
    rows = jnp.concatenate([ref[0:8, :], jnp.zeros((LANES - 8, ref.shape[1]), F32)], axis=0)
    keep = lax.broadcasted_iota(jnp.int32, rows.shape, 0) < 4
    return jnp.where(keep, rows, 0.0).T[0:depth, :].astype(BF16)


def conv_rows(offsets, me, x_refs, halo_refs, w_ref, rows_scr, y_scr):
    taps, width = w_ref.shape[0], w_ref.shape[2]
    length = x_refs[0].shape[1]
    x = jnp.concatenate([ref[...] for ref in x_refs], axis=0)
    depth = x.shape[0] // len(offsets)
    halo = jnp.concatenate([edge_block(ref, depth) for ref in halo_refs], axis=0)
    rows_scr[0:length, :] = x.T
    rows_scr[length : length + 16, :] = halo.T[0:16]
    starts = [pl.multiple_of((me ^ off) * depth, 16) for off in offsets]
    for first in range(0, taps, 2):
        group = range(first, min(first + 2, taps))
        w = jnp.concatenate(
            [
                jnp.concatenate([w_ref[k, pl.ds(s, depth), :] for s in starts], axis=0)
                for k in group
            ],
            axis=1,
        )
        y = jnp.dot(rows_scr[...], w, preferred_element_type=F32)
        for c in range(w.shape[1] // LANES):
            part = y[:, c * LANES : (c + 1) * LANES]
            at = first * width // LANES + c
            y_scr[at, EDGE : EDGE + length, :] = part[0:length]
            y_scr[at, EDGE - 2 : EDGE, :] = part[length : length + 2]
            y_scr[at, EDGE + length : EDGE + length + 2, :] = part[length + 2 : length + 4]


def tap_sum(y_scr, start, count, phase, taps, c):
    total = None
    for k in range(taps):
        at = k * (y_scr.shape[0] // taps) + c
        part = y_scr[at, pl.ds(EDGE + 2 * start + phase + k - 2, count, stride=2), :]
        total = part if total is None else total + part
    return total


def first_kernel(offsets, idx_ref, *refs):
    n = len(offsets)
    *x_refs, w_ref, even_ref, odd_ref, rows_scr, y_scr = refs
    x_refs, halo_refs = x_refs[:-n], x_refs[-n:]
    conv_rows(offsets, idx_ref[0], x_refs, halo_refs, w_ref, rows_scr, y_scr)
    taps, width = w_ref.shape[0], w_ref.shape[2]
    half = even_ref.shape[0]
    step = min(64, half)
    for start in range(0, half, step):
        rows = slice(start, start + step)
        for c in range(width // LANES):
            lanes = slice(c * LANES, (c + 1) * LANES)
            even_ref[rows, lanes] = tap_sum(y_scr, start, step, 0, taps, c)
            odd_ref[rows, lanes] = tap_sum(y_scr, start, step, 1, taps, c)


def second_kernel(offsets, far, per, idx_ref, *refs):
    n = len(offsets)
    blocks, pays, refs = refs[:n], refs[n : 2 * n], refs[2 * n :]
    w_ref, even_ref, odd_ref, grad_ref, enc_ref, pre_ref, *sent_refs = refs[:-5]
    rows_scr, y_scr, p_scr, x_scr, edge_scr = refs[-5:]
    me = idx_ref[0]
    pick = lambda items: [items[j] for j in far]
    conv_rows(pick(offsets), me, pick(blocks), pick(pays), w_ref, rows_scr, y_scr)
    taps, width = w_ref.shape[0], w_ref.shape[2]
    half = even_ref.shape[0]
    step = min(64, half)
    length = 2 * half
    zero = jnp.zeros((EDGE, width), F32)
    pre_ref[0:EDGE, :] = zero
    pre_ref[EDGE + length : 2 * EDGE + length, :] = zero
    for start in range(0, half, step):
        rows = slice(start, start + step)
        for c in range(width // LANES):
            lanes = slice(c * LANES, (c + 1) * LANES)
            even = even_ref[rows, lanes] + tap_sum(y_scr, start, step, 0, taps, c)
            odd = odd_ref[rows, lanes] + tap_sum(y_scr, start, step, 1, taps, c)
            act_even, slope_even = gelu_parts(even)
            act_odd, slope_odd = gelu_parts(odd)
            enc_ref[rows, lanes] = (0.5 * (act_even + act_odd)).astype(BF16)
            spread = grad_ref[rows, lanes].astype(F32)
            p_scr[c, pl.ds(2 * start, step, stride=2), :] = slope_even * 0.5 * spread
            p_scr[c, pl.ds(2 * start + 1, step, stride=2), :] = slope_odd * 0.5 * spread
    for c in range(width // LANES):
        lanes = slice(c * LANES, (c + 1) * LANES)
        pre_ref[EDGE : EDGE + length, lanes] = p_scr[c].astype(BF16).astype(F32)
    if not sent_refs:
        return
    wanted = (1 - idx_ref[1]) * per
    depth = blocks[0].shape[0]
    for off, block, pay in zip(offsets, blocks, pays):

        @pl.when(me ^ off == wanted)
        def _(block=block, pay=pay):
            x_scr[:, 0:length] = block[...]
            x_scr[:, length : length + LANES] = edge_block(pay, depth)

    p, edge = shifted_rows(pre_ref, edge_scr, (0,))
    res = jnp.dot(x_scr[:, 0:length], p, preferred_element_type=F32)
    res = res + jnp.dot(x_scr[:, length : length + LANES], edge, preferred_element_type=F32)
    sent_refs[0][...] = res.astype(BF16)


def shifted_rows(p_ref, edge_scr, group):
    length, width = p_ref.shape[0] - 2 * EDGE, p_ref.shape[1]
    edge_scr[...] = jnp.zeros_like(edge_scr)
    shifted = []
    for i, tap in enumerate(group):
        cols = slice(i * width, (i + 1) * width)
        edge_scr[0:2, cols] = p_ref[EDGE - tap : EDGE - tap + 2, :]
        edge_scr[2:4, cols] = p_ref[EDGE + length + 2 - tap : EDGE + length + 4 - tap, :]
        shifted.append(p_ref[EDGE + 2 - tap : EDGE + 2 - tap + length, :].astype(BF16))
    return jnp.concatenate(shifted, axis=1), edge_scr[:, 0 : len(group) * width].astype(BF16)


def grad_kernel(offsets, group, per, pieces, idx_ref, *refs):
    n = len(offsets)
    blocks, pays, p_ref = refs[:n], refs[n : 2 * n], refs[2 * n]
    out_refs, edge_scr = list(refs[2 * n + 1 : -1]), refs[-1]
    width = p_ref.shape[1]
    me = idx_ref[0]
    x = jnp.concatenate([ref[...] for ref in blocks], axis=0)
    depth = x.shape[0] // n
    halo = jnp.concatenate([edge_block(ref, depth) for ref in pays], axis=0)
    for first in range(0, len(group), 2):
        some = group[first : first + 2]
        p, edge = shifted_rows(p_ref, edge_scr, some)
        res = jnp.dot(x, p, preferred_element_type=F32) + jnp.dot(halo, edge, preferred_element_type=F32)
        res = res.astype(BF16)
        for i in range(len(some)):
            own_ref = out_refs.pop(0)
            named = pieces[first + i]
            other_refs = [out_refs.pop(0) for _ in range(len(named) or min(per, 1))]
            for j, off in enumerate(offsets):
                part = res[j * depth : (j + 1) * depth, i * width : (i + 1) * width]
                at = me ^ off
                if not per:
                    own_ref[pl.ds(pl.multiple_of(at * depth, 16), depth), :] = part
                    continue
                mine = lax.div(at, per) == idx_ref[1]
                other = jnp.logical_not(mine)
                row = lax.rem(at, per)
                hits = [(own_ref, mine)]
                if not named:
                    hits.append((other_refs[0], other))
                for ref, hit in hits:

                    @pl.when(hit)
                    def _(ref=ref, part=part, row=row):
                        ref[pl.ds(pl.multiple_of(row * depth, 16), depth), :] = part

                for r, ref in zip(named, other_refs):

                    @pl.when(jnp.logical_and(other, row == r))
                    def _(ref=ref, part=part):
                        ref[...] = part


def qkv_kernel(offsets, idx_ref, *refs):
    n = len(offsets)
    enc_refs, gain_refs, (w_ref, out_ref) = refs[:n], refs[n : 2 * n], refs[2 * n :]
    depth = enc_refs[0].shape[1]
    values = [ref[...].astype(F32) for ref in enc_refs]
    channels = n * depth
    sums = sum(jnp.sum(v, axis=1, keepdims=True) for v in values)
    squares = sum(jnp.sum(v * v, axis=1, keepdims=True) for v in values)
    mean = sums / channels
    var = squares / channels - mean * mean
    scale = lax.rsqrt(var + 1e-05)
    total = None
    for off, v, gain_ref in zip(offsets, values, gain_refs):
        normal = ((v - mean) * scale * gain_ref[4:5, 0:depth]).astype(BF16)
        w = w_ref[pl.ds(pl.multiple_of((idx_ref[0] ^ off) * depth, 16), depth), :]
        part = jnp.dot(normal, w, preferred_element_type=F32)
        total = part if total is None else total + part
    out_ref[...] = total.astype(BF16)


def call(kernel, out, scratch, mib, idx, *arrays):
    vmem = pl.BlockSpec(memory_space=pltpu.VMEM)
    return pl.pallas_call(
        kernel,
        out_shape=out,
        in_specs=[pl.BlockSpec(memory_space=pltpu.SMEM)] + [vmem] * len(arrays),
        out_specs=jax.tree.map(lambda _: vmem, out),
        scratch_shapes=scratch,
        compiler_params=pltpu.CompilerParams(vmem_limit_bytes=mib * 1024 * 1024),
    )(idx, *arrays)


def after(value, *others):
    return lax.optimization_barrier((value, *others))[0]


def write_kernel(end_ref, *refs):
    *part_refs, out_ref = refs
    count = len(part_refs) // 2
    pieces = count // out_ref.shape[0]
    rows = part_refs[0].shape[0]
    for i in range(count):
        tap, r = i // pieces, i % pieces
        for ref, here in ((part_refs[2 * i], end_ref[0] > 0), (part_refs[2 * i + 1], end_ref[0] == 0)):

            @pl.when(here)
            def _(ref=ref, tap=tap, r=r):
                out_ref[tap, r * rows : (r + 1) * rows, :] = ref[...].astype(F32)


def written(parts, taps, at, buffer, shape):
    me = lax.axis_index("dp")
    end = jnp.logical_or(me == 0, me == lax.axis_size("dp") - 1).astype(jnp.int32).reshape(1)
    parts = [v for pair in parts for v in pair]
    rows, width = parts[0].shape
    extra = [] if buffer is None else [buffer]
    kernel = write_kernel if buffer is None else lambda end, b, *refs: write_kernel(end, *refs)
    return pl.pallas_call(
        kernel,
        out_shape=jax.ShapeDtypeStruct(shape, F32),
        grid=(1,),
        in_specs=[pl.BlockSpec(memory_space=pltpu.SMEM)]
        + [pl.BlockSpec(memory_space=pl.ANY)] * len(extra)
        + [pl.BlockSpec((rows, width), lambda i: (0, 0))] * len(parts),
        out_specs=pl.BlockSpec((taps, shape[1], width), lambda i: (at // taps, 0, 0)),
        input_output_aliases={1: 0} if extra else {},
        compiler_params=pltpu.CompilerParams(vmem_limit_bytes=16 * 1024 * 1024),
    )(end, *extra, *parts)


def edge_kernel(head_ref, tail_ref, out_ref):
    depth = head_ref.shape[0]
    extra = jnp.zeros((out_ref.shape[1] - depth, LANES), F32)
    head = jnp.concatenate([head_ref[...].astype(F32), extra], axis=0).T
    tail = jnp.concatenate([tail_ref[...].astype(F32), extra], axis=0).T
    out_ref[...] = jnp.zeros_like(out_ref)
    out_ref[0:2, :] = head[0:2]
    out_ref[2:4, :] = tail[LANES - 2 : LANES]


def edge_rows(x, width):
    peers = lax.axis_size("seq")
    me = lax.axis_index("seq")
    depth, length = x.shape
    ends = pl.pallas_call(
        edge_kernel,
        out_shape=jax.ShapeDtypeStruct((8, width), F32),
        grid=(1,),
        in_specs=[
            pl.BlockSpec((depth, LANES), lambda i: (0, 0)),
            pl.BlockSpec((depth, LANES), lambda i: (0, length // LANES - 1)),
        ],
        out_specs=pl.BlockSpec((8, width), lambda i: (0, 0)),
        compiler_params=pltpu.CompilerParams(vmem_limit_bytes=2 * 1024 * 1024),
    )(x, x)
    if peers == 2:
        before = behind = swap(ends, "seq", 1)
    else:
        up = [(i, (i + 1) % peers) for i in range(peers - 1)]
        down = [(j, i) for i, j in up]
        before, behind = lax.ppermute(ends, "seq", up), lax.ppermute(ends, "seq", down)
    before = jnp.where(me == 0, 0.0, before[2:4])
    behind = jnp.where(me == peers - 1, 0.0, behind[0:2])
    return jnp.concatenate([before, behind], axis=0)


def added(a, b):
    return (a.astype(F32) + b.astype(F32)).astype(BF16)


def chain_sums(count, part, sent, idle):
    me = lax.axis_index("dp")
    end = jnp.logical_or(me == 0, me == 3)
    outer_pairs = [(0, 1), (1, 0), (2, 3), (3, 2)]
    middle_pairs = [(1, 2), (2, 1)]
    last = None
    h, p, s, outer, middle, sums = {}, {}, {}, {}, {}, {}
    for r in range(count + 5):
        if r < count:
            h[r] = part(r, last)
        if r < count + 3:
            value = h.get(r, s.get(r - 3))
            if r in h and r - 3 in s:
                value = jnp.where(end, h[r], s[r - 3])
            last = value = lax.optimization_barrier(value)
            outer[r] = lax.ppermute(value, "dp", outer_pairs)
            last = sent(r, last, sums)
        if r - 1 in outer:
            got = after(outer.pop(r - 1), last)
            if r - 1 < count:
                last = p[r - 1] = lax.optimization_barrier(added(h[r - 1], got))
                middle[r - 1] = lax.ppermute(last, "dp", middle_pairs)
            if r >= 4:
                sums[r - 4] = (got, s[r - 4])
                if r - 1 >= count:
                    last = got
            last = idle(r - 1, last, sums)
        if r - 2 in middle:
            got = after(middle.pop(r - 2), last)
            last = s[r - 2] = lax.optimization_barrier(added(p[r - 2], got))
    return [sums[c] for c in range(count)]


def on_device(block_input, conv_weight, norm_gain, qkv_weight, encoder_grad):
    x = jnp.swapaxes(block_input[0], 0, 1)
    depth, length = x.shape
    taps, _, width = conv_weight.shape
    peers, shards = lax.axis_size("mp"), lax.axis_size("seq")
    bits = [1 << b for b in reversed(range(peers.bit_length() - 1))]
    idx = jnp.stack([lax.axis_index("mp"), lax.axis_index("seq")]).astype(jnp.int32)

    offsets = [0]
    for bit in bits:
        offsets = offsets + [o ^ bit for o in offsets]
    near = [j for j, o in enumerate(offsets) if o < 2]
    far = [j for j, o in enumerate(offsets) if o >= 2]
    half = length // 2
    pick = lambda items, at: [items[j] for j in at]
    scratch = lambda at: [
        pltpu.VMEM((length + 16, len(at) * depth), BF16),
        pltpu.VMEM((taps * width // LANES, length + 2 * EDGE, LANES), F32),
    ]

    blocks = [x]
    for bit in bits[:-1]:
        blocks = blocks + [swap(b, "mp", bit) for b in blocks]
    own = swap(x, "mp", bits[-1])
    edges = edge_rows(x, width)
    payload = jnp.concatenate([edges, norm_gain.reshape(1, -1), jnp.zeros((3, width), F32)], axis=0)
    payloads = [payload] + [swap(payload, "mp", o) for o in offsets[1:]]

    part = jax.ShapeDtypeStruct((half, width), F32)
    even, odd = call(
        functools.partial(first_kernel, pick(offsets, near)),
        (part, part),
        scratch(near),
        24,
        idx, x, own, *pick(payloads, near), conv_weight,
    )
    hold = [even] + pick(payloads, far)
    blocks = blocks + [own] + [swap(after(b, *hold), "mp", bits[-1]) for b in blocks[1:]]
    pair = shards == 2 and peers % shards == 0 and lax.axis_size("dp") == 4
    per = peers // shards if pair else 0
    piece = jax.ShapeDtypeStruct((depth, width), BF16)
    encoded, pre_grad, *first = call(
        functools.partial(second_kernel, offsets, far, per),
        (
            jax.ShapeDtypeStruct((half, width), BF16),
            jax.ShapeDtypeStruct((length + 2 * EDGE, width), F32),
            *([piece] if pair else []),
        ),
        scratch(far)
        + [
            pltpu.VMEM((width // LANES, length, LANES), F32),
            pltpu.VMEM((depth, length + LANES), BF16),
            pltpu.VMEM((LANES, width), F32),
        ],
        26,
        idx, *blocks, *payloads, conv_weight, even, odd, encoder_grad[0],
    )
    encs = [encoded]
    for bit in bits[:-1]:
        encs = encs + [swap(e, "mp", bit) for e in encs]

    everything = tuple(range(per))
    pieces_of = lambda k: everything[1:] if k == 0 else (everything if k in (1, taps - 1) else ())

    def gradient(group, hold):
        pieces = [pieces_of(k) for k in group]
        outs = []
        for q in pieces:
            if not pair:
                outs.append([jax.ShapeDtypeStruct((peers * depth, width), BF16)])
                continue
            whole = jax.ShapeDtypeStruct((per * depth, width), BF16)
            outs.append([whole] + ([piece] * len(q) if q else [whole]))
        flat = call(
            functools.partial(grad_kernel, offsets, group, per, pieces),
            tuple(o for tap in outs for o in tap),
            [pltpu.VMEM((LANES, width * min(len(group), 2)), F32)],
            24 if len(group) > 2 else 16,
            after(idx, *hold) if hold else idx, *blocks, *payloads, pre_grad,
        )
        flat = list(flat)
        taken = [[flat.pop(0) for _ in tap] for tap in outs]
        return [t[0] for t in taken], [t[1:] for t in taken]

    qkv_call = lambda idx, encs: call(
        functools.partial(qkv_kernel, offsets),
        jax.ShapeDtypeStruct((half, qkv_weight.shape[1]), BF16),
        [],
        8,
        idx, *encs, *payloads, qkv_weight,
    )
    if not pair:
        sums = [gradient((k,), [])[0][0] for k in range(taps)]
        sums = [lax.psum_scatter(v, "seq", scatter_dimension=0, tiled=True) for v in sums]
        sums = [lax.psum(v, "dp").astype(F32) for v in sums]
        encs = encs + [swap(e, "mp", bits[-1]) for e in encs]
        return (qkv_call(idx, encs)[None], jnp.stack(sums, axis=1))

    chunks = taps * per
    keep, send, got, relays, done = [], [], {}, [], {}

    def work(group, hold):
        if not group:
            return
        mine, other = gradient(group, hold)
        keep.extend(mine)
        send.extend(other if send else [list(first) + other[0]] + other[1:])

    def launch(tap, hold):
        if tap < taps:
            got[tap] = [swap(after(v, *hold) if hold else v, "seq", 1) for v in send[tap]]

    work((0,), [])
    launch(0, [])
    work(tuple(range(1, min(3, taps))), [keep[-1]])
    launch(1, [])

    def share(c, last):
        tap, row = c // per, c % per
        rows = slice(row * depth, (row + 1) * depth)
        value = got[tap][row] if len(got[tap]) > 1 else got[tap][0][rows]
        return added(keep[tap][rows], value if last is None else after(value, last))

    def sent(r, last, sums):
        if r == per - 1:
            work(tuple(range(3, taps)), [last] + encs[1:])
            last = keep[-1]
        if r % per == per - 1 and r // per + 2 < taps and r < chunks:
            launch(r // per + 2, [last])
        if r == chunks + 2:
            last = done["qkv"] = qkv_call(after(idx, last, *relays), encs + relays)
        return last

    def idle(c, last, sums):
        if c == per:
            held = encs[1:]
            relays.extend([swap(after(e, last, *held), "mp", bits[-1]) for e in encs])
        if c == chunks:
            early = len(sums) // per
            parts = [sums[i] for i in range(early * per)]
            parts[0] = (after(parts[0][0], last), parts[0][1])
            last = done["early"] = written(parts, early, 0, None, (taps, per * depth, width))
            done["at"] = early
        return last

    sums = chain_sums(chunks, share, sent, idle)
    shape = (taps, per * depth, width)
    conv_grad, early = done["early"], done["at"]
    for k in range(early, taps):
        conv_grad = written(sums[k * per : (k + 1) * per], 1, k, conv_grad, shape)
    return (done["qkv"][None], jnp.swapaxes(conv_grad, 0, 1))


def solution(mesh):
    return jax.shard_map(
        on_device,
        mesh=mesh,
        in_specs=(
            P("dp", "seq", "mp"),
            P(None, None, "mp"),
            P("mp"),
            P(None, "mp"),
            P("dp", "seq", "mp"),
        ),
        out_specs=(P("dp", "seq", "mp"), P("seq", None, "mp")),
        check_vma=False,
    )
```

```python
import functools

import jax
import jax.numpy as jnp
from jax import lax
from jax.experimental import pallas as pl
from jax.experimental.pallas import tpu as pltpu
from jax.sharding import PartitionSpec as P

EDGE = 8
LANES = 128
F32 = jnp.float32
BF16 = jnp.bfloat16


def gelu_parts(v):
    u = 0.7978845608 * (v + 0.044715 * v * v * v)
    th = jnp.tanh(u)
    value = 0.5 * v * (1.0 + th)
    slope = 0.5 * (1.0 + th) + 0.5 * v * (1.0 - th * th) * 0.7978845608 * (1.0 + 0.134145 * v * v)
    return value, slope


def swap(value, axis, bit):
    peers = lax.axis_size(axis)
    return lax.ppermute(value, axis, [(i, i ^ bit) for i in range(peers)])


def edge_block(ref, depth):
    rows = jnp.concatenate([ref[0:8, :], jnp.zeros((LANES - 8, ref.shape[1]), F32)], axis=0)
    keep = lax.broadcasted_iota(jnp.int32, rows.shape, 0) < 4
    return jnp.where(keep, rows, 0.0).T[0:depth, :].astype(BF16)


def conv_rows(offsets, me, x_refs, halo_refs, w_ref, rows_scr, y_scr):
    taps, width = w_ref.shape[0], w_ref.shape[2]
    length = x_refs[0].shape[1]
    x = jnp.concatenate([ref[...] for ref in x_refs], axis=0)
    depth = x.shape[0] // len(offsets)
    halo = jnp.concatenate([edge_block(ref, depth) for ref in halo_refs], axis=0)
    rows_scr[0:length, :] = x.T
    rows_scr[length : length + 16, :] = halo.T[0:16]
    starts = [pl.multiple_of((me ^ off) * depth, 16) for off in offsets]
    for first in range(0, taps, 2):
        group = range(first, min(first + 2, taps))
        w = jnp.concatenate(
            [
                jnp.concatenate([w_ref[k, pl.ds(s, depth), :] for s in starts], axis=0)
                for k in group
            ],
            axis=1,
        )
        y = jnp.dot(rows_scr[...], w, preferred_element_type=F32)
        for c in range(w.shape[1] // LANES):
            part = y[:, c * LANES : (c + 1) * LANES]
            at = first * width // LANES + c
            y_scr[at, EDGE : EDGE + length, :] = part[0:length]
            y_scr[at, EDGE - 2 : EDGE, :] = part[length : length + 2]
            y_scr[at, EDGE + length : EDGE + length + 2, :] = part[length + 2 : length + 4]


def tap_sum(y_scr, start, count, phase, taps, c):
    total = None
    for k in range(taps):
        at = k * (y_scr.shape[0] // taps) + c
        part = y_scr[at, pl.ds(EDGE + 2 * start + phase + k - 2, count, stride=2), :]
        total = part if total is None else total + part
    return total


def first_kernel(offsets, idx_ref, *refs):
    n = len(offsets)
    *x_refs, w_ref, even_ref, odd_ref, rows_scr, y_scr = refs
    x_refs, halo_refs = x_refs[:-n], x_refs[-n:]
    conv_rows(offsets, idx_ref[0], x_refs, halo_refs, w_ref, rows_scr, y_scr)
    taps, width = w_ref.shape[0], w_ref.shape[2]
    half = even_ref.shape[0]
    step = min(64, half)
    for start in range(0, half, step):
        rows = slice(start, start + step)
        for c in range(width // LANES):
            lanes = slice(c * LANES, (c + 1) * LANES)
            even_ref[rows, lanes] = tap_sum(y_scr, start, step, 0, taps, c)
            odd_ref[rows, lanes] = tap_sum(y_scr, start, step, 1, taps, c)


def second_kernel(offsets, far, per, idx_ref, *refs):
    n = len(offsets)
    blocks, pays, refs = refs[:n], refs[n : 2 * n], refs[2 * n :]
    w_ref, even_ref, odd_ref, grad_ref, enc_ref, pre_ref, all_ref, *sent_refs = refs[:-4]
    rows_scr, y_scr, p_scr, edge_scr = refs[-4:]
    me = idx_ref[0]
    pick = lambda items: [items[j] for j in far]
    conv_rows(pick(offsets), me, pick(blocks), pick(pays), w_ref, rows_scr, y_scr)
    taps, width = w_ref.shape[0], w_ref.shape[2]
    half = even_ref.shape[0]
    step = min(64, half)
    length = 2 * half
    zero = jnp.zeros((EDGE, width), F32)
    pre_ref[0:EDGE, :] = zero
    pre_ref[EDGE + length : 2 * EDGE + length, :] = zero
    for start in range(0, half, step):
        rows = slice(start, start + step)
        for c in range(width // LANES):
            lanes = slice(c * LANES, (c + 1) * LANES)
            even = even_ref[rows, lanes] + tap_sum(y_scr, start, step, 0, taps, c)
            odd = odd_ref[rows, lanes] + tap_sum(y_scr, start, step, 1, taps, c)
            act_even, slope_even = gelu_parts(even)
            act_odd, slope_odd = gelu_parts(odd)
            enc_ref[rows, lanes] = (0.5 * (act_even + act_odd)).astype(BF16)
            spread = grad_ref[rows, lanes].astype(F32)
            p_scr[c, pl.ds(2 * start, step, stride=2), :] = slope_even * 0.5 * spread
            p_scr[c, pl.ds(2 * start + 1, step, stride=2), :] = slope_odd * 0.5 * spread
    for c in range(width // LANES):
        lanes = slice(c * LANES, (c + 1) * LANES)
        pre_ref[EDGE : EDGE + length, lanes] = p_scr[c].astype(BF16).astype(F32)
    depth = blocks[0].shape[0]
    for off, block, pay in zip(offsets, blocks, pays):
        rows = pl.ds(pl.multiple_of((me ^ off) * depth, 16), depth)
        all_ref[rows, 0:length] = block[...]
        all_ref[rows, length : length + LANES] = edge_block(pay, depth)
    if sent_refs:
        wanted = pl.ds(pl.multiple_of((1 - idx_ref[1]) * per * depth, 16), depth)
        rows = shifted_rows(pre_ref, edge_scr, (0,))
        sent_refs[0][...] = jnp.dot(all_ref[wanted, :], rows, preferred_element_type=F32).astype(BF16)


def shifted_rows(p_ref, edge_scr, group):
    length, width = p_ref.shape[0] - 2 * EDGE, p_ref.shape[1]
    edge_scr[...] = jnp.zeros_like(edge_scr)
    shifted = []
    for i, tap in enumerate(group):
        cols = slice(i * width, (i + 1) * width)
        edge_scr[0:2, cols] = p_ref[EDGE - tap : EDGE - tap + 2, :]
        edge_scr[2:4, cols] = p_ref[EDGE + length + 2 - tap : EDGE + length + 4 - tap, :]
        shifted.append(p_ref[EDGE + 2 - tap : EDGE + 2 - tap + length, :].astype(BF16))
    edge = edge_scr[:, 0 : len(group) * width].astype(BF16)
    return jnp.concatenate([jnp.concatenate(shifted, axis=1), edge], axis=0)


def grad_kernel(group, depth, per, pieces, idx_ref, all_ref, p_ref, *refs):
    out_refs, edge_scr = list(refs[:-1]), refs[-1]
    width = p_ref.shape[1]
    half = per * depth
    for first in range(0, len(group), 2):
        some = group[first : first + 2]
        rows = shifted_rows(p_ref, edge_scr, some)
        res = jnp.dot(all_ref[...], rows, preferred_element_type=F32).astype(BF16)
        for i in range(len(some)):
            part = res[:, i * width : (i + 1) * width]
            own_ref = out_refs.pop(0)
            if not per:
                own_ref[...] = part
                continue
            lower = idx_ref[1] == 0
            own_ref[...] = jnp.where(lower, part[0:half], part[half : 2 * half])
            other = jnp.where(lower, part[half : 2 * half], part[0:half])
            named = pieces[first + i]
            if not named:
                out_refs.pop(0)[...] = other
            for r in named:
                out_refs.pop(0)[...] = other[r * depth : (r + 1) * depth]


def qkv_kernel(offsets, idx_ref, *refs):
    n = len(offsets)
    enc_refs, gain_refs, (w_ref, out_ref) = refs[:n], refs[n : 2 * n], refs[2 * n :]
    depth = enc_refs[0].shape[1]
    values = [ref[...].astype(F32) for ref in enc_refs]
    channels = n * depth
    sums = sum(jnp.sum(v, axis=1, keepdims=True) for v in values)
    squares = sum(jnp.sum(v * v, axis=1, keepdims=True) for v in values)
    mean = sums / channels
    var = squares / channels - mean * mean
    scale = lax.rsqrt(var + 1e-05)
    total = None
    for off, v, gain_ref in zip(offsets, values, gain_refs):
        normal = ((v - mean) * scale * gain_ref[4:5, 0:depth]).astype(BF16)
        w = w_ref[pl.ds(pl.multiple_of((idx_ref[0] ^ off) * depth, 16), depth), :]
        part = jnp.dot(normal, w, preferred_element_type=F32)
        total = part if total is None else total + part
    out_ref[...] = total.astype(BF16)


def call(kernel, out, scratch, mib, idx, *arrays):
    vmem = pl.BlockSpec(memory_space=pltpu.VMEM)
    return pl.pallas_call(
        kernel,
        out_shape=out,
        in_specs=[pl.BlockSpec(memory_space=pltpu.SMEM)] + [vmem] * len(arrays),
        out_specs=jax.tree.map(lambda _: vmem, out),
        scratch_shapes=scratch,
        compiler_params=pltpu.CompilerParams(vmem_limit_bytes=mib * 1024 * 1024),
    )(idx, *arrays)


def after(value, *others):
    return lax.optimization_barrier((value, *others))[0]


def write_kernel(end_ref, *refs):
    *part_refs, out_ref = refs
    count = len(part_refs) // 2
    pieces = count // out_ref.shape[0]
    rows = part_refs[0].shape[0]
    for i in range(count):
        tap, r = i // pieces, i % pieces
        for ref, here in ((part_refs[2 * i], end_ref[0] > 0), (part_refs[2 * i + 1], end_ref[0] == 0)):

            @pl.when(here)
            def _(ref=ref, tap=tap, r=r):
                out_ref[tap, r * rows : (r + 1) * rows, :] = ref[...].astype(F32)


def written(parts, taps, at, buffer, shape):
    me = lax.axis_index("dp")
    end = jnp.logical_or(me == 0, me == lax.axis_size("dp") - 1).astype(jnp.int32).reshape(1)
    parts = [v for pair in parts for v in pair]
    rows, width = parts[0].shape
    extra = [] if buffer is None else [buffer]
    kernel = write_kernel if buffer is None else lambda end, b, *refs: write_kernel(end, *refs)
    return pl.pallas_call(
        kernel,
        out_shape=jax.ShapeDtypeStruct(shape, F32),
        grid=(1,),
        in_specs=[pl.BlockSpec(memory_space=pltpu.SMEM)]
        + [pl.BlockSpec(memory_space=pl.ANY)] * len(extra)
        + [pl.BlockSpec((rows, width), lambda i: (0, 0))] * len(parts),
        out_specs=pl.BlockSpec((taps, shape[1], width), lambda i: (at // taps, 0, 0)),
        input_output_aliases={1: 0} if extra else {},
        compiler_params=pltpu.CompilerParams(vmem_limit_bytes=16 * 1024 * 1024),
    )(end, *extra, *parts)


def edge_kernel(head_ref, tail_ref, out_ref):
    depth = head_ref.shape[0]
    extra = jnp.zeros((out_ref.shape[1] - depth, LANES), F32)
    head = jnp.concatenate([head_ref[...].astype(F32), extra], axis=0).T
    tail = jnp.concatenate([tail_ref[...].astype(F32), extra], axis=0).T
    out_ref[...] = jnp.zeros_like(out_ref)
    out_ref[0:2, :] = head[0:2]
    out_ref[2:4, :] = tail[LANES - 2 : LANES]


def edge_rows(x, width):
    peers = lax.axis_size("seq")
    me = lax.axis_index("seq")
    depth, length = x.shape
    ends = pl.pallas_call(
        edge_kernel,
        out_shape=jax.ShapeDtypeStruct((8, width), F32),
        grid=(1,),
        in_specs=[
            pl.BlockSpec((depth, LANES), lambda i: (0, 0)),
            pl.BlockSpec((depth, LANES), lambda i: (0, length // LANES - 1)),
        ],
        out_specs=pl.BlockSpec((8, width), lambda i: (0, 0)),
        compiler_params=pltpu.CompilerParams(vmem_limit_bytes=2 * 1024 * 1024),
    )(x, x)
    if peers == 2:
        before = behind = swap(ends, "seq", 1)
    else:
        up = [(i, (i + 1) % peers) for i in range(peers - 1)]
        down = [(j, i) for i, j in up]
        before, behind = lax.ppermute(ends, "seq", up), lax.ppermute(ends, "seq", down)
    before = jnp.where(me == 0, 0.0, before[2:4])
    behind = jnp.where(me == peers - 1, 0.0, behind[0:2])
    return jnp.concatenate([before, behind], axis=0)


def added(a, b):
    return (a.astype(F32) + b.astype(F32)).astype(BF16)


def chain_sums(count, part, sent, idle):
    me = lax.axis_index("dp")
    end = jnp.logical_or(me == 0, me == 3)
    outer_pairs = [(0, 1), (1, 0), (2, 3), (3, 2)]
    middle_pairs = [(1, 2), (2, 1)]
    last = None
    h, p, s, outer, middle, sums = {}, {}, {}, {}, {}, {}
    for r in range(count + 5):
        if r < count:
            h[r] = part(r, last)
        if r < count + 3:
            value = h.get(r, s.get(r - 3))
            if r in h and r - 3 in s:
                value = jnp.where(end, h[r], s[r - 3])
            last = value = lax.optimization_barrier(value)
            outer[r] = lax.ppermute(value, "dp", outer_pairs)
            last = sent(r, last, sums)
        if r - 1 in outer:
            got = after(outer.pop(r - 1), last)
            if r - 1 < count:
                last = p[r - 1] = lax.optimization_barrier(added(h[r - 1], got))
                middle[r - 1] = lax.ppermute(last, "dp", middle_pairs)
            if r >= 4:
                sums[r - 4] = (got, s[r - 4])
                if r - 1 >= count:
                    last = got
            last = idle(r - 1, last, sums)
        if r - 2 in middle:
            got = after(middle.pop(r - 2), last)
            last = s[r - 2] = lax.optimization_barrier(added(p[r - 2], got))
    return [sums[c] for c in range(count)]


def on_device(block_input, conv_weight, norm_gain, qkv_weight, encoder_grad):
    x = jnp.swapaxes(block_input[0], 0, 1)
    depth, length = x.shape
    taps, _, width = conv_weight.shape
    peers, shards = lax.axis_size("mp"), lax.axis_size("seq")
    bits = [1 << b for b in reversed(range(peers.bit_length() - 1))]
    idx = jnp.stack([lax.axis_index("mp"), lax.axis_index("seq")]).astype(jnp.int32)

    offsets = [0]
    for bit in bits:
        offsets = offsets + [o ^ bit for o in offsets]
    near = [j for j, o in enumerate(offsets) if o < 2]
    far = [j for j, o in enumerate(offsets) if o >= 2]
    half = length // 2
    pick = lambda items, at: [items[j] for j in at]
    scratch = lambda at: [
        pltpu.VMEM((length + 16, len(at) * depth), BF16),
        pltpu.VMEM((taps * width // LANES, length + 2 * EDGE, LANES), F32),
    ]

    blocks = [x]
    for bit in bits[:-1]:
        blocks = blocks + [swap(b, "mp", bit) for b in blocks]
    own = swap(x, "mp", bits[-1])
    edges = edge_rows(x, width)
    payload = jnp.concatenate([edges, norm_gain.reshape(1, -1), jnp.zeros((3, width), F32)], axis=0)
    payloads = [payload] + [swap(payload, "mp", o) for o in offsets[1:]]

    part = jax.ShapeDtypeStruct((half, width), F32)
    even, odd = call(
        functools.partial(first_kernel, pick(offsets, near)),
        (part, part),
        scratch(near),
        24,
        idx, x, own, *pick(payloads, near), conv_weight,
    )
    hold = [even] + pick(payloads, far)
    blocks = blocks + [own] + [swap(after(b, *hold), "mp", bits[-1]) for b in blocks[1:]]
    pair = shards == 2 and peers % shards == 0 and lax.axis_size("dp") == 4
    per = peers // shards if pair else 0
    piece = jax.ShapeDtypeStruct((depth, width), BF16)
    encoded, pre_grad, joined, *first = call(
        functools.partial(second_kernel, offsets, far, per),
        (
            jax.ShapeDtypeStruct((half, width), BF16),
            jax.ShapeDtypeStruct((length + 2 * EDGE, width), F32),
            jax.ShapeDtypeStruct((peers * depth, length + LANES), BF16),
            *([piece] if pair else []),
        ),
        scratch(far)
        + [
            pltpu.VMEM((width // LANES, length, LANES), F32),
            pltpu.VMEM((LANES, width), F32),
        ],
        26,
        idx, *blocks, *payloads, conv_weight, even, odd, encoder_grad[0],
    )
    encs = [encoded]
    for bit in bits[:-1]:
        encs = encs + [swap(e, "mp", bit) for e in encs]

    everything = tuple(range(per))
    pieces_of = lambda k: everything[1:] if k == 0 else (everything if k == 1 else ())

    def gradient(group, hold):
        pieces = [pieces_of(k) for k in group]
        outs = []
        for q in pieces:
            if not pair:
                outs.append([jax.ShapeDtypeStruct((peers * depth, width), BF16)])
                continue
            whole = jax.ShapeDtypeStruct((per * depth, width), BF16)
            outs.append([whole] + ([piece] * len(q) if q else [whole]))
        flat = call(
            functools.partial(grad_kernel, group, depth, per, pieces),
            tuple(o for tap in outs for o in tap),
            [pltpu.VMEM((LANES, width * min(len(group), 2)), F32)],
            24 if len(group) > 2 else 16,
            after(idx, *hold) if hold else idx, joined, pre_grad,
        )
        flat = list(flat)
        taken = [[flat.pop(0) for _ in tap] for tap in outs]
        return [t[0] for t in taken], [t[1:] for t in taken]

    qkv_call = lambda idx, encs: call(
        functools.partial(qkv_kernel, offsets),
        jax.ShapeDtypeStruct((half, qkv_weight.shape[1]), BF16),
        [],
        8,
        idx, *encs, *payloads, qkv_weight,
    )
    if not pair:
        sums = [gradient((k,), [])[0][0] for k in range(taps)]
        sums = [lax.psum_scatter(v, "seq", scatter_dimension=0, tiled=True) for v in sums]
        sums = [lax.psum(v, "dp").astype(F32) for v in sums]
        encs = encs + [swap(e, "mp", bits[-1]) for e in encs]
        return (qkv_call(idx, encs)[None], jnp.stack(sums, axis=1))

    chunks = taps * per
    keep, send, got, relays, done = [], [], {}, [], {}

    def work(group, hold):
        if not group:
            return
        mine, other = gradient(group, hold)
        keep.extend(mine)
        send.extend(other if send else [list(first) + other[0]] + other[1:])

    def launch(tap, hold):
        if tap < taps:
            got[tap] = [swap(after(v, *hold) if hold else v, "seq", 1) for v in send[tap]]

    work((0,), [])
    launch(0, [])
    work(tuple(range(1, min(3, taps))), [keep[-1]])
    launch(1, [])

    def share(c, last):
        tap, row = c // per, c % per
        rows = slice(row * depth, (row + 1) * depth)
        value = got[tap][row] if len(got[tap]) > 1 else got[tap][0][rows]
        return added(keep[tap][rows], value if last is None else after(value, last))

    starts = {(k - 1) * per - 1 - (k == 3): k for k in range(2, taps)}

    def sent(r, last, sums):
        if r < chunks and r in starts:
            launch(starts[r], [last])
        if r == chunks + 2:
            early = len(sums) // per
            parts = [sums[i] for i in range(early * per)]
            parts[0] = (after(parts[0][0], last), parts[0][1])
            last = done["early"] = written(parts, early, 0, None, (taps, per * depth, width))
            done["at"] = early
        return last

    def idle(c, last, sums):
        if c == per + 4:
            held = encs[1:]
            relays.extend([swap(after(e, last, *held), "mp", bits[-1]) for e in encs])
        if c == 0:
            work(tuple(range(3, taps)), [last] + encs[1:])
            last = keep[-1]
        if c == chunks:
            last = done["qkv"] = qkv_call(after(idx, last, *relays), encs + relays)
        return last

    sums = chain_sums(chunks, share, sent, idle)
    shape = (taps, per * depth, width)
    conv_grad, early = done["early"], done["at"]
    for k in range(early, taps):
        conv_grad = written(sums[k * per : (k + 1) * per], 1, k, conv_grad, shape)
    return (done["qkv"][None], jnp.swapaxes(conv_grad, 0, 1))


def solution(mesh):
    return jax.shard_map(
        on_device,
        mesh=mesh,
        in_specs=(
            P("dp", "seq", "mp"),
            P(None, None, "mp"),
            P("mp"),
            P(None, "mp"),
            P("dp", "seq", "mp"),
        ),
        out_specs=(P("dp", "seq", "mp"), P("seq", None, "mp")),
        check_vma=False,
    )
```

```python
import functools

import jax
import jax.numpy as jnp
from jax import lax
from jax.experimental import pallas as pl
from jax.experimental.pallas import tpu as pltpu
from jax.sharding import PartitionSpec as P

EDGE = 8
LANES = 128
F32 = jnp.float32
BF16 = jnp.bfloat16


def gelu_parts(v):
    u = 0.7978845608 * (v + 0.044715 * v * v * v)
    th = jnp.tanh(u)
    value = 0.5 * v * (1.0 + th)
    slope = 0.5 * (1.0 + th) + 0.5 * v * (1.0 - th * th) * 0.7978845608 * (1.0 + 0.134145 * v * v)
    return value, slope


def swap(value, axis, bit):
    peers = lax.axis_size(axis)
    return lax.ppermute(value, axis, [(i, i ^ bit) for i in range(peers)])


def edge_block(ref, depth):
    rows = jnp.concatenate([ref[0:8, :], jnp.zeros((LANES - 8, ref.shape[1]), F32)], axis=0)
    keep = lax.broadcasted_iota(jnp.int32, rows.shape, 0) < 4
    return jnp.where(keep, rows, 0.0).T[0:depth, :].astype(BF16)


def conv_rows(offsets, me, x_refs, halo_refs, w_ref, rows_scr, y_scr):
    taps, width = w_ref.shape[0], w_ref.shape[2]
    length = x_refs[0].shape[1]
    x = jnp.concatenate([ref[...] for ref in x_refs], axis=0)
    depth = x.shape[0] // len(offsets)
    halo = jnp.concatenate([edge_block(ref, depth) for ref in halo_refs], axis=0)
    rows_scr[0:length, :] = x.T
    rows_scr[length : length + 16, :] = halo.T[0:16]
    starts = [pl.multiple_of((me ^ off) * depth, 16) for off in offsets]
    for first in range(0, taps, 2):
        group = range(first, min(first + 2, taps))
        w = jnp.concatenate(
            [
                jnp.concatenate([w_ref[k, pl.ds(s, depth), :] for s in starts], axis=0)
                for k in group
            ],
            axis=1,
        )
        y = jnp.dot(rows_scr[...], w, preferred_element_type=F32)
        for c in range(w.shape[1] // LANES):
            part = y[:, c * LANES : (c + 1) * LANES]
            at = first * width // LANES + c
            y_scr[at, EDGE : EDGE + length, :] = part[0:length]
            y_scr[at, EDGE - 2 : EDGE, :] = part[length : length + 2]
            y_scr[at, EDGE + length : EDGE + length + 2, :] = part[length + 2 : length + 4]


def tap_sum(y_scr, start, count, phase, taps, c):
    total = None
    for k in range(taps):
        at = k * (y_scr.shape[0] // taps) + c
        part = y_scr[at, pl.ds(EDGE + 2 * start + phase + k - 2, count, stride=2), :]
        total = part if total is None else total + part
    return total


def first_kernel(offsets, idx_ref, *refs):
    n = len(offsets)
    *x_refs, w_ref, even_ref, odd_ref, rows_scr, y_scr = refs
    x_refs, halo_refs = x_refs[:-n], x_refs[-n:]
    conv_rows(offsets, idx_ref[0], x_refs, halo_refs, w_ref, rows_scr, y_scr)
    taps, width = w_ref.shape[0], w_ref.shape[2]
    half = even_ref.shape[0]
    step = min(64, half)
    for start in range(0, half, step):
        rows = slice(start, start + step)
        for c in range(width // LANES):
            lanes = slice(c * LANES, (c + 1) * LANES)
            even_ref[rows, lanes] = tap_sum(y_scr, start, step, 0, taps, c)
            odd_ref[rows, lanes] = tap_sum(y_scr, start, step, 1, taps, c)


def second_kernel(offsets, far, per, idx_ref, *refs):
    n = len(offsets)
    blocks, pays, refs = refs[:n], refs[n : 2 * n], refs[2 * n :]
    w_ref, even_ref, odd_ref, grad_ref, enc_ref, pre_ref, all_ref, *sent_refs = refs[:-4]
    rows_scr, y_scr, p_scr, edge_scr = refs[-4:]
    me = idx_ref[0]
    pick = lambda items: [items[j] for j in far]
    conv_rows(pick(offsets), me, pick(blocks), pick(pays), w_ref, rows_scr, y_scr)
    taps, width = w_ref.shape[0], w_ref.shape[2]
    half = even_ref.shape[0]
    step = min(64, half)
    length = 2 * half
    zero = jnp.zeros((EDGE, width), F32)
    pre_ref[0:EDGE, :] = zero
    pre_ref[EDGE + length : 2 * EDGE + length, :] = zero
    for start in range(0, half, step):
        rows = slice(start, start + step)
        for c in range(width // LANES):
            lanes = slice(c * LANES, (c + 1) * LANES)
            even = even_ref[rows, lanes] + tap_sum(y_scr, start, step, 0, taps, c)
            odd = odd_ref[rows, lanes] + tap_sum(y_scr, start, step, 1, taps, c)
            act_even, slope_even = gelu_parts(even)
            act_odd, slope_odd = gelu_parts(odd)
            enc_ref[rows, lanes] = (0.5 * (act_even + act_odd)).astype(BF16)
            spread = grad_ref[rows, lanes].astype(F32)
            p_scr[c, pl.ds(2 * start, step, stride=2), :] = slope_even * 0.5 * spread
            p_scr[c, pl.ds(2 * start + 1, step, stride=2), :] = slope_odd * 0.5 * spread
    for c in range(width // LANES):
        lanes = slice(c * LANES, (c + 1) * LANES)
        pre_ref[EDGE : EDGE + length, lanes] = p_scr[c].astype(BF16).astype(F32)
    depth = blocks[0].shape[0]
    for off, block, pay in zip(offsets, blocks, pays):
        rows = pl.ds(pl.multiple_of((me ^ off) * depth, 16), depth)
        all_ref[rows, 0:length] = block[...]
        all_ref[rows, length : length + LANES] = edge_block(pay, depth)
    if sent_refs:
        wanted = pl.ds(pl.multiple_of((1 - idx_ref[1]) * per * depth, 16), depth)
        rows = shifted_rows(pre_ref, edge_scr, (0,))
        sent_refs[0][...] = jnp.dot(all_ref[wanted, :], rows, preferred_element_type=F32).astype(BF16)


def shifted_rows(p_ref, edge_scr, group):
    length, width = p_ref.shape[0] - 2 * EDGE, p_ref.shape[1]
    edge_scr[...] = jnp.zeros_like(edge_scr)
    shifted = []
    for i, tap in enumerate(group):
        cols = slice(i * width, (i + 1) * width)
        edge_scr[0:2, cols] = p_ref[EDGE - tap : EDGE - tap + 2, :]
        edge_scr[2:4, cols] = p_ref[EDGE + length + 2 - tap : EDGE + length + 4 - tap, :]
        shifted.append(p_ref[EDGE + 2 - tap : EDGE + 2 - tap + length, :].astype(BF16))
    edge = edge_scr[:, 0 : len(group) * width].astype(BF16)
    return jnp.concatenate([jnp.concatenate(shifted, axis=1), edge], axis=0)


def grad_kernel(group, depth, per, pieces, idx_ref, all_ref, p_ref, *refs):
    out_refs, edge_scr = list(refs[:-1]), refs[-1]
    width = p_ref.shape[1]
    half = per * depth
    for first in range(0, len(group), 2):
        some = group[first : first + 2]
        rows = shifted_rows(p_ref, edge_scr, some)
        res = jnp.dot(all_ref[...], rows, preferred_element_type=F32).astype(BF16)
        for i in range(len(some)):
            part = res[:, i * width : (i + 1) * width]
            own_ref = out_refs.pop(0)
            if not per:
                own_ref[...] = part
                continue
            lower = idx_ref[1] == 0
            own_ref[...] = jnp.where(lower, part[0:half], part[half : 2 * half])
            other = jnp.where(lower, part[half : 2 * half], part[0:half])
            named = pieces[first + i]
            if not named:
                out_refs.pop(0)[...] = other
            for r in named:
                out_refs.pop(0)[...] = other[r * depth : (r + 1) * depth]


def qkv_kernel(offsets, idx_ref, *refs):
    n = len(offsets)
    enc_refs, gain_refs, (w_ref, out_ref) = refs[:n], refs[n : 2 * n], refs[2 * n :]
    depth = enc_refs[0].shape[1]
    values = [ref[...].astype(F32) for ref in enc_refs]
    channels = n * depth
    sums = sum(jnp.sum(v, axis=1, keepdims=True) for v in values)
    squares = sum(jnp.sum(v * v, axis=1, keepdims=True) for v in values)
    mean = sums / channels
    var = squares / channels - mean * mean
    scale = lax.rsqrt(var + 1e-05)
    total = None
    for off, v, gain_ref in zip(offsets, values, gain_refs):
        normal = ((v - mean) * scale * gain_ref[4:5, 0:depth]).astype(BF16)
        w = w_ref[pl.ds(pl.multiple_of((idx_ref[0] ^ off) * depth, 16), depth), :]
        part = jnp.dot(normal, w, preferred_element_type=F32)
        total = part if total is None else total + part
    out_ref[...] = total.astype(BF16)


def call(kernel, out, scratch, mib, idx, *arrays):
    vmem = pl.BlockSpec(memory_space=pltpu.VMEM)
    return pl.pallas_call(
        kernel,
        out_shape=out,
        in_specs=[pl.BlockSpec(memory_space=pltpu.SMEM)] + [vmem] * len(arrays),
        out_specs=jax.tree.map(lambda _: vmem, out),
        scratch_shapes=scratch,
        compiler_params=pltpu.CompilerParams(vmem_limit_bytes=mib * 1024 * 1024),
    )(idx, *arrays)


def after(value, *others):
    return lax.optimization_barrier((value, *others))[0]


def write_kernel(end_ref, *refs):
    *part_refs, out_ref = refs
    count = len(part_refs) // 2
    pieces = count // out_ref.shape[0]
    rows = part_refs[0].shape[0]
    for i in range(count):
        tap, r = i // pieces, i % pieces
        for ref, here in ((part_refs[2 * i], end_ref[0] > 0), (part_refs[2 * i + 1], end_ref[0] == 0)):

            @pl.when(here)
            def _(ref=ref, tap=tap, r=r):
                out_ref[tap, r * rows : (r + 1) * rows, :] = ref[...].astype(F32)


def written(parts, taps, at, buffer, shape):
    me = lax.axis_index("dp")
    end = jnp.logical_or(me == 0, me == lax.axis_size("dp") - 1).astype(jnp.int32).reshape(1)
    parts = [v for pair in parts for v in pair]
    rows, width = parts[0].shape
    extra = [] if buffer is None else [buffer]
    kernel = write_kernel if buffer is None else lambda end, b, *refs: write_kernel(end, *refs)
    return pl.pallas_call(
        kernel,
        out_shape=jax.ShapeDtypeStruct(shape, F32),
        grid=(1,),
        in_specs=[pl.BlockSpec(memory_space=pltpu.SMEM)]
        + [pl.BlockSpec(memory_space=pl.ANY)] * len(extra)
        + [pl.BlockSpec((rows, width), lambda i: (0, 0))] * len(parts),
        out_specs=pl.BlockSpec((taps, shape[1], width), lambda i: (at // taps, 0, 0)),
        input_output_aliases={1: 0} if extra else {},
        compiler_params=pltpu.CompilerParams(vmem_limit_bytes=16 * 1024 * 1024),
    )(end, *extra, *parts)


def edge_kernel(head_ref, tail_ref, out_ref):
    depth = head_ref.shape[0]
    extra = jnp.zeros((out_ref.shape[1] - depth, LANES), F32)
    head = jnp.concatenate([head_ref[...].astype(F32), extra], axis=0).T
    tail = jnp.concatenate([tail_ref[...].astype(F32), extra], axis=0).T
    out_ref[...] = jnp.zeros_like(out_ref)
    out_ref[0:2, :] = head[0:2]
    out_ref[2:4, :] = tail[LANES - 2 : LANES]


def edge_rows(x, width):
    peers = lax.axis_size("seq")
    me = lax.axis_index("seq")
    depth, length = x.shape
    ends = pl.pallas_call(
        edge_kernel,
        out_shape=jax.ShapeDtypeStruct((8, width), F32),
        grid=(1,),
        in_specs=[
            pl.BlockSpec((depth, LANES), lambda i: (0, 0)),
            pl.BlockSpec((depth, LANES), lambda i: (0, length // LANES - 1)),
        ],
        out_specs=pl.BlockSpec((8, width), lambda i: (0, 0)),
        compiler_params=pltpu.CompilerParams(vmem_limit_bytes=2 * 1024 * 1024),
    )(x, x)
    if peers == 2:
        before = behind = swap(ends, "seq", 1)
    else:
        up = [(i, (i + 1) % peers) for i in range(peers - 1)]
        down = [(j, i) for i, j in up]
        before, behind = lax.ppermute(ends, "seq", up), lax.ppermute(ends, "seq", down)
    before = jnp.where(me == 0, 0.0, before[2:4])
    behind = jnp.where(me == peers - 1, 0.0, behind[0:2])
    return jnp.concatenate([before, behind], axis=0)


def added(a, b):
    return (a.astype(F32) + b.astype(F32)).astype(BF16)


def chain_sums(count, part, sent, idle):
    me = lax.axis_index("dp")
    end = jnp.logical_or(me == 0, me == 3)
    outer_pairs = [(0, 1), (1, 0), (2, 3), (3, 2)]
    middle_pairs = [(1, 2), (2, 1)]
    last = None
    h, p, s, outer, middle, sums = {}, {}, {}, {}, {}, {}
    for r in range(count + 5):
        if r < count:
            h[r] = part(r, last)
        if r < count + 3:
            value = h.get(r, s.get(r - 3))
            if r in h and r - 3 in s:
                value = jnp.where(end, h[r], s[r - 3])
            last = value = lax.optimization_barrier(value)
            outer[r] = lax.ppermute(value, "dp", outer_pairs)
            last = sent(r, last, sums)
        if r - 1 in outer:
            got = after(outer.pop(r - 1), last)
            if r - 1 < count:
                last = p[r - 1] = lax.optimization_barrier(added(h[r - 1], got))
                middle[r - 1] = lax.ppermute(last, "dp", middle_pairs)
            if r >= 4:
                sums[r - 4] = (got, s[r - 4])
                if r - 1 >= count:
                    last = got
            last = idle(r - 1, last, sums)
        if r - 2 in middle:
            got = after(middle.pop(r - 2), last)
            last = s[r - 2] = lax.optimization_barrier(added(p[r - 2], got))
    return [sums[c] for c in range(count)]


def on_device(block_input, conv_weight, norm_gain, qkv_weight, encoder_grad):
    x = jnp.swapaxes(block_input[0], 0, 1)
    depth, length = x.shape
    taps, _, width = conv_weight.shape
    peers, shards = lax.axis_size("mp"), lax.axis_size("seq")
    bits = [1 << b for b in reversed(range(peers.bit_length() - 1))]
    idx = jnp.stack([lax.axis_index("mp"), lax.axis_index("seq")]).astype(jnp.int32)

    offsets = [0]
    for bit in bits:
        offsets = offsets + [o ^ bit for o in offsets]
    near = [j for j, o in enumerate(offsets) if o < 2]
    far = [j for j, o in enumerate(offsets) if o >= 2]
    half = length // 2
    pick = lambda items, at: [items[j] for j in at]
    scratch = lambda at: [
        pltpu.VMEM((length + 16, len(at) * depth), BF16),
        pltpu.VMEM((taps * width // LANES, length + 2 * EDGE, LANES), F32),
    ]

    blocks = [x]
    for bit in bits[:-1]:
        blocks = blocks + [swap(b, "mp", bit) for b in blocks]
    own = swap(x, "mp", bits[-1])
    edges = edge_rows(x, width)
    payload = jnp.concatenate([edges, norm_gain.reshape(1, -1), jnp.zeros((3, width), F32)], axis=0)
    payloads = [payload] + [swap(payload, "mp", o) for o in offsets[1:]]

    part = jax.ShapeDtypeStruct((half, width), F32)
    even, odd = call(
        functools.partial(first_kernel, pick(offsets, near)),
        (part, part),
        scratch(near),
        24,
        idx, x, own, *pick(payloads, near), conv_weight,
    )
    hold = [even] + pick(payloads, far)
    blocks = blocks + [own] + [swap(after(b, *hold), "mp", bits[-1]) for b in blocks[1:]]
    pair = shards == 2 and peers % shards == 0 and lax.axis_size("dp") == 4
    per = peers // shards if pair else 0
    piece = jax.ShapeDtypeStruct((depth, width), BF16)
    encoded, pre_grad, joined, *first = call(
        functools.partial(second_kernel, offsets, far, per),
        (
            jax.ShapeDtypeStruct((half, width), BF16),
            jax.ShapeDtypeStruct((length + 2 * EDGE, width), F32),
            jax.ShapeDtypeStruct((peers * depth, length + LANES), BF16),
            *([piece] if pair else []),
        ),
        scratch(far)
        + [
            pltpu.VMEM((width // LANES, length, LANES), F32),
            pltpu.VMEM((LANES, width), F32),
        ],
        26,
        idx, *blocks, *payloads, conv_weight, even, odd, encoder_grad[0],
    )
    encs = [encoded]
    for bit in bits[:-1]:
        encs = encs + [swap(e, "mp", bit) for e in encs]

    everything = tuple(range(per))
    pieces_of = lambda k: everything[1:] if k == 0 else (everything if k == 1 else ())

    def gradient(group, hold):
        pieces = [pieces_of(k) for k in group]
        outs = []
        for q in pieces:
            if not pair:
                outs.append([jax.ShapeDtypeStruct((peers * depth, width), BF16)])
                continue
            whole = jax.ShapeDtypeStruct((per * depth, width), BF16)
            outs.append([whole] + ([piece] * len(q) if q else [whole]))
        flat = call(
            functools.partial(grad_kernel, group, depth, per, pieces),
            tuple(o for tap in outs for o in tap),
            [pltpu.VMEM((LANES, width * min(len(group), 2)), F32)],
            18,
            after(idx, *hold) if hold else idx, joined, pre_grad,
        )
        flat = list(flat)
        taken = [[flat.pop(0) for _ in tap] for tap in outs]
        return [t[0] for t in taken], [t[1:] for t in taken]

    qkv_call = lambda idx, encs: call(
        functools.partial(qkv_kernel, offsets),
        jax.ShapeDtypeStruct((half, qkv_weight.shape[1]), BF16),
        [],
        8,
        idx, *encs, *payloads, qkv_weight,
    )
    if not pair:
        sums = [gradient((k,), [])[0][0] for k in range(taps)]
        sums = [lax.psum_scatter(v, "seq", scatter_dimension=0, tiled=True) for v in sums]
        sums = [lax.psum(v, "dp").astype(F32) for v in sums]
        encs = encs + [swap(e, "mp", bits[-1]) for e in encs]
        return (qkv_call(idx, encs)[None], jnp.stack(sums, axis=1))

    chunks = taps * per
    keep, send, got, relays, done = [], [], {}, [], {}

    def work(group, hold):
        if not group:
            return
        mine, other = gradient(group, hold)
        keep.extend(mine)
        send.extend(other if send else [list(first) + other[0]] + other[1:])

    def launch(tap, hold):
        if tap < taps:
            got[tap] = [swap(after(v, *hold) if hold else v, "seq", 1) for v in send[tap]]

    work(tuple(range(min(3, taps))), [])
    launch(0, [])
    launch(1, [])

    def share(c, last):
        tap, row = c // per, c % per
        rows = slice(row * depth, (row + 1) * depth)
        value = got[tap][row] if len(got[tap]) > 1 else got[tap][0][rows]
        hold = ([] if last is None else [last]) + (encs[1:] if c == 2 else [])
        return added(keep[tap][rows], after(value, *hold) if hold else value)

    starts = {(k - 1) * per - 1 - (k == 3): k for k in range(2, taps)}

    def sent(r, last, sums):
        if r < chunks and r in starts:
            launch(starts[r], [last])
        if r == chunks + 2:
            early = len(sums) // per
            parts = [sums[i] for i in range(early * per)]
            parts[0] = (after(parts[0][0], last), parts[0][1])
            last = done["early"] = written(parts, early, 0, None, (taps, per * depth, width))
            done["at"] = early
        return last

    def idle(c, last, sums):
        if c == per + 4:
            held = encs[1:]
            relays.extend([swap(after(e, last, *held), "mp", bits[-1]) for e in encs])
        if c == 0:
            work(tuple(range(3, taps)), [last])
            last = keep[-1]
        if c == chunks:
            last = done["qkv"] = qkv_call(after(idx, last, *relays), encs + relays)
        return last

    sums = chain_sums(chunks, share, sent, idle)
    shape = (taps, per * depth, width)
    conv_grad, early = done["early"], done["at"]
    for k in range(early, taps):
        conv_grad = written(sums[k * per : (k + 1) * per], 1, k, conv_grad, shape)
    return (done["qkv"][None], jnp.swapaxes(conv_grad, 0, 1))


def solution(mesh):
    return jax.shard_map(
        on_device,
        mesh=mesh,
        in_specs=(
            P("dp", "seq", "mp"),
            P(None, None, "mp"),
            P("mp"),
            P(None, "mp"),
            P("dp", "seq", "mp"),
        ),
        out_specs=(P("dp", "seq", "mp"), P("seq", None, "mp")),
        check_vma=False,
    )
```

```python
import functools

import jax
import jax.numpy as jnp
from jax import lax
from jax.experimental import pallas as pl
from jax.experimental.pallas import tpu as pltpu
from jax.sharding import PartitionSpec as P

EDGE = 8
LANES = 128
F32 = jnp.float32
BF16 = jnp.bfloat16


def gelu_parts(v):
    u = 0.7978845608 * (v + 0.044715 * v * v * v)
    th = jnp.tanh(u)
    value = 0.5 * v * (1.0 + th)
    slope = 0.5 * (1.0 + th) + 0.5 * v * (1.0 - th * th) * 0.7978845608 * (1.0 + 0.134145 * v * v)
    return value, slope


def swap(value, axis, bit):
    peers = lax.axis_size(axis)
    return lax.ppermute(value, axis, [(i, i ^ bit) for i in range(peers)])


def edge_block(ref, depth):
    rows = jnp.concatenate([ref[0:8, :], jnp.zeros((LANES - 8, ref.shape[1]), F32)], axis=0)
    keep = lax.broadcasted_iota(jnp.int32, rows.shape, 0) < 4
    return jnp.where(keep, rows, 0.0).T[0:depth, :].astype(BF16)


def conv_rows(offsets, me, x_refs, halo_refs, w_ref, rows_scr, y_scr):
    taps, width = w_ref.shape[0], w_ref.shape[2]
    length = x_refs[0].shape[1]
    x = jnp.concatenate([ref[...] for ref in x_refs], axis=0)
    depth = x.shape[0] // len(offsets)
    halo = jnp.concatenate([edge_block(ref, depth) for ref in halo_refs], axis=0)
    rows_scr[0:length, :] = x.T
    rows_scr[length : length + 16, :] = halo.T[0:16]
    starts = [pl.multiple_of((me ^ off) * depth, 16) for off in offsets]
    for first in range(0, taps, 2):
        group = range(first, min(first + 2, taps))
        w = jnp.concatenate(
            [
                jnp.concatenate([w_ref[k, pl.ds(s, depth), :] for s in starts], axis=0)
                for k in group
            ],
            axis=1,
        )
        y = jnp.dot(rows_scr[...], w, preferred_element_type=F32)
        for c in range(w.shape[1] // LANES):
            part = y[:, c * LANES : (c + 1) * LANES]
            at = first * width // LANES + c
            y_scr[at, EDGE : EDGE + length, :] = part[0:length]
            y_scr[at, EDGE - 2 : EDGE, :] = part[length : length + 2]
            y_scr[at, EDGE + length : EDGE + length + 2, :] = part[length + 2 : length + 4]


def tap_sum(y_scr, start, count, phase, taps, c):
    total = None
    for k in range(taps):
        at = k * (y_scr.shape[0] // taps) + c
        part = y_scr[at, pl.ds(EDGE + 2 * start + phase + k - 2, count, stride=2), :]
        total = part if total is None else total + part
    return total


def first_kernel(offsets, idx_ref, *refs):
    n = len(offsets)
    *x_refs, w_ref, even_ref, odd_ref, rows_scr, y_scr = refs
    x_refs, halo_refs = x_refs[:-n], x_refs[-n:]
    conv_rows(offsets, idx_ref[0], x_refs, halo_refs, w_ref, rows_scr, y_scr)
    taps, width = w_ref.shape[0], w_ref.shape[2]
    half = even_ref.shape[0]
    step = min(64, half)
    for start in range(0, half, step):
        rows = slice(start, start + step)
        for c in range(width // LANES):
            lanes = slice(c * LANES, (c + 1) * LANES)
            even_ref[rows, lanes] = tap_sum(y_scr, start, step, 0, taps, c)
            odd_ref[rows, lanes] = tap_sum(y_scr, start, step, 1, taps, c)


def second_kernel(offsets, far, per, idx_ref, *refs):
    n = len(offsets)
    blocks, pays, refs = refs[:n], refs[n : 2 * n], refs[2 * n :]
    w_ref, even_ref, odd_ref, grad_ref, enc_ref, pre_ref, all_ref, *sent_refs = refs[:-4]
    rows_scr, y_scr, p_scr, edge_scr = refs[-4:]
    me = idx_ref[0]
    pick = lambda items: [items[j] for j in far]
    conv_rows(pick(offsets), me, pick(blocks), pick(pays), w_ref, rows_scr, y_scr)
    taps, width = w_ref.shape[0], w_ref.shape[2]
    half = even_ref.shape[0]
    step = min(64, half)
    length = 2 * half
    zero = jnp.zeros((EDGE, width), F32)
    pre_ref[0:EDGE, :] = zero
    pre_ref[EDGE + length : 2 * EDGE + length, :] = zero
    for start in range(0, half, step):
        rows = slice(start, start + step)
        for c in range(width // LANES):
            lanes = slice(c * LANES, (c + 1) * LANES)
            even = even_ref[rows, lanes] + tap_sum(y_scr, start, step, 0, taps, c)
            odd = odd_ref[rows, lanes] + tap_sum(y_scr, start, step, 1, taps, c)
            act_even, slope_even = gelu_parts(even)
            act_odd, slope_odd = gelu_parts(odd)
            enc_ref[rows, lanes] = (0.5 * (act_even + act_odd)).astype(BF16)
            spread = grad_ref[rows, lanes].astype(F32)
            p_scr[c, pl.ds(2 * start, step, stride=2), :] = slope_even * 0.5 * spread
            p_scr[c, pl.ds(2 * start + 1, step, stride=2), :] = slope_odd * 0.5 * spread
    for c in range(width // LANES):
        lanes = slice(c * LANES, (c + 1) * LANES)
        pre_ref[EDGE : EDGE + length, lanes] = p_scr[c].astype(BF16).astype(F32)
    depth = blocks[0].shape[0]
    for off, block, pay in zip(offsets, blocks, pays):
        rows = pl.ds(pl.multiple_of((me ^ off) * depth, 16), depth)
        all_ref[rows, 0:length] = block[...]
        all_ref[rows, length : length + LANES] = edge_block(pay, depth)
    if sent_refs:
        wanted = pl.ds(pl.multiple_of((1 - idx_ref[1]) * per * depth, 16), depth)
        rows = shifted_rows(pre_ref, edge_scr, (0,))
        sent_refs[0][...] = jnp.dot(all_ref[wanted, :], rows, preferred_element_type=F32).astype(BF16)


def shifted_rows(p_ref, edge_scr, group):
    length, width = p_ref.shape[0] - 2 * EDGE, p_ref.shape[1]
    edge_scr[...] = jnp.zeros_like(edge_scr)
    shifted = []
    for i, tap in enumerate(group):
        cols = slice(i * width, (i + 1) * width)
        edge_scr[0:2, cols] = p_ref[EDGE - tap : EDGE - tap + 2, :]
        edge_scr[2:4, cols] = p_ref[EDGE + length + 2 - tap : EDGE + length + 4 - tap, :]
        shifted.append(p_ref[EDGE + 2 - tap : EDGE + 2 - tap + length, :].astype(BF16))
    edge = edge_scr[:, 0 : len(group) * width].astype(BF16)
    return jnp.concatenate([jnp.concatenate(shifted, axis=1), edge], axis=0)


def grad_kernel(group, depth, per, pieces, idx_ref, all_ref, p_ref, *refs):
    out_refs, edge_scr = list(refs[:-1]), refs[-1]
    width = p_ref.shape[1]
    half = per * depth
    for first in range(0, len(group), 2):
        some = group[first : first + 2]
        rows = shifted_rows(p_ref, edge_scr, some)
        res = jnp.dot(all_ref[...], rows, preferred_element_type=F32).astype(BF16)
        for i in range(len(some)):
            part = res[:, i * width : (i + 1) * width]
            own_ref = out_refs.pop(0)
            if not per:
                own_ref[...] = part
                continue
            lower = idx_ref[1] == 0
            own_ref[...] = jnp.where(lower, part[0:half], part[half : 2 * half])
            other = jnp.where(lower, part[half : 2 * half], part[0:half])
            named = pieces[first + i]
            if not named:
                out_refs.pop(0)[...] = other
            for r in named:
                out_refs.pop(0)[...] = other[r * depth : (r + 1) * depth]


def qkv_kernel(offsets, idx_ref, *refs):
    n = len(offsets)
    enc_refs, gain_refs, (w_ref, out_ref) = refs[:n], refs[n : 2 * n], refs[2 * n :]
    depth = enc_refs[0].shape[1]
    values = [ref[...].astype(F32) for ref in enc_refs]
    channels = n * depth
    sums = sum(jnp.sum(v, axis=1, keepdims=True) for v in values)
    squares = sum(jnp.sum(v * v, axis=1, keepdims=True) for v in values)
    mean = sums / channels
    var = squares / channels - mean * mean
    scale = lax.rsqrt(var + 1e-05)
    total = None
    for off, v, gain_ref in zip(offsets, values, gain_refs):
        normal = ((v - mean) * scale * gain_ref[4:5, 0:depth]).astype(BF16)
        w = w_ref[pl.ds(pl.multiple_of((idx_ref[0] ^ off) * depth, 16), depth), :]
        part = jnp.dot(normal, w, preferred_element_type=F32)
        total = part if total is None else total + part
    out_ref[...] = total.astype(BF16)


def call(kernel, out, scratch, mib, idx, *arrays):
    vmem = pl.BlockSpec(memory_space=pltpu.VMEM)
    return pl.pallas_call(
        kernel,
        out_shape=out,
        in_specs=[pl.BlockSpec(memory_space=pltpu.SMEM)] + [vmem] * len(arrays),
        out_specs=jax.tree.map(lambda _: vmem, out),
        scratch_shapes=scratch,
        compiler_params=pltpu.CompilerParams(vmem_limit_bytes=mib * 1024 * 1024),
    )(idx, *arrays)


def after(value, *others):
    return lax.optimization_barrier((value, *others))[0]


def write_kernel(end_ref, *refs):
    *part_refs, out_ref = refs
    count = len(part_refs) // 2
    pieces = count // out_ref.shape[0]
    rows = part_refs[0].shape[0]
    for i in range(count):
        tap, r = i // pieces, i % pieces
        for ref, here in ((part_refs[2 * i], end_ref[0] > 0), (part_refs[2 * i + 1], end_ref[0] == 0)):

            @pl.when(here)
            def _(ref=ref, tap=tap, r=r):
                out_ref[tap, r * rows : (r + 1) * rows, :] = ref[...].astype(F32)


def written(parts, taps, at, buffer, shape):
    me = lax.axis_index("dp")
    end = jnp.logical_or(me == 0, me == lax.axis_size("dp") - 1).astype(jnp.int32).reshape(1)
    parts = [v for pair in parts for v in pair]
    rows, width = parts[0].shape
    extra = [] if buffer is None else [buffer]
    kernel = write_kernel if buffer is None else lambda end, b, *refs: write_kernel(end, *refs)
    return pl.pallas_call(
        kernel,
        out_shape=jax.ShapeDtypeStruct(shape, F32),
        grid=(1,),
        in_specs=[pl.BlockSpec(memory_space=pltpu.SMEM)]
        + [pl.BlockSpec(memory_space=pl.ANY)] * len(extra)
        + [pl.BlockSpec((rows, width), lambda i: (0, 0))] * len(parts),
        out_specs=pl.BlockSpec((taps, shape[1], width), lambda i: (at // taps, 0, 0)),
        input_output_aliases={1: 0} if extra else {},
        compiler_params=pltpu.CompilerParams(vmem_limit_bytes=16 * 1024 * 1024),
    )(end, *extra, *parts)


def edge_kernel(head_ref, tail_ref, out_ref):
    depth = head_ref.shape[0]
    extra = jnp.zeros((out_ref.shape[1] - depth, LANES), F32)
    head = jnp.concatenate([head_ref[...].astype(F32), extra], axis=0).T
    tail = jnp.concatenate([tail_ref[...].astype(F32), extra], axis=0).T
    out_ref[...] = jnp.zeros_like(out_ref)
    out_ref[0:2, :] = head[0:2]
    out_ref[2:4, :] = tail[LANES - 2 : LANES]


def edge_rows(x, width):
    peers = lax.axis_size("seq")
    me = lax.axis_index("seq")
    depth, length = x.shape
    ends = pl.pallas_call(
        edge_kernel,
        out_shape=jax.ShapeDtypeStruct((8, width), F32),
        grid=(1,),
        in_specs=[
            pl.BlockSpec((depth, LANES), lambda i: (0, 0)),
            pl.BlockSpec((depth, LANES), lambda i: (0, length // LANES - 1)),
        ],
        out_specs=pl.BlockSpec((8, width), lambda i: (0, 0)),
        compiler_params=pltpu.CompilerParams(vmem_limit_bytes=2 * 1024 * 1024),
    )(x, x)
    if peers == 2:
        before = behind = swap(ends, "seq", 1)
    else:
        up = [(i, (i + 1) % peers) for i in range(peers - 1)]
        down = [(j, i) for i, j in up]
        before, behind = lax.ppermute(ends, "seq", up), lax.ppermute(ends, "seq", down)
    before = jnp.where(me == 0, 0.0, before[2:4])
    behind = jnp.where(me == peers - 1, 0.0, behind[0:2])
    return jnp.concatenate([before, behind], axis=0)


def added(a, b):
    return (a.astype(F32) + b.astype(F32)).astype(BF16)


def chain_sums(count, part, sent, idle):
    me = lax.axis_index("dp")
    end = jnp.logical_or(me == 0, me == 3)
    outer_pairs = [(0, 1), (1, 0), (2, 3), (3, 2)]
    middle_pairs = [(1, 2), (2, 1)]
    last = None
    h, p, s, outer, middle, sums = {}, {}, {}, {}, {}, {}
    for r in range(count + 5):
        if r < count:
            h[r] = part(r, last)
        if r < count + 3:
            value = h.get(r, s.get(r - 3))
            if r in h and r - 3 in s:
                value = jnp.where(end, h[r], s[r - 3])
            last = value = lax.optimization_barrier(value)
            outer[r] = lax.ppermute(value, "dp", outer_pairs)
            last = sent(r, last, sums)
        if r - 1 in outer:
            got = after(outer.pop(r - 1), last)
            if r - 1 < count:
                last = p[r - 1] = lax.optimization_barrier(added(h[r - 1], got))
                middle[r - 1] = lax.ppermute(last, "dp", middle_pairs)
            if r >= 4:
                sums[r - 4] = (got, s[r - 4])
                if r - 1 >= count:
                    last = got
            last = idle(r - 1, last, sums)
        if r - 2 in middle:
            got = after(middle.pop(r - 2), last)
            last = s[r - 2] = lax.optimization_barrier(added(p[r - 2], got))
    return [sums[c] for c in range(count)]


def on_device(block_input, conv_weight, norm_gain, qkv_weight, encoder_grad):
    x = jnp.swapaxes(block_input[0], 0, 1)
    depth, length = x.shape
    taps, _, width = conv_weight.shape
    peers, shards = lax.axis_size("mp"), lax.axis_size("seq")
    bits = [1 << b for b in reversed(range(peers.bit_length() - 1))]
    idx = jnp.stack([lax.axis_index("mp"), lax.axis_index("seq")]).astype(jnp.int32)

    offsets = [0]
    for bit in bits:
        offsets = offsets + [o ^ bit for o in offsets]
    near = [j for j, o in enumerate(offsets) if o < 2]
    far = [j for j, o in enumerate(offsets) if o >= 2]
    half = length // 2
    pick = lambda items, at: [items[j] for j in at]
    scratch = lambda at: [
        pltpu.VMEM((length + 16, len(at) * depth), BF16),
        pltpu.VMEM((taps * width // LANES, length + 2 * EDGE, LANES), F32),
    ]

    blocks = [x]
    for bit in bits[:-1]:
        blocks = blocks + [swap(b, "mp", bit) for b in blocks]
    own = swap(x, "mp", bits[-1])
    edges = edge_rows(x, width)
    payload = jnp.concatenate([edges, norm_gain.reshape(1, -1), jnp.zeros((3, width), F32)], axis=0)
    payloads = [payload] + [swap(payload, "mp", o) for o in offsets[1:]]

    part = jax.ShapeDtypeStruct((half, width), F32)
    even, odd = call(
        functools.partial(first_kernel, pick(offsets, near)),
        (part, part),
        scratch(near),
        24,
        idx, x, own, *pick(payloads, near), conv_weight,
    )
    hold = [even] + pick(payloads, far)
    blocks = blocks + [own] + [swap(after(b, *hold), "mp", bits[-1]) for b in blocks[1:]]
    pair = shards == 2 and peers % shards == 0 and lax.axis_size("dp") == 4
    per = peers // shards if pair else 0
    piece = jax.ShapeDtypeStruct((depth, width), BF16)
    encoded, pre_grad, joined, *first = call(
        functools.partial(second_kernel, offsets, far, per),
        (
            jax.ShapeDtypeStruct((half, width), BF16),
            jax.ShapeDtypeStruct((length + 2 * EDGE, width), F32),
            jax.ShapeDtypeStruct((peers * depth, length + LANES), BF16),
            *([piece] if pair else []),
        ),
        scratch(far)
        + [
            pltpu.VMEM((width // LANES, length, LANES), F32),
            pltpu.VMEM((LANES, width), F32),
        ],
        26,
        idx, *blocks, *payloads, conv_weight, even, odd, encoder_grad[0],
    )
    encs = [encoded]
    for bit in bits[:-1]:
        encs = encs + [swap(e, "mp", bit) for e in encs]

    everything = tuple(range(per))
    pieces_of = lambda k: everything[1:] if k == 0 else (everything if k == 1 else ())

    def gradient(group, hold):
        pieces = [pieces_of(k) for k in group]
        outs = []
        for q in pieces:
            if not pair:
                outs.append([jax.ShapeDtypeStruct((peers * depth, width), BF16)])
                continue
            whole = pltpu.HBM((per * depth, width), BF16)
            outs.append([whole] + ([piece] * len(q) if q else [whole]))
        flat = call(
            functools.partial(grad_kernel, group, depth, per, pieces),
            tuple(o for tap in outs for o in tap),
            [pltpu.VMEM((LANES, width * min(len(group), 2)), F32)],
            24 if len(group) > 2 else 16,
            after(idx, *hold) if hold else idx, joined, pre_grad,
        )
        flat = list(flat)
        taken = [[flat.pop(0) for _ in tap] for tap in outs]
        return [t[0] for t in taken], [t[1:] for t in taken]

    qkv_call = lambda idx, encs: call(
        functools.partial(qkv_kernel, offsets),
        jax.ShapeDtypeStruct((half, qkv_weight.shape[1]), BF16),
        [],
        8,
        idx, *encs, *payloads, qkv_weight,
    )
    if not pair:
        sums = [gradient((k,), [])[0][0] for k in range(taps)]
        sums = [lax.psum_scatter(v, "seq", scatter_dimension=0, tiled=True) for v in sums]
        sums = [lax.psum(v, "dp").astype(F32) for v in sums]
        encs = encs + [swap(e, "mp", bits[-1]) for e in encs]
        return (qkv_call(idx, encs)[None], jnp.stack(sums, axis=1))

    chunks = taps * per
    keep, send, got, relays, done = [], [], {}, [], {}

    def work(group, hold):
        if not group:
            return
        mine, other = gradient(group, hold)
        keep.extend(mine)
        send.extend(other if send else [list(first) + other[0]] + other[1:])

    def launch(tap, hold):
        if tap < taps:
            got[tap] = [swap(after(v, *hold) if hold else v, "seq", 1) for v in send[tap]]

    work((0,), [])
    launch(0, [])
    work(tuple(range(1, min(3, taps))), [keep[-1]])
    launch(1, [])

    def share(c, last):
        tap, row = c // per, c % per
        rows = slice(row * depth, (row + 1) * depth)
        value = got[tap][row] if len(got[tap]) > 1 else got[tap][0][rows]
        return added(keep[tap][rows], value if last is None else after(value, last))

    starts = {(k - 1) * per - 1 - (k == 3): k for k in range(2, taps)}

    def sent(r, last, sums):
        if r < chunks and r in starts:
            launch(starts[r], [last])
        if r == chunks + 2:
            early = len(sums) // per
            parts = [sums[i] for i in range(early * per)]
            parts[0] = (after(parts[0][0], last), parts[0][1])
            last = done["early"] = written(parts, early, 0, None, (taps, per * depth, width))
            done["at"] = early
        return last

    def idle(c, last, sums):
        if c == per + 4:
            held = encs[1:]
            relays.extend([swap(after(e, last, *held), "mp", bits[-1]) for e in encs])
        if c == 0:
            work(tuple(range(3, taps)), [last] + encs[1:])
            last = keep[-1]
        if c == chunks:
            last = done["qkv"] = qkv_call(after(idx, last, *relays), encs + relays)
        return last

    sums = chain_sums(chunks, share, sent, idle)
    shape = (taps, per * depth, width)
    conv_grad, early = done["early"], done["at"]
    for k in range(early, taps):
        conv_grad = written(sums[k * per : (k + 1) * per], 1, k, conv_grad, shape)
    return (done["qkv"][None], jnp.swapaxes(conv_grad, 0, 1))


def solution(mesh):
    return jax.shard_map(
        on_device,
        mesh=mesh,
        in_specs=(
            P("dp", "seq", "mp"),
            P(None, None, "mp"),
            P("mp"),
            P(None, "mp"),
            P("dp", "seq", "mp"),
        ),
        out_specs=(P("dp", "seq", "mp"), P("seq", None, "mp")),
        check_vma=False,
    )
```

```python
import functools

import jax
import jax.numpy as jnp
from jax import lax
from jax.experimental import pallas as pl
from jax.experimental.pallas import tpu as pltpu
from jax.sharding import PartitionSpec as P

EDGE = 8
LANES = 128
F32 = jnp.float32
BF16 = jnp.bfloat16


def gelu_parts(v):
    u = 0.7978845608 * (v + 0.044715 * v * v * v)
    th = jnp.tanh(u)
    value = 0.5 * v * (1.0 + th)
    slope = 0.5 * (1.0 + th) + 0.5 * v * (1.0 - th * th) * 0.7978845608 * (1.0 + 0.134145 * v * v)
    return value, slope


def swap(value, axis, bit):
    peers = lax.axis_size(axis)
    return lax.ppermute(value, axis, [(i, i ^ bit) for i in range(peers)])


def edge_block(ref, depth):
    rows = jnp.concatenate([ref[0:8, :], jnp.zeros((LANES - 8, ref.shape[1]), F32)], axis=0)
    keep = lax.broadcasted_iota(jnp.int32, rows.shape, 0) < 4
    return jnp.where(keep, rows, 0.0).T[0:depth, :].astype(BF16)


def conv_rows(offsets, me, x_refs, halo_refs, w_ref, rows_scr, y_scr):
    taps, width = w_ref.shape[0], w_ref.shape[2]
    length = x_refs[0].shape[1]
    x = jnp.concatenate([ref[...] for ref in x_refs], axis=0)
    depth = x.shape[0] // len(offsets)
    halo = jnp.concatenate([edge_block(ref, depth) for ref in halo_refs], axis=0)
    rows_scr[0:length, :] = x.T
    rows_scr[length : length + 16, :] = halo.T[0:16]
    starts = [pl.multiple_of((me ^ off) * depth, 16) for off in offsets]
    for first in range(0, taps, 2):
        group = range(first, min(first + 2, taps))
        w = jnp.concatenate(
            [
                jnp.concatenate([w_ref[k, pl.ds(s, depth), :] for s in starts], axis=0)
                for k in group
            ],
            axis=1,
        )
        y = jnp.dot(rows_scr[...], w, preferred_element_type=F32)
        for c in range(w.shape[1] // LANES):
            part = y[:, c * LANES : (c + 1) * LANES]
            at = first * width // LANES + c
            y_scr[at, EDGE : EDGE + length, :] = part[0:length]
            y_scr[at, EDGE - 2 : EDGE, :] = part[length : length + 2]
            y_scr[at, EDGE + length : EDGE + length + 2, :] = part[length + 2 : length + 4]


def tap_sum(y_scr, start, count, phase, taps, c):
    total = None
    for k in range(taps):
        at = k * (y_scr.shape[0] // taps) + c
        part = y_scr[at, pl.ds(EDGE + 2 * start + phase + k - 2, count, stride=2), :]
        total = part if total is None else total + part
    return total


def first_kernel(offsets, idx_ref, *refs):
    n = len(offsets)
    *x_refs, w_ref, even_ref, odd_ref, rows_scr, y_scr = refs
    x_refs, halo_refs = x_refs[:-n], x_refs[-n:]
    conv_rows(offsets, idx_ref[0], x_refs, halo_refs, w_ref, rows_scr, y_scr)
    taps, width = w_ref.shape[0], w_ref.shape[2]
    half = even_ref.shape[0]
    step = min(64, half)
    for start in range(0, half, step):
        rows = slice(start, start + step)
        for c in range(width // LANES):
            lanes = slice(c * LANES, (c + 1) * LANES)
            even_ref[rows, lanes] = tap_sum(y_scr, start, step, 0, taps, c)
            odd_ref[rows, lanes] = tap_sum(y_scr, start, step, 1, taps, c)


def second_kernel(offsets, far, per, idx_ref, *refs):
    n = len(offsets)
    blocks, pays, refs = refs[:n], refs[n : 2 * n], refs[2 * n :]
    w_ref, even_ref, odd_ref, grad_ref, enc_ref, pre_ref, all_ref, *sent_refs = refs[:-4]
    rows_scr, y_scr, p_scr, edge_scr = refs[-4:]
    me = idx_ref[0]
    pick = lambda items: [items[j] for j in far]
    conv_rows(pick(offsets), me, pick(blocks), pick(pays), w_ref, rows_scr, y_scr)
    taps, width = w_ref.shape[0], w_ref.shape[2]
    half = even_ref.shape[0]
    step = min(64, half)
    length = 2 * half
    zero = jnp.zeros((EDGE, width), F32)
    pre_ref[0:EDGE, :] = zero
    pre_ref[EDGE + length : 2 * EDGE + length, :] = zero
    for start in range(0, half, step):
        rows = slice(start, start + step)
        for c in range(width // LANES):
            lanes = slice(c * LANES, (c + 1) * LANES)
            even = even_ref[rows, lanes] + tap_sum(y_scr, start, step, 0, taps, c)
            odd = odd_ref[rows, lanes] + tap_sum(y_scr, start, step, 1, taps, c)
            act_even, slope_even = gelu_parts(even)
            act_odd, slope_odd = gelu_parts(odd)
            enc_ref[rows, lanes] = (0.5 * (act_even + act_odd)).astype(BF16)
            spread = grad_ref[rows, lanes].astype(F32)
            p_scr[c, pl.ds(2 * start, step, stride=2), :] = slope_even * 0.5 * spread
            p_scr[c, pl.ds(2 * start + 1, step, stride=2), :] = slope_odd * 0.5 * spread
    for c in range(width // LANES):
        lanes = slice(c * LANES, (c + 1) * LANES)
        pre_ref[EDGE : EDGE + length, lanes] = p_scr[c].astype(BF16).astype(F32)
    depth = blocks[0].shape[0]
    for off, block, pay in zip(offsets, blocks, pays):
        rows = pl.ds(pl.multiple_of((me ^ off) * depth, 16), depth)
        all_ref[rows, 0:length] = block[...]
        all_ref[rows, length : length + LANES] = edge_block(pay, depth)
    if sent_refs:
        wanted = pl.ds(pl.multiple_of((1 - idx_ref[1]) * per * depth, 16), depth)
        rows = shifted_rows(pre_ref, edge_scr, (0,))
        sent_refs[0][...] = jnp.dot(all_ref[wanted, :], rows, preferred_element_type=F32).astype(BF16)


def shifted_rows(p_ref, edge_scr, group):
    length, width = p_ref.shape[0] - 2 * EDGE, p_ref.shape[1]
    edge_scr[...] = jnp.zeros_like(edge_scr)
    shifted = []
    for i, tap in enumerate(group):
        cols = slice(i * width, (i + 1) * width)
        edge_scr[0:2, cols] = p_ref[EDGE - tap : EDGE - tap + 2, :]
        edge_scr[2:4, cols] = p_ref[EDGE + length + 2 - tap : EDGE + length + 4 - tap, :]
        shifted.append(p_ref[EDGE + 2 - tap : EDGE + 2 - tap + length, :].astype(BF16))
    edge = edge_scr[:, 0 : len(group) * width].astype(BF16)
    return jnp.concatenate([jnp.concatenate(shifted, axis=1), edge], axis=0)


def grad_kernel(group, depth, per, pieces, idx_ref, all_ref, p_ref, *refs):
    out_refs, edge_scr = list(refs[:-1]), refs[-1]
    width = p_ref.shape[1]
    half = per * depth
    for first in range(0, len(group), 2):
        some = group[first : first + 2]
        rows = shifted_rows(p_ref, edge_scr, some)
        res = jnp.dot(all_ref[...], rows, preferred_element_type=F32).astype(BF16)
        for i in range(len(some)):
            part = res[:, i * width : (i + 1) * width]
            own_ref = out_refs.pop(0)
            if not per:
                own_ref[...] = part
                continue
            lower = idx_ref[1] == 0
            own_ref[...] = jnp.where(lower, part[0:half], part[half : 2 * half])
            other = jnp.where(lower, part[half : 2 * half], part[0:half])
            named = pieces[first + i]
            if not named:
                out_refs.pop(0)[...] = other
            for r in named:
                out_refs.pop(0)[...] = other[r * depth : (r + 1) * depth]


def qkv_kernel(offsets, idx_ref, *refs):
    n = len(offsets)
    enc_refs, gain_refs, (w_ref, out_ref) = refs[:n], refs[n : 2 * n], refs[2 * n :]
    depth = enc_refs[0].shape[1]
    values = [ref[...].astype(F32) for ref in enc_refs]
    channels = n * depth
    sums = sum(jnp.sum(v, axis=1, keepdims=True) for v in values)
    squares = sum(jnp.sum(v * v, axis=1, keepdims=True) for v in values)
    mean = sums / channels
    var = squares / channels - mean * mean
    scale = lax.rsqrt(var + 1e-05)
    total = None
    for off, v, gain_ref in zip(offsets, values, gain_refs):
        normal = ((v - mean) * scale * gain_ref[4:5, 0:depth]).astype(BF16)
        w = w_ref[pl.ds(pl.multiple_of((idx_ref[0] ^ off) * depth, 16), depth), :]
        part = jnp.dot(normal, w, preferred_element_type=F32)
        total = part if total is None else total + part
    out_ref[...] = total.astype(BF16)


def call(kernel, out, scratch, mib, idx, *arrays):
    vmem = pl.BlockSpec(memory_space=pltpu.VMEM)
    return pl.pallas_call(
        kernel,
        out_shape=out,
        in_specs=[pl.BlockSpec(memory_space=pltpu.SMEM)] + [vmem] * len(arrays),
        out_specs=jax.tree.map(lambda _: vmem, out),
        scratch_shapes=scratch,
        compiler_params=pltpu.CompilerParams(vmem_limit_bytes=mib * 1024 * 1024),
    )(idx, *arrays)


def after(value, *others):
    return lax.optimization_barrier((value, *others))[0]


def write_kernel(end_ref, *refs):
    *part_refs, out_ref = refs
    count = len(part_refs) // 2
    pieces = count // out_ref.shape[0]
    rows = part_refs[0].shape[0]
    for i in range(count):
        tap, r = i // pieces, i % pieces
        for ref, here in ((part_refs[2 * i], end_ref[0] > 0), (part_refs[2 * i + 1], end_ref[0] == 0)):

            @pl.when(here)
            def _(ref=ref, tap=tap, r=r):
                out_ref[tap, r * rows : (r + 1) * rows, :] = ref[...].astype(F32)


def written(parts, taps, at, buffer, shape):
    me = lax.axis_index("dp")
    end = jnp.logical_or(me == 0, me == lax.axis_size("dp") - 1).astype(jnp.int32).reshape(1)
    parts = [v for pair in parts for v in pair]
    rows, width = parts[0].shape
    extra = [] if buffer is None else [buffer]
    kernel = write_kernel if buffer is None else lambda end, b, *refs: write_kernel(end, *refs)
    return pl.pallas_call(
        kernel,
        out_shape=jax.ShapeDtypeStruct(shape, F32),
        grid=(1,),
        in_specs=[pl.BlockSpec(memory_space=pltpu.SMEM)]
        + [pl.BlockSpec(memory_space=pl.ANY)] * len(extra)
        + [pl.BlockSpec((rows, width), lambda i: (0, 0))] * len(parts),
        out_specs=pl.BlockSpec((taps, shape[1], width), lambda i: (at // taps, 0, 0)),
        input_output_aliases={1: 0} if extra else {},
        compiler_params=pltpu.CompilerParams(vmem_limit_bytes=16 * 1024 * 1024),
    )(end, *extra, *parts)


def edge_kernel(head_ref, tail_ref, out_ref):
    depth = head_ref.shape[0]
    extra = jnp.zeros((out_ref.shape[1] - depth, LANES), F32)
    head = jnp.concatenate([head_ref[...].astype(F32), extra], axis=0).T
    tail = jnp.concatenate([tail_ref[...].astype(F32), extra], axis=0).T
    out_ref[...] = jnp.zeros_like(out_ref)
    out_ref[0:2, :] = head[0:2]
    out_ref[2:4, :] = tail[LANES - 2 : LANES]


def edge_rows(x, width):
    peers = lax.axis_size("seq")
    me = lax.axis_index("seq")
    depth, length = x.shape
    ends = pl.pallas_call(
        edge_kernel,
        out_shape=jax.ShapeDtypeStruct((8, width), F32),
        grid=(1,),
        in_specs=[
            pl.BlockSpec((depth, LANES), lambda i: (0, 0)),
            pl.BlockSpec((depth, LANES), lambda i: (0, length // LANES - 1)),
        ],
        out_specs=pl.BlockSpec((8, width), lambda i: (0, 0)),
        compiler_params=pltpu.CompilerParams(vmem_limit_bytes=2 * 1024 * 1024),
    )(x, x)
    if peers == 2:
        before = behind = swap(ends, "seq", 1)
    else:
        up = [(i, (i + 1) % peers) for i in range(peers - 1)]
        down = [(j, i) for i, j in up]
        before, behind = lax.ppermute(ends, "seq", up), lax.ppermute(ends, "seq", down)
    before = jnp.where(me == 0, 0.0, before[2:4])
    behind = jnp.where(me == peers - 1, 0.0, behind[0:2])
    return jnp.concatenate([before, behind], axis=0)


def added(a, b):
    return (a.astype(F32) + b.astype(F32)).astype(BF16)


def chain_sums(count, part, sent, idle):
    me = lax.axis_index("dp")
    end = jnp.logical_or(me == 0, me == 3)
    outer_pairs = [(0, 1), (1, 0), (2, 3), (3, 2)]
    middle_pairs = [(1, 2), (2, 1)]
    last = None
    h, p, s, outer, middle, sums = {}, {}, {}, {}, {}, {}
    for r in range(count + 5):
        if r < count:
            h[r] = part(r, last)
        if r < count + 3:
            value = h.get(r, s.get(r - 3))
            if r in h and r - 3 in s:
                value = jnp.where(end, h[r], s[r - 3])
            last = value = lax.optimization_barrier(value)
            outer[r] = lax.ppermute(value, "dp", outer_pairs)
            last = sent(r, last, sums)
        if r - 1 in outer:
            got = after(outer.pop(r - 1), last)
            if r - 1 < count:
                last = p[r - 1] = lax.optimization_barrier(added(h[r - 1], got))
                middle[r - 1] = lax.ppermute(last, "dp", middle_pairs)
            if r >= 4:
                sums[r - 4] = (got, s[r - 4])
                if r - 1 >= count:
                    last = got
            last = idle(r - 1, last, sums)
        if r - 2 in middle:
            got = after(middle.pop(r - 2), last)
            last = s[r - 2] = lax.optimization_barrier(added(p[r - 2], got))
    return [sums[c] for c in range(count)]


def on_device(block_input, conv_weight, norm_gain, qkv_weight, encoder_grad):
    x = jnp.swapaxes(block_input[0], 0, 1)
    depth, length = x.shape
    taps, _, width = conv_weight.shape
    peers, shards = lax.axis_size("mp"), lax.axis_size("seq")
    bits = [1 << b for b in reversed(range(peers.bit_length() - 1))]
    idx = jnp.stack([lax.axis_index("mp"), lax.axis_index("seq")]).astype(jnp.int32)

    offsets = [0]
    for bit in bits:
        offsets = offsets + [o ^ bit for o in offsets]
    near = [j for j, o in enumerate(offsets) if o < 2]
    far = [j for j, o in enumerate(offsets) if o >= 2]
    half = length // 2
    pick = lambda items, at: [items[j] for j in at]
    scratch = lambda at: [
        pltpu.VMEM((length + 16, len(at) * depth), BF16),
        pltpu.VMEM((taps * width // LANES, length + 2 * EDGE, LANES), F32),
    ]

    blocks = [x]
    for bit in bits[:-1]:
        blocks = blocks + [swap(b, "mp", bit) for b in blocks]
    own = swap(x, "mp", bits[-1])
    edges = edge_rows(x, width)
    payload = jnp.concatenate([edges, norm_gain.reshape(1, -1), jnp.zeros((3, width), F32)], axis=0)
    payloads = [payload] + [swap(payload, "mp", o) for o in offsets[1:]]

    part = jax.ShapeDtypeStruct((half, width), F32)
    even, odd = call(
        functools.partial(first_kernel, pick(offsets, near)),
        (part, part),
        scratch(near),
        24,
        idx, x, own, *pick(payloads, near), conv_weight,
    )
    hold = [even] + pick(payloads, far)
    blocks = blocks + [own] + [swap(after(b, *hold), "mp", bits[-1]) for b in blocks[1:]]
    pair = shards == 2 and peers % shards == 0 and lax.axis_size("dp") == 4
    per = peers // shards if pair else 0
    piece = jax.ShapeDtypeStruct((depth, width), BF16)
    encoded, pre_grad, joined, *first = call(
        functools.partial(second_kernel, offsets, far, per),
        (
            jax.ShapeDtypeStruct((half, width), BF16),
            jax.ShapeDtypeStruct((length + 2 * EDGE, width), F32),
            jax.ShapeDtypeStruct((peers * depth, length + LANES), BF16),
            *([piece] if pair else []),
        ),
        scratch(far)
        + [
            pltpu.VMEM((width // LANES, length, LANES), F32),
            pltpu.VMEM((LANES, width), F32),
        ],
        26,
        idx, *blocks, *payloads, conv_weight, even, odd, encoder_grad[0],
    )
    encs = [encoded]
    for bit in bits[:-1]:
        encs = encs + [swap(e, "mp", bit) for e in encs]

    everything = tuple(range(per))
    pieces_of = lambda k: everything[1:] if k == 0 else (everything if k == 1 else ())

    def gradient(group, hold):
        pieces = [pieces_of(k) for k in group]
        outs = []
        for q in pieces:
            if not pair:
                outs.append([jax.ShapeDtypeStruct((peers * depth, width), BF16)])
                continue
            whole = jax.ShapeDtypeStruct((per * depth, width), BF16)
            outs.append([whole] + ([piece] * len(q) if q else [whole]))
        flat = call(
            functools.partial(grad_kernel, group, depth, per, pieces),
            tuple(o for tap in outs for o in tap),
            [pltpu.VMEM((LANES, width * min(len(group), 2)), F32)],
            24 if len(group) > 2 else 16,
            after(idx, *hold) if hold else idx, joined, pre_grad,
        )
        flat = list(flat)
        taken = [[flat.pop(0) for _ in tap] for tap in outs]
        return [t[0] for t in taken], [t[1:] for t in taken]

    qkv_call = lambda idx, encs: call(
        functools.partial(qkv_kernel, offsets),
        jax.ShapeDtypeStruct((half, qkv_weight.shape[1]), BF16),
        [],
        8,
        idx, *encs, *payloads, qkv_weight,
    )
    if not pair:
        sums = [gradient((k,), [])[0][0] for k in range(taps)]
        sums = [lax.psum_scatter(v, "seq", scatter_dimension=0, tiled=True) for v in sums]
        sums = [lax.psum(v, "dp").astype(F32) for v in sums]
        encs = encs + [swap(e, "mp", bits[-1]) for e in encs]
        return (qkv_call(idx, encs)[None], jnp.stack(sums, axis=1))

    chunks = taps * per
    keep, send, got, relays, done = [], [], {}, [], {}

    def work(group, hold):
        if not group:
            return
        mine, other = gradient(group, hold)
        keep.extend(mine)
        send.extend(other if send else [list(first) + other[0]] + other[1:])

    def launch(tap, hold):
        if tap < taps:
            got[tap] = [swap(after(v, *hold) if hold else v, "seq", 1) for v in send[tap]]

    work((0,), [])
    launch(0, [])
    work(tuple(range(1, min(3, taps))), [keep[-1]])
    launch(1, [])

    def share(c, last):
        tap, row = c // per, c % per
        rows = slice(row * depth, (row + 1) * depth)
        value = got[tap][row] if len(got[tap]) > 1 else got[tap][0][rows]
        hold = [keep[1]] if last is None else [last]
        if c == -1:
            hold = hold + encs[1:]
        return added(keep[tap][rows], after(value, *hold))

    starts = {(k - 1) * per - 1 - (k == 3): k for k in range(2, taps)}

    def sent(r, last, sums):
        if r < chunks and r in starts:
            launch(starts[r], [last])
        if r == chunks + 2:
            early = len(sums) // per
            parts = [sums[i] for i in range(early * per)]
            parts[0] = (after(parts[0][0], last), parts[0][1])
            last = done["early"] = written(parts, early, 0, None, (taps, per * depth, width))
            done["at"] = early
        return last

    def idle(c, last, sums):
        if c == per + 4:
            held = encs[1:]
            relays.extend([swap(after(e, last, *held), "mp", bits[-1]) for e in encs])
        if c == 0:
            work(tuple(range(3, taps)), [last] + encs[1:])
            last = keep[-1]
        if c == chunks:
            last = done["qkv"] = qkv_call(after(idx, last, *relays), encs + relays)
        return last

    sums = chain_sums(chunks, share, sent, idle)
    shape = (taps, per * depth, width)
    conv_grad, early = done["early"], done["at"]
    for k in range(early, taps):
        conv_grad = written(sums[k * per : (k + 1) * per], 1, k, conv_grad, shape)
    return (done["qkv"][None], jnp.swapaxes(conv_grad, 0, 1))


def solution(mesh):
    return jax.shard_map(
        on_device,
        mesh=mesh,
        in_specs=(
            P("dp", "seq", "mp"),
            P(None, None, "mp"),
            P("mp"),
            P(None, "mp"),
            P("dp", "seq", "mp"),
        ),
        out_specs=(P("dp", "seq", "mp"), P("seq", None, "mp")),
        check_vma=False,
    )
```

```python
import functools

import jax
import jax.numpy as jnp
from jax import lax
from jax.experimental import pallas as pl
from jax.experimental.pallas import tpu as pltpu
from jax.sharding import PartitionSpec as P

EDGE = 8
LANES = 128
F32 = jnp.float32
BF16 = jnp.bfloat16


def gelu_parts(v):
    u = 0.7978845608 * (v + 0.044715 * v * v * v)
    th = jnp.tanh(u)
    value = 0.5 * v * (1.0 + th)
    slope = 0.5 * (1.0 + th) + 0.5 * v * (1.0 - th * th) * 0.7978845608 * (1.0 + 0.134145 * v * v)
    return value, slope


def swap(value, axis, bit):
    peers = lax.axis_size(axis)
    return lax.ppermute(value, axis, [(i, i ^ bit) for i in range(peers)])


def edge_block(ref, depth):
    rows = jnp.concatenate([ref[0:8, :], jnp.zeros((LANES - 8, ref.shape[1]), F32)], axis=0)
    keep = lax.broadcasted_iota(jnp.int32, rows.shape, 0) < 4
    return jnp.where(keep, rows, 0.0).T[0:depth, :].astype(BF16)


def conv_rows(offsets, me, x_refs, halo_refs, w_ref, rows_scr, y_scr):
    taps, width = w_ref.shape[0], w_ref.shape[2]
    length = x_refs[0].shape[1]
    x = jnp.concatenate([ref[...] for ref in x_refs], axis=0)
    depth = x.shape[0] // len(offsets)
    halo = jnp.concatenate([edge_block(ref, depth) for ref in halo_refs], axis=0)
    rows_scr[0:length, :] = x.T
    rows_scr[length : length + 16, :] = halo.T[0:16]
    starts = [pl.multiple_of((me ^ off) * depth, 16) for off in offsets]
    for first in range(0, taps, 2):
        group = range(first, min(first + 2, taps))
        w = jnp.concatenate(
            [
                jnp.concatenate([w_ref[k, pl.ds(s, depth), :] for s in starts], axis=0)
                for k in group
            ],
            axis=1,
        )
        y = jnp.dot(rows_scr[...], w, preferred_element_type=F32)
        for c in range(w.shape[1] // LANES):
            part = y[:, c * LANES : (c + 1) * LANES]
            at = first * width // LANES + c
            y_scr[at, EDGE : EDGE + length, :] = part[0:length]
            y_scr[at, EDGE - 2 : EDGE, :] = part[length : length + 2]
            y_scr[at, EDGE + length : EDGE + length + 2, :] = part[length + 2 : length + 4]


def tap_sum(y_scr, start, count, phase, taps, c):
    total = None
    for k in range(taps):
        at = k * (y_scr.shape[0] // taps) + c
        part = y_scr[at, pl.ds(EDGE + 2 * start + phase + k - 2, count, stride=2), :]
        total = part if total is None else total + part
    return total


def first_kernel(offsets, idx_ref, *refs):
    n = len(offsets)
    *x_refs, w_ref, even_ref, odd_ref, rows_scr, y_scr = refs
    x_refs, halo_refs = x_refs[:-n], x_refs[-n:]
    conv_rows(offsets, idx_ref[0], x_refs, halo_refs, w_ref, rows_scr, y_scr)
    taps, width = w_ref.shape[0], w_ref.shape[2]
    half = even_ref.shape[0]
    step = min(64, half)
    for start in range(0, half, step):
        rows = slice(start, start + step)
        for c in range(width // LANES):
            lanes = slice(c * LANES, (c + 1) * LANES)
            even_ref[rows, lanes] = tap_sum(y_scr, start, step, 0, taps, c)
            odd_ref[rows, lanes] = tap_sum(y_scr, start, step, 1, taps, c)


def second_kernel(offsets, far, per, idx_ref, *refs):
    n = len(offsets)
    blocks, pays, refs = refs[:n], refs[n : 2 * n], refs[2 * n :]
    w_ref, even_ref, odd_ref, grad_ref, enc_ref, pre_ref, all_ref, *sent_refs = refs[:-4]
    rows_scr, y_scr, p_scr, edge_scr = refs[-4:]
    me = idx_ref[0]
    pick = lambda items: [items[j] for j in far]
    conv_rows(pick(offsets), me, pick(blocks), pick(pays), w_ref, rows_scr, y_scr)
    taps, width = w_ref.shape[0], w_ref.shape[2]
    half = even_ref.shape[0]
    step = min(64, half)
    length = 2 * half
    zero = jnp.zeros((EDGE, width), F32)
    pre_ref[0:EDGE, :] = zero
    pre_ref[EDGE + length : 2 * EDGE + length, :] = zero
    for start in range(0, half, step):
        rows = slice(start, start + step)
        for c in range(width // LANES):
            lanes = slice(c * LANES, (c + 1) * LANES)
            even = even_ref[rows, lanes] + tap_sum(y_scr, start, step, 0, taps, c)
            odd = odd_ref[rows, lanes] + tap_sum(y_scr, start, step, 1, taps, c)
            act_even, slope_even = gelu_parts(even)
            act_odd, slope_odd = gelu_parts(odd)
            enc_ref[rows, lanes] = (0.5 * (act_even + act_odd)).astype(BF16)
            spread = grad_ref[rows, lanes].astype(F32)
            p_scr[c, pl.ds(2 * start, step, stride=2), :] = slope_even * 0.5 * spread
            p_scr[c, pl.ds(2 * start + 1, step, stride=2), :] = slope_odd * 0.5 * spread
    for c in range(width // LANES):
        lanes = slice(c * LANES, (c + 1) * LANES)
        pre_ref[EDGE : EDGE + length, lanes] = p_scr[c].astype(BF16).astype(F32)
    depth = blocks[0].shape[0]
    for off, block, pay in zip(offsets, blocks, pays):
        rows = pl.ds(pl.multiple_of((me ^ off) * depth, 16), depth)
        all_ref[rows, 0:length] = block[...]
        all_ref[rows, length : length + LANES] = edge_block(pay, depth)
    if sent_refs:
        wanted = pl.ds(pl.multiple_of((1 - idx_ref[1]) * per * depth, 16), depth)
        rows = shifted_rows(pre_ref, edge_scr, (0,))
        sent_refs[0][...] = jnp.dot(all_ref[wanted, :], rows, preferred_element_type=F32).astype(BF16)


def shifted_rows(p_ref, edge_scr, group):
    length, width = p_ref.shape[0] - 2 * EDGE, p_ref.shape[1]
    edge_scr[...] = jnp.zeros_like(edge_scr)
    shifted = []
    for i, tap in enumerate(group):
        cols = slice(i * width, (i + 1) * width)
        edge_scr[0:2, cols] = p_ref[EDGE - tap : EDGE - tap + 2, :]
        edge_scr[2:4, cols] = p_ref[EDGE + length + 2 - tap : EDGE + length + 4 - tap, :]
        shifted.append(p_ref[EDGE + 2 - tap : EDGE + 2 - tap + length, :].astype(BF16))
    edge = edge_scr[:, 0 : len(group) * width].astype(BF16)
    return jnp.concatenate([jnp.concatenate(shifted, axis=1), edge], axis=0)


def grad_kernel(group, depth, per, pieces, idx_ref, all_ref, p_ref, *refs):
    out_refs, edge_scr = list(refs[:-1]), refs[-1]
    width = p_ref.shape[1]
    half = per * depth
    for first in range(0, len(group), 2):
        some = group[first : first + 2]
        rows = shifted_rows(p_ref, edge_scr, some)
        res = jnp.dot(all_ref[...], rows, preferred_element_type=F32).astype(BF16)
        for i in range(len(some)):
            part = res[:, i * width : (i + 1) * width]
            own_ref = out_refs.pop(0)
            if not per:
                own_ref[...] = part
                continue
            lower = idx_ref[1] == 0
            own_ref[...] = jnp.where(lower, part[0:half], part[half : 2 * half])
            other = jnp.where(lower, part[half : 2 * half], part[0:half])
            named = pieces[first + i]
            if not named:
                out_refs.pop(0)[...] = other
            for r in named:
                out_refs.pop(0)[...] = other[r * depth : (r + 1) * depth]


def qkv_kernel(offsets, idx_ref, *refs):
    n = len(offsets)
    enc_refs, gain_refs, (w_ref, out_ref) = refs[:n], refs[n : 2 * n], refs[2 * n :]
    depth = enc_refs[0].shape[1]
    values = [ref[...].astype(F32) for ref in enc_refs]
    channels = n * depth
    sums = sum(jnp.sum(v, axis=1, keepdims=True) for v in values)
    squares = sum(jnp.sum(v * v, axis=1, keepdims=True) for v in values)
    mean = sums / channels
    var = squares / channels - mean * mean
    scale = lax.rsqrt(var + 1e-05)
    total = None
    for off, v, gain_ref in zip(offsets, values, gain_refs):
        normal = ((v - mean) * scale * gain_ref[4:5, 0:depth]).astype(BF16)
        w = w_ref[pl.ds(pl.multiple_of((idx_ref[0] ^ off) * depth, 16), depth), :]
        part = jnp.dot(normal, w, preferred_element_type=F32)
        total = part if total is None else total + part
    out_ref[...] = total.astype(BF16)


def call(kernel, out, scratch, mib, idx, *arrays):
    vmem = pl.BlockSpec(memory_space=pltpu.VMEM)
    return pl.pallas_call(
        kernel,
        out_shape=out,
        in_specs=[pl.BlockSpec(memory_space=pltpu.SMEM)] + [vmem] * len(arrays),
        out_specs=jax.tree.map(lambda _: vmem, out),
        scratch_shapes=scratch,
        compiler_params=pltpu.CompilerParams(vmem_limit_bytes=mib * 1024 * 1024),
    )(idx, *arrays)


def after(value, *others):
    return lax.optimization_barrier((value, *others))[0]


def write_kernel(end_ref, *refs):
    *part_refs, out_ref = refs
    count = len(part_refs) // 2
    pieces = count // out_ref.shape[0]
    rows = part_refs[0].shape[0]
    for i in range(count):
        tap, r = i // pieces, i % pieces
        for ref, here in ((part_refs[2 * i], end_ref[0] > 0), (part_refs[2 * i + 1], end_ref[0] == 0)):

            @pl.when(here)
            def _(ref=ref, tap=tap, r=r):
                out_ref[tap, r * rows : (r + 1) * rows, :] = ref[...].astype(F32)


def written(parts, taps, at, buffer, shape):
    me = lax.axis_index("dp")
    end = jnp.logical_or(me == 0, me == lax.axis_size("dp") - 1).astype(jnp.int32).reshape(1)
    parts = [v for pair in parts for v in pair]
    rows, width = parts[0].shape
    extra = [] if buffer is None else [buffer]
    kernel = write_kernel if buffer is None else lambda end, b, *refs: write_kernel(end, *refs)
    return pl.pallas_call(
        kernel,
        out_shape=jax.ShapeDtypeStruct(shape, F32),
        grid=(1,),
        in_specs=[pl.BlockSpec(memory_space=pltpu.SMEM)]
        + [pl.BlockSpec(memory_space=pl.ANY)] * len(extra)
        + [pl.BlockSpec((rows, width), lambda i: (0, 0))] * len(parts),
        out_specs=pl.BlockSpec((taps, shape[1], width), lambda i: (at // taps, 0, 0)),
        input_output_aliases={1: 0} if extra else {},
        compiler_params=pltpu.CompilerParams(vmem_limit_bytes=12 * 1024 * 1024),
    )(end, *extra, *parts)


def edge_kernel(head_ref, tail_ref, out_ref):
    depth = head_ref.shape[0]
    extra = jnp.zeros((out_ref.shape[1] - depth, LANES), F32)
    head = jnp.concatenate([head_ref[...].astype(F32), extra], axis=0).T
    tail = jnp.concatenate([tail_ref[...].astype(F32), extra], axis=0).T
    out_ref[...] = jnp.zeros_like(out_ref)
    out_ref[0:2, :] = head[0:2]
    out_ref[2:4, :] = tail[LANES - 2 : LANES]


def edge_rows(x, width):
    peers = lax.axis_size("seq")
    me = lax.axis_index("seq")
    depth, length = x.shape
    ends = pl.pallas_call(
        edge_kernel,
        out_shape=jax.ShapeDtypeStruct((8, width), F32),
        grid=(1,),
        in_specs=[
            pl.BlockSpec((depth, LANES), lambda i: (0, 0)),
            pl.BlockSpec((depth, LANES), lambda i: (0, length // LANES - 1)),
        ],
        out_specs=pl.BlockSpec((8, width), lambda i: (0, 0)),
        compiler_params=pltpu.CompilerParams(vmem_limit_bytes=2 * 1024 * 1024),
    )(x, x)
    if peers == 2:
        before = behind = swap(ends, "seq", 1)
    else:
        up = [(i, (i + 1) % peers) for i in range(peers - 1)]
        down = [(j, i) for i, j in up]
        before, behind = lax.ppermute(ends, "seq", up), lax.ppermute(ends, "seq", down)
    before = jnp.where(me == 0, 0.0, before[2:4])
    behind = jnp.where(me == peers - 1, 0.0, behind[0:2])
    return jnp.concatenate([before, behind], axis=0)


def added(a, b):
    return (a.astype(F32) + b.astype(F32)).astype(BF16)


def chain_sums(count, part, sent, idle):
    me = lax.axis_index("dp")
    end = jnp.logical_or(me == 0, me == 3)
    outer_pairs = [(0, 1), (1, 0), (2, 3), (3, 2)]
    middle_pairs = [(1, 2), (2, 1)]
    last = None
    h, p, s, outer, middle, sums = {}, {}, {}, {}, {}, {}
    for r in range(count + 5):
        if r < count:
            h[r] = part(r, last)
        if r < count + 3:
            value = h.get(r, s.get(r - 3))
            if r in h and r - 3 in s:
                value = jnp.where(end, h[r], s[r - 3])
            last = value = lax.optimization_barrier(value)
            outer[r] = lax.ppermute(value, "dp", outer_pairs)
            last = sent(r, last, sums)
        if r - 1 in outer:
            got = after(outer.pop(r - 1), last)
            if r - 1 < count:
                last = p[r - 1] = lax.optimization_barrier(added(h[r - 1], got))
                middle[r - 1] = lax.ppermute(last, "dp", middle_pairs)
            if r >= 4:
                sums[r - 4] = (got, s[r - 4])
                if r - 1 >= count:
                    last = got
            last = idle(r - 1, last, sums)
        if r - 2 in middle:
            got = after(middle.pop(r - 2), last)
            last = s[r - 2] = lax.optimization_barrier(added(p[r - 2], got))
    return [sums[c] for c in range(count)]


def on_device(block_input, conv_weight, norm_gain, qkv_weight, encoder_grad):
    x = jnp.swapaxes(block_input[0], 0, 1)
    depth, length = x.shape
    taps, _, width = conv_weight.shape
    peers, shards = lax.axis_size("mp"), lax.axis_size("seq")
    bits = [1 << b for b in reversed(range(peers.bit_length() - 1))]
    idx = jnp.stack([lax.axis_index("mp"), lax.axis_index("seq")]).astype(jnp.int32)

    offsets = [0]
    for bit in bits:
        offsets = offsets + [o ^ bit for o in offsets]
    near = [j for j, o in enumerate(offsets) if o < 2]
    far = [j for j, o in enumerate(offsets) if o >= 2]
    half = length // 2
    pick = lambda items, at: [items[j] for j in at]
    scratch = lambda at: [
        pltpu.VMEM((length + 16, len(at) * depth), BF16),
        pltpu.VMEM((taps * width // LANES, length + 2 * EDGE, LANES), F32),
    ]

    blocks = [x]
    for bit in bits[:-1]:
        blocks = blocks + [swap(b, "mp", bit) for b in blocks]
    own = swap(x, "mp", bits[-1])
    edges = edge_rows(x, width)
    payload = jnp.concatenate([edges, norm_gain.reshape(1, -1), jnp.zeros((3, width), F32)], axis=0)
    payloads = [payload] + [swap(payload, "mp", o) for o in offsets[1:]]

    part = jax.ShapeDtypeStruct((half, width), F32)
    even, odd = call(
        functools.partial(first_kernel, pick(offsets, near)),
        (part, part),
        scratch(near),
        14,
        idx, x, own, *pick(payloads, near), conv_weight,
    )
    hold = [even] + pick(payloads, far)
    blocks = blocks + [own] + [swap(after(b, *hold), "mp", bits[-1]) for b in blocks[1:]]
    pair = shards == 2 and peers % shards == 0 and lax.axis_size("dp") == 4
    per = peers // shards if pair else 0
    piece = jax.ShapeDtypeStruct((depth, width), BF16)
    encoded, pre_grad, joined, *first = call(
        functools.partial(second_kernel, offsets, far, per),
        (
            jax.ShapeDtypeStruct((half, width), BF16),
            jax.ShapeDtypeStruct((length + 2 * EDGE, width), F32),
            jax.ShapeDtypeStruct((peers * depth, length + LANES), BF16),
            *([piece] if pair else []),
        ),
        scratch(far)
        + [
            pltpu.VMEM((width // LANES, length, LANES), F32),
            pltpu.VMEM((LANES, width), F32),
        ],
        16,
        idx, *blocks, *payloads, conv_weight, even, odd, encoder_grad[0],
    )
    encs = [encoded]
    for bit in bits[:-1]:
        encs = encs + [swap(e, "mp", bit) for e in encs]

    everything = tuple(range(per))
    pieces_of = lambda k: everything[1:] if k == 0 else (everything if k == 1 else ())

    def gradient(group, hold):
        pieces = [pieces_of(k) for k in group]
        outs = []
        for q in pieces:
            if not pair:
                outs.append([jax.ShapeDtypeStruct((peers * depth, width), BF16)])
                continue
            whole = jax.ShapeDtypeStruct((per * depth, width), BF16)
            outs.append([whole] + ([piece] * len(q) if q else [whole]))
        flat = call(
            functools.partial(grad_kernel, group, depth, per, pieces),
            tuple(o for tap in outs for o in tap),
            [pltpu.VMEM((LANES, width * min(len(group), 2)), F32)],
            24 if len(group) > 2 else 8,
            after(idx, *hold) if hold else idx, joined, pre_grad,
        )
        flat = list(flat)
        taken = [[flat.pop(0) for _ in tap] for tap in outs]
        return [t[0] for t in taken], [t[1:] for t in taken]

    qkv_call = lambda idx, encs: call(
        functools.partial(qkv_kernel, offsets),
        jax.ShapeDtypeStruct((half, qkv_weight.shape[1]), BF16),
        [],
        5,
        idx, *encs, *payloads, qkv_weight,
    )
    if not pair:
        sums = [gradient((k,), [])[0][0] for k in range(taps)]
        sums = [lax.psum_scatter(v, "seq", scatter_dimension=0, tiled=True) for v in sums]
        sums = [lax.psum(v, "dp").astype(F32) for v in sums]
        encs = encs + [swap(e, "mp", bits[-1]) for e in encs]
        return (qkv_call(idx, encs)[None], jnp.stack(sums, axis=1))

    chunks = taps * per
    keep, send, got, relays, done = [], [], {}, [], {}

    def work(group, hold):
        if not group:
            return
        mine, other = gradient(group, hold)
        keep.extend(mine)
        send.extend(other if send else [list(first) + other[0]] + other[1:])

    def launch(tap, hold):
        if tap < taps:
            got[tap] = [swap(after(v, *hold) if hold else v, "seq", 1) for v in send[tap]]

    work((0,), [])
    launch(0, [])
    work(tuple(range(1, min(3, taps))), [keep[-1]])
    launch(1, [])

    def share(c, last):
        tap, row = c // per, c % per
        rows = slice(row * depth, (row + 1) * depth)
        value = got[tap][row] if len(got[tap]) > 1 else got[tap][0][rows]
        return added(keep[tap][rows], value if last is None else after(value, last))

    starts = {(k - 1) * per - 1 - (k == 3): k for k in range(2, taps)}

    def sent(r, last, sums):
        if r < chunks and r in starts:
            launch(starts[r], [last])
        if r == chunks + 2:
            early = len(sums) // per
            parts = [sums[i] for i in range(early * per)]
            parts[0] = (after(parts[0][0], last), parts[0][1])
            last = done["early"] = written(parts, early, 0, None, (taps, per * depth, width))
            done["at"] = early
        return last

    def idle(c, last, sums):
        if c == per + 4:
            held = encs[1:]
            relays.extend([swap(after(e, last, *held), "mp", bits[-1]) for e in encs])
        if c == 0:
            work(tuple(range(3, taps)), [last] + encs[1:])
            last = keep[-1]
        if c == chunks:
            last = done["qkv"] = qkv_call(after(idx, last, *relays), encs + relays)
        return last

    sums = chain_sums(chunks, share, sent, idle)
    shape = (taps, per * depth, width)
    conv_grad, early = done["early"], done["at"]
    for k in range(early, taps):
        conv_grad = written(sums[k * per : (k + 1) * per], 1, k, conv_grad, shape)
    return (done["qkv"][None], jnp.swapaxes(conv_grad, 0, 1))


def solution(mesh):
    return jax.shard_map(
        on_device,
        mesh=mesh,
        in_specs=(
            P("dp", "seq", "mp"),
            P(None, None, "mp"),
            P("mp"),
            P(None, "mp"),
            P("dp", "seq", "mp"),
        ),
        out_specs=(P("dp", "seq", "mp"), P("seq", None, "mp")),
        check_vma=False,
    )
```

```python
import functools

import jax
import jax.numpy as jnp
from jax import lax
from jax.experimental import pallas as pl
from jax.experimental.pallas import tpu as pltpu
from jax.sharding import PartitionSpec as P

EDGE = 8
LANES = 128
F32 = jnp.float32
BF16 = jnp.bfloat16


def gelu_parts(v):
    u = 0.7978845608 * (v + 0.044715 * v * v * v)
    th = jnp.tanh(u)
    value = 0.5 * v * (1.0 + th)
    slope = 0.5 * (1.0 + th) + 0.5 * v * (1.0 - th * th) * 0.7978845608 * (1.0 + 0.134145 * v * v)
    return value, slope


def swap(value, axis, bit):
    peers = lax.axis_size(axis)
    return lax.ppermute(value, axis, [(i, i ^ bit) for i in range(peers)])


def edge_block(ref, depth):
    rows = jnp.concatenate([ref[0:8, :], jnp.zeros((LANES - 8, ref.shape[1]), F32)], axis=0)
    keep = lax.broadcasted_iota(jnp.int32, rows.shape, 0) < 4
    return jnp.where(keep, rows, 0.0).T[0:depth, :].astype(BF16)


def conv_rows(offsets, me, x_refs, halo_refs, w_ref, rows_scr, y_scr):
    taps, width = w_ref.shape[0], w_ref.shape[2]
    length = x_refs[0].shape[1]
    x = jnp.concatenate([ref[...] for ref in x_refs], axis=0)
    depth = x.shape[0] // len(offsets)
    halo = jnp.concatenate([edge_block(ref, depth) for ref in halo_refs], axis=0)
    rows_scr[0:length, :] = x.T
    rows_scr[length : length + 16, :] = halo.T[0:16]
    starts = [pl.multiple_of((me ^ off) * depth, 16) for off in offsets]
    for first in range(0, taps, 2):
        group = range(first, min(first + 2, taps))
        w = jnp.concatenate(
            [
                jnp.concatenate([w_ref[k, pl.ds(s, depth), :] for s in starts], axis=0)
                for k in group
            ],
            axis=1,
        )
        y = jnp.dot(rows_scr[...], w, preferred_element_type=F32)
        for c in range(w.shape[1] // LANES):
            part = y[:, c * LANES : (c + 1) * LANES]
            at = first * width // LANES + c
            y_scr[at, EDGE : EDGE + length, :] = part[0:length]
            y_scr[at, EDGE - 2 : EDGE, :] = part[length : length + 2]
            y_scr[at, EDGE + length : EDGE + length + 2, :] = part[length + 2 : length + 4]


def tap_sum(y_scr, start, count, phase, taps, c):
    total = None
    for k in range(taps):
        at = k * (y_scr.shape[0] // taps) + c
        part = y_scr[at, pl.ds(EDGE + 2 * start + phase + k - 2, count, stride=2), :]
        total = part if total is None else total + part
    return total


def first_kernel(offsets, idx_ref, *refs):
    n = len(offsets)
    *x_refs, w_ref, even_ref, odd_ref, rows_scr, y_scr = refs
    x_refs, halo_refs = x_refs[:-n], x_refs[-n:]
    conv_rows(offsets, idx_ref[0], x_refs, halo_refs, w_ref, rows_scr, y_scr)
    taps, width = w_ref.shape[0], w_ref.shape[2]
    half = even_ref.shape[0]
    step = min(64, half)
    for start in range(0, half, step):
        rows = slice(start, start + step)
        for c in range(width // LANES):
            lanes = slice(c * LANES, (c + 1) * LANES)
            even_ref[rows, lanes] = tap_sum(y_scr, start, step, 0, taps, c)
            odd_ref[rows, lanes] = tap_sum(y_scr, start, step, 1, taps, c)


def second_kernel(offsets, far, per, idx_ref, *refs):
    n = len(offsets)
    blocks, pays, refs = refs[:n], refs[n : 2 * n], refs[2 * n :]
    w_ref, even_ref, odd_ref, grad_ref, enc_ref, pre_ref, all_ref, *sent_refs = refs[:-4]
    rows_scr, y_scr, p_scr, edge_scr = refs[-4:]
    me = idx_ref[0]
    pick = lambda items: [items[j] for j in far]
    conv_rows(pick(offsets), me, pick(blocks), pick(pays), w_ref, rows_scr, y_scr)
    taps, width = w_ref.shape[0], w_ref.shape[2]
    half = even_ref.shape[0]
    step = min(64, half)
    length = 2 * half
    zero = jnp.zeros((EDGE, width), F32)
    pre_ref[0:EDGE, :] = zero
    pre_ref[EDGE + length : 2 * EDGE + length, :] = zero
    for start in range(0, half, step):
        rows = slice(start, start + step)
        for c in range(width // LANES):
            lanes = slice(c * LANES, (c + 1) * LANES)
            even = even_ref[rows, lanes] + tap_sum(y_scr, start, step, 0, taps, c)
            odd = odd_ref[rows, lanes] + tap_sum(y_scr, start, step, 1, taps, c)
            act_even, slope_even = gelu_parts(even)
            act_odd, slope_odd = gelu_parts(odd)
            enc_ref[rows, lanes] = (0.5 * (act_even + act_odd)).astype(BF16)
            spread = grad_ref[rows, lanes].astype(F32)
            p_scr[c, pl.ds(2 * start, step, stride=2), :] = slope_even * 0.5 * spread
            p_scr[c, pl.ds(2 * start + 1, step, stride=2), :] = slope_odd * 0.5 * spread
    for c in range(width // LANES):
        lanes = slice(c * LANES, (c + 1) * LANES)
        pre_ref[EDGE : EDGE + length, lanes] = p_scr[c].astype(BF16).astype(F32)
    depth = blocks[0].shape[0]
    for off, block, pay in zip(offsets, blocks, pays):
        rows = pl.ds(pl.multiple_of((me ^ off) * depth, 16), depth)
        all_ref[rows, 0:length] = block[...]
        all_ref[rows, length : length + LANES] = edge_block(pay, depth)
    if sent_refs:
        wanted = pl.ds(pl.multiple_of((1 - idx_ref[1]) * per * depth, 16), depth)
        rows = shifted_rows(pre_ref, edge_scr, (0,))
        sent_refs[0][...] = jnp.dot(all_ref[wanted, :], rows, preferred_element_type=F32).astype(BF16)


def shifted_rows(p_ref, edge_scr, group):
    length, width = p_ref.shape[0] - 2 * EDGE, p_ref.shape[1]
    edge_scr[...] = jnp.zeros_like(edge_scr)
    shifted = []
    for i, tap in enumerate(group):
        cols = slice(i * width, (i + 1) * width)
        edge_scr[0:2, cols] = p_ref[EDGE - tap : EDGE - tap + 2, :]
        edge_scr[2:4, cols] = p_ref[EDGE + length + 2 - tap : EDGE + length + 4 - tap, :]
        shifted.append(p_ref[EDGE + 2 - tap : EDGE + 2 - tap + length, :].astype(BF16))
    edge = edge_scr[:, 0 : len(group) * width].astype(BF16)
    return jnp.concatenate([jnp.concatenate(shifted, axis=1), edge], axis=0)


def grad_kernel(group, depth, per, pieces, idx_ref, all_ref, p_ref, *refs):
    out_refs, edge_scr = list(refs[:-1]), refs[-1]
    width = p_ref.shape[1]
    half = per * depth
    for first in range(0, len(group), 2):
        some = group[first : first + 2]
        rows = shifted_rows(p_ref, edge_scr, some)
        res = jnp.dot(all_ref[...], rows, preferred_element_type=F32).astype(BF16)
        for i in range(len(some)):
            part = res[:, i * width : (i + 1) * width]
            own_ref = out_refs.pop(0)
            if not per:
                own_ref[...] = part
                continue
            lower = idx_ref[1] == 0
            own_ref[...] = jnp.where(lower, part[0:half], part[half : 2 * half])
            other = jnp.where(lower, part[half : 2 * half], part[0:half])
            named = pieces[first + i]
            if not named:
                out_refs.pop(0)[...] = other
            for r in named:
                out_refs.pop(0)[...] = other[r * depth : (r + 1) * depth]


def qkv_kernel(offsets, idx_ref, *refs):
    n = len(offsets)
    enc_refs, gain_refs, (w_ref, out_ref) = refs[:n], refs[n : 2 * n], refs[2 * n :]
    depth = enc_refs[0].shape[1]
    values = [ref[...].astype(F32) for ref in enc_refs]
    channels = n * depth
    sums = sum(jnp.sum(v, axis=1, keepdims=True) for v in values)
    squares = sum(jnp.sum(v * v, axis=1, keepdims=True) for v in values)
    mean = sums / channels
    var = squares / channels - mean * mean
    scale = lax.rsqrt(var + 1e-05)
    total = None
    for off, v, gain_ref in zip(offsets, values, gain_refs):
        normal = ((v - mean) * scale * gain_ref[4:5, 0:depth]).astype(BF16)
        w = w_ref[pl.ds(pl.multiple_of((idx_ref[0] ^ off) * depth, 16), depth), :]
        part = jnp.dot(normal, w, preferred_element_type=F32)
        total = part if total is None else total + part
    out_ref[...] = total.astype(BF16)


def call(kernel, out, scratch, mib, idx, *arrays):
    vmem = pl.BlockSpec(memory_space=pltpu.VMEM)
    return pl.pallas_call(
        kernel,
        out_shape=out,
        in_specs=[pl.BlockSpec(memory_space=pltpu.SMEM)] + [vmem] * len(arrays),
        out_specs=jax.tree.map(lambda _: vmem, out),
        scratch_shapes=scratch,
        compiler_params=pltpu.CompilerParams(vmem_limit_bytes=mib * 1024 * 1024),
    )(idx, *arrays)


def after(value, *others):
    return lax.optimization_barrier((value, *others))[0]


def write_kernel(each, end_ref, *refs):
    *part_refs, out_ref = refs
    count = len(part_refs) // each
    pieces = count // out_ref.shape[0]
    rows = part_refs[0].shape[0]
    for i in range(count):
        tap, r = i // pieces, i % pieces
        if each == 1:
            out_ref[tap, r * rows : (r + 1) * rows, :] = part_refs[i][...].astype(F32)
            continue
        for ref, here in ((part_refs[2 * i], end_ref[0] > 0), (part_refs[2 * i + 1], end_ref[0] == 0)):

            @pl.when(here)
            def _(ref=ref, tap=tap, r=r):
                out_ref[tap, r * rows : (r + 1) * rows, :] = ref[...].astype(F32)


def written(parts, taps, at, buffer, shape):
    me = lax.axis_index("dp")
    end = jnp.logical_or(me == 0, me == lax.axis_size("dp") - 1).astype(jnp.int32).reshape(1)
    each = len(parts[0])
    parts = [v for part in parts for v in part]
    rows, width = parts[0].shape
    extra = [] if buffer is None else [buffer]
    kernel = functools.partial(write_kernel, each)
    if buffer is not None:
        kernel = lambda end, b, *refs: write_kernel(each, end, *refs)
    return pl.pallas_call(
        kernel,
        out_shape=jax.ShapeDtypeStruct(shape, F32),
        grid=(1,),
        in_specs=[pl.BlockSpec(memory_space=pltpu.SMEM)]
        + [pl.BlockSpec(memory_space=pl.ANY)] * len(extra)
        + [pl.BlockSpec((rows, width), lambda i: (0, 0))] * len(parts),
        out_specs=pl.BlockSpec((taps, shape[1], width), lambda i: (at // taps, 0, 0)),
        input_output_aliases={1: 0} if extra else {},
        compiler_params=pltpu.CompilerParams(vmem_limit_bytes=16 * 1024 * 1024),
    )(end, *extra, *parts)


def edge_kernel(head_ref, tail_ref, out_ref):
    depth = head_ref.shape[0]
    extra = jnp.zeros((out_ref.shape[1] - depth, LANES), F32)
    head = jnp.concatenate([head_ref[...].astype(F32), extra], axis=0).T
    tail = jnp.concatenate([tail_ref[...].astype(F32), extra], axis=0).T
    out_ref[...] = jnp.zeros_like(out_ref)
    out_ref[0:2, :] = head[0:2]
    out_ref[2:4, :] = tail[LANES - 2 : LANES]


def edge_rows(x, width):
    peers = lax.axis_size("seq")
    me = lax.axis_index("seq")
    depth, length = x.shape
    ends = pl.pallas_call(
        edge_kernel,
        out_shape=jax.ShapeDtypeStruct((8, width), F32),
        grid=(1,),
        in_specs=[
            pl.BlockSpec((depth, LANES), lambda i: (0, 0)),
            pl.BlockSpec((depth, LANES), lambda i: (0, length // LANES - 1)),
        ],
        out_specs=pl.BlockSpec((8, width), lambda i: (0, 0)),
        compiler_params=pltpu.CompilerParams(vmem_limit_bytes=2 * 1024 * 1024),
    )(x, x)
    if peers == 2:
        before = behind = swap(ends, "seq", 1)
    else:
        up = [(i, (i + 1) % peers) for i in range(peers - 1)]
        down = [(j, i) for i, j in up]
        before, behind = lax.ppermute(ends, "seq", up), lax.ppermute(ends, "seq", down)
    before = jnp.where(me == 0, 0.0, before[2:4])
    behind = jnp.where(me == peers - 1, 0.0, behind[0:2])
    return jnp.concatenate([before, behind], axis=0)


def added(a, b):
    return (a.astype(F32) + b.astype(F32)).astype(BF16)


def chain_sums(count, part, sent, idle):
    me = lax.axis_index("dp")
    end = jnp.logical_or(me == 0, me == 3)
    outer_pairs = [(0, 1), (1, 0), (2, 3), (3, 2)]
    middle_pairs = [(1, 2), (2, 1)]
    last = None
    h, p, s, outer, middle, sums = {}, {}, {}, {}, {}, {}
    for r in range(count + 5):
        if r < count:
            h[r] = part(r, last)
        if r < count + 3:
            value = h.get(r, s.get(r - 3))
            if r in h and r - 3 in s:
                value = jnp.where(end, h[r], s[r - 3])
            last = value = lax.optimization_barrier(value)
            outer[r] = lax.ppermute(value, "dp", outer_pairs)
            last = sent(r, last, sums)
        if r - 1 in outer:
            got = after(outer.pop(r - 1), last)
            if r - 1 < count:
                last = p[r - 1] = lax.optimization_barrier(added(h[r - 1], got))
                middle[r - 1] = lax.ppermute(last, "dp", middle_pairs)
            if r >= 4:
                sums[r - 4] = (got, s[r - 4])
                if r - 1 >= count:
                    last = got
            last = idle(r - 1, last, sums)
        if r - 2 in middle:
            got = after(middle.pop(r - 2), last)
            last = s[r - 2] = lax.optimization_barrier(added(p[r - 2], got))
    return [sums[c] for c in range(count)]


def on_device(block_input, conv_weight, norm_gain, qkv_weight, encoder_grad):
    x = jnp.swapaxes(block_input[0], 0, 1)
    depth, length = x.shape
    taps, _, width = conv_weight.shape
    peers, shards = lax.axis_size("mp"), lax.axis_size("seq")
    bits = [1 << b for b in reversed(range(peers.bit_length() - 1))]
    idx = jnp.stack([lax.axis_index("mp"), lax.axis_index("seq")]).astype(jnp.int32)

    offsets = [0]
    for bit in bits:
        offsets = offsets + [o ^ bit for o in offsets]
    near = [j for j, o in enumerate(offsets) if o < 2]
    far = [j for j, o in enumerate(offsets) if o >= 2]
    half = length // 2
    pick = lambda items, at: [items[j] for j in at]
    scratch = lambda at: [
        pltpu.VMEM((length + 16, len(at) * depth), BF16),
        pltpu.VMEM((taps * width // LANES, length + 2 * EDGE, LANES), F32),
    ]

    blocks = [x]
    for bit in bits[:-1]:
        blocks = blocks + [swap(b, "mp", bit) for b in blocks]
    own = swap(x, "mp", bits[-1])
    edges = edge_rows(x, width)
    payload = jnp.concatenate([edges, norm_gain.reshape(1, -1), jnp.zeros((3, width), F32)], axis=0)
    payloads = [payload] + [swap(payload, "mp", o) for o in offsets[1:]]

    part = jax.ShapeDtypeStruct((half, width), F32)
    even, odd = call(
        functools.partial(first_kernel, pick(offsets, near)),
        (part, part),
        scratch(near),
        24,
        idx, x, own, *pick(payloads, near), conv_weight,
    )
    hold = [even] + pick(payloads, far)
    blocks = blocks + [own] + [swap(after(b, *hold), "mp", bits[-1]) for b in blocks[1:]]
    pair = shards == 2 and peers % shards == 0 and lax.axis_size("dp") == 4
    per = peers // shards if pair else 0
    piece = jax.ShapeDtypeStruct((depth, width), BF16)
    encoded, pre_grad, joined, *first = call(
        functools.partial(second_kernel, offsets, far, per),
        (
            jax.ShapeDtypeStruct((half, width), BF16),
            jax.ShapeDtypeStruct((length + 2 * EDGE, width), F32),
            jax.ShapeDtypeStruct((peers * depth, length + LANES), BF16),
            *([piece] if pair else []),
        ),
        scratch(far)
        + [
            pltpu.VMEM((width // LANES, length, LANES), F32),
            pltpu.VMEM((LANES, width), F32),
        ],
        26,
        idx, *blocks, *payloads, conv_weight, even, odd, encoder_grad[0],
    )
    encs = [encoded]
    for bit in bits[:-1]:
        encs = encs + [swap(e, "mp", bit) for e in encs]

    everything = tuple(range(per))
    pieces_of = lambda k: everything[1:] if k == 0 else (everything if k == 1 else ())

    def gradient(group, hold):
        pieces = [pieces_of(k) for k in group]
        outs = []
        for q in pieces:
            if not pair:
                outs.append([jax.ShapeDtypeStruct((peers * depth, width), BF16)])
                continue
            whole = jax.ShapeDtypeStruct((per * depth, width), BF16)
            outs.append([whole] + ([piece] * len(q) if q else [whole]))
        flat = call(
            functools.partial(grad_kernel, group, depth, per, pieces),
            tuple(o for tap in outs for o in tap),
            [pltpu.VMEM((LANES, width * min(len(group), 2)), F32)],
            24 if len(group) > 2 else 16,
            after(idx, *hold) if hold else idx, joined, pre_grad,
        )
        flat = list(flat)
        taken = [[flat.pop(0) for _ in tap] for tap in outs]
        return [t[0] for t in taken], [t[1:] for t in taken]

    qkv_call = lambda idx, encs: call(
        functools.partial(qkv_kernel, offsets),
        jax.ShapeDtypeStruct((half, qkv_weight.shape[1]), BF16),
        [],
        8,
        idx, *encs, *payloads, qkv_weight,
    )
    if not pair:
        sums = [gradient((k,), [])[0][0] for k in range(taps)]
        sums = [lax.psum_scatter(v, "seq", scatter_dimension=0, tiled=True) for v in sums]
        sums = [lax.psum(v, "dp").astype(F32) for v in sums]
        encs = encs + [swap(e, "mp", bits[-1]) for e in encs]
        return (qkv_call(idx, encs)[None], jnp.stack(sums, axis=1))

    chunks = taps * per
    keep, send, got, relays, done = [], [], {}, [], {}

    def work(group, hold):
        if not group:
            return
        mine, other = gradient(group, hold)
        keep.extend(mine)
        send.extend(other if send else [list(first) + other[0]] + other[1:])

    def launch(tap, hold):
        if tap < taps:
            got[tap] = [swap(after(v, *hold) if hold else v, "seq", 1) for v in send[tap]]

    work((0,), [])
    launch(0, [])
    work(tuple(range(1, min(3, taps))), [keep[-1]])
    launch(1, [])

    def share(c, last):
        tap, row = c // per, c % per
        rows = slice(row * depth, (row + 1) * depth)
        value = got[tap][row] if len(got[tap]) > 1 else got[tap][0][rows]
        return added(keep[tap][rows], value if last is None else after(value, last))

    starts = {(k - 1) * per - 1 - (k == 3): k for k in range(2, taps)}

    def sent(r, last, sums):
        if r < chunks and r in starts:
            launch(starts[r], [last])
        if r == chunks + 2:
            early = len(sums) // per
            parts = [sums[i] for i in range(early * per)]
            parts[0] = (after(parts[0][0], last), parts[0][1])
            last = done["early"] = written(parts, early, 0, None, (taps, per * depth, width))
            done["at"] = early
        return last

    def idle(c, last, sums):
        if c == per + 4:
            held = encs[1:]
            relays.extend([swap(after(e, last, *held), "mp", bits[-1]) for e in encs])
        if c == 0:
            work(tuple(range(3, taps)), [last] + encs[1:])
            last = keep[-1]
        if c == chunks:
            last = done["qkv"] = qkv_call(after(idx, last, *relays), encs + relays)
        return last

    sums = chain_sums(chunks, share, sent, idle)
    shape = (taps, per * depth, width)
    conv_grad, early = done["early"], done["at"]
    me = lax.axis_index("dp")
    end = jnp.logical_or(me == 0, me == lax.axis_size("dp") - 1)
    for k in range(early, taps):
        parts = [(jnp.where(end, got, own),) for got, own in sums[k * per : (k + 1) * per]]
        conv_grad = written(parts, 1, k, conv_grad, shape)
    return (done["qkv"][None], jnp.swapaxes(conv_grad, 0, 1))


def solution(mesh):
    return jax.shard_map(
        on_device,
        mesh=mesh,
        in_specs=(
            P("dp", "seq", "mp"),
            P(None, None, "mp"),
            P("mp"),
            P(None, "mp"),
            P("dp", "seq", "mp"),
        ),
        out_specs=(P("dp", "seq", "mp"), P("seq", None, "mp")),
        check_vma=False,
    )
```

```python
import functools

import jax
import jax.numpy as jnp
from jax import lax
from jax.experimental import pallas as pl
from jax.experimental.pallas import tpu as pltpu
from jax.sharding import PartitionSpec as P

EDGE = 8
LANES = 128
F32 = jnp.float32
BF16 = jnp.bfloat16


def gelu_parts(v):
    u = 0.7978845608 * (v + 0.044715 * v * v * v)
    th = jnp.tanh(u)
    value = 0.5 * v * (1.0 + th)
    slope = 0.5 * (1.0 + th) + 0.5 * v * (1.0 - th * th) * 0.7978845608 * (1.0 + 0.134145 * v * v)
    return value, slope


def swap(value, axis, bit):
    peers = lax.axis_size(axis)
    return lax.ppermute(value, axis, [(i, i ^ bit) for i in range(peers)])


def edge_block(ref, depth):
    rows = jnp.concatenate([ref[0:8, :], jnp.zeros((LANES - 8, ref.shape[1]), F32)], axis=0)
    keep = lax.broadcasted_iota(jnp.int32, rows.shape, 0) < 4
    return jnp.where(keep, rows, 0.0).T[0:depth, :].astype(BF16)


def conv_rows(offsets, me, x_refs, halo_refs, w_ref, rows_scr, y_scr):
    taps, width = w_ref.shape[0], w_ref.shape[2]
    length = x_refs[0].shape[1]
    x = jnp.concatenate([ref[...] for ref in x_refs], axis=0)
    depth = x.shape[0] // len(offsets)
    halo = jnp.concatenate([edge_block(ref, depth) for ref in halo_refs], axis=0)
    rows_scr[0:length, :] = x.T
    rows_scr[length : length + 16, :] = halo.T[0:16]
    starts = [pl.multiple_of((me ^ off) * depth, 16) for off in offsets]
    for first in range(0, taps, 2):
        group = range(first, min(first + 2, taps))
        w = jnp.concatenate(
            [
                jnp.concatenate([w_ref[k, pl.ds(s, depth), :] for s in starts], axis=0)
                for k in group
            ],
            axis=1,
        )
        y = jnp.dot(rows_scr[...], w, preferred_element_type=F32)
        for c in range(w.shape[1] // LANES):
            part = y[:, c * LANES : (c + 1) * LANES]
            at = first * width // LANES + c
            y_scr[at, EDGE : EDGE + length, :] = part[0:length]
            y_scr[at, EDGE - 2 : EDGE, :] = part[length : length + 2]
            y_scr[at, EDGE + length : EDGE + length + 2, :] = part[length + 2 : length + 4]


def tap_sum(y_scr, start, count, phase, taps, c):
    total = None
    for k in range(taps):
        at = k * (y_scr.shape[0] // taps) + c
        part = y_scr[at, pl.ds(EDGE + 2 * start + phase + k - 2, count, stride=2), :]
        total = part if total is None else total + part
    return total


def first_kernel(offsets, idx_ref, *refs):
    n = len(offsets)
    *x_refs, w_ref, even_ref, odd_ref, rows_scr, y_scr = refs
    x_refs, halo_refs = x_refs[:-n], x_refs[-n:]
    conv_rows(offsets, idx_ref[0], x_refs, halo_refs, w_ref, rows_scr, y_scr)
    taps, width = w_ref.shape[0], w_ref.shape[2]
    half = even_ref.shape[0]
    step = min(64, half)
    for start in range(0, half, step):
        rows = slice(start, start + step)
        for c in range(width // LANES):
            lanes = slice(c * LANES, (c + 1) * LANES)
            even_ref[rows, lanes] = tap_sum(y_scr, start, step, 0, taps, c)
            odd_ref[rows, lanes] = tap_sum(y_scr, start, step, 1, taps, c)


def second_kernel(offsets, far, per, idx_ref, *refs):
    n = len(offsets)
    blocks, pays, refs = refs[:n], refs[n : 2 * n], refs[2 * n :]
    w_ref, even_ref, odd_ref, grad_ref, enc_ref, pre_ref, all_ref, *sent_refs = refs[:-4]
    rows_scr, y_scr, p_scr, edge_scr = refs[-4:]
    me = idx_ref[0]
    pick = lambda items: [items[j] for j in far]
    conv_rows(pick(offsets), me, pick(blocks), pick(pays), w_ref, rows_scr, y_scr)
    taps, width = w_ref.shape[0], w_ref.shape[2]
    half = even_ref.shape[0]
    step = min(64, half)
    length = 2 * half
    zero = jnp.zeros((EDGE, width), F32)
    pre_ref[0:EDGE, :] = zero
    pre_ref[EDGE + length : 2 * EDGE + length, :] = zero
    for start in range(0, half, step):
        rows = slice(start, start + step)
        for c in range(width // LANES):
            lanes = slice(c * LANES, (c + 1) * LANES)
            even = even_ref[rows, lanes] + tap_sum(y_scr, start, step, 0, taps, c)
            odd = odd_ref[rows, lanes] + tap_sum(y_scr, start, step, 1, taps, c)
            act_even, slope_even = gelu_parts(even)
            act_odd, slope_odd = gelu_parts(odd)
            enc_ref[rows, lanes] = (0.5 * (act_even + act_odd)).astype(BF16)
            spread = grad_ref[rows, lanes].astype(F32)
            p_scr[c, pl.ds(2 * start, step, stride=2), :] = slope_even * 0.5 * spread
            p_scr[c, pl.ds(2 * start + 1, step, stride=2), :] = slope_odd * 0.5 * spread
    for c in range(width // LANES):
        lanes = slice(c * LANES, (c + 1) * LANES)
        pre_ref[EDGE : EDGE + length, lanes] = p_scr[c].astype(BF16).astype(F32)
    depth = blocks[0].shape[0]
    for off, block, pay in zip(offsets, blocks, pays):
        rows = pl.ds(pl.multiple_of((me ^ off) * depth, 16), depth)
        all_ref[rows, 0:length] = block[...]
        all_ref[rows, length : length + LANES] = edge_block(pay, depth)
    if sent_refs:
        wanted = pl.ds(pl.multiple_of((1 - idx_ref[1]) * per * depth, 16), depth)
        rows = shifted_rows(pre_ref, edge_scr, (0,))
        sent_refs[0][...] = jnp.dot(all_ref[wanted, :], rows, preferred_element_type=F32).astype(BF16)


def shifted_rows(p_ref, edge_scr, group):
    length, width = p_ref.shape[0] - 2 * EDGE, p_ref.shape[1]
    edge_scr[...] = jnp.zeros_like(edge_scr)
    shifted = []
    for i, tap in enumerate(group):
        cols = slice(i * width, (i + 1) * width)
        edge_scr[0:2, cols] = p_ref[EDGE - tap : EDGE - tap + 2, :]
        edge_scr[2:4, cols] = p_ref[EDGE + length + 2 - tap : EDGE + length + 4 - tap, :]
        shifted.append(p_ref[EDGE + 2 - tap : EDGE + 2 - tap + length, :].astype(BF16))
    edge = edge_scr[:, 0 : len(group) * width].astype(BF16)
    return jnp.concatenate([jnp.concatenate(shifted, axis=1), edge], axis=0)


def grad_kernel(group, depth, per, pieces, idx_ref, all_ref, p_ref, *refs):
    out_refs, edge_scr = list(refs[:-1]), refs[-1]
    width = p_ref.shape[1]
    half = per * depth
    for first in range(0, len(group), 2):
        some = group[first : first + 2]
        rows = shifted_rows(p_ref, edge_scr, some)
        res = jnp.dot(all_ref[...], rows, preferred_element_type=F32).astype(BF16)
        for i in range(len(some)):
            part = res[:, i * width : (i + 1) * width]
            own_ref = out_refs.pop(0)
            if not per:
                own_ref[...] = part
                continue
            lower = idx_ref[1] == 0
            own_ref[...] = jnp.where(lower, part[0:half], part[half : 2 * half])
            other = jnp.where(lower, part[half : 2 * half], part[0:half])
            named = pieces[first + i]
            if not named:
                out_refs.pop(0)[...] = other
            for r in named:
                out_refs.pop(0)[...] = other[r * depth : (r + 1) * depth]


def qkv_kernel(offsets, idx_ref, *refs):
    n = len(offsets)
    enc_refs, gain_refs, (w_ref, out_ref) = refs[:n], refs[n : 2 * n], refs[2 * n :]
    depth = enc_refs[0].shape[1]
    values = [ref[...].astype(F32) for ref in enc_refs]
    channels = n * depth
    sums = sum(jnp.sum(v, axis=1, keepdims=True) for v in values)
    squares = sum(jnp.sum(v * v, axis=1, keepdims=True) for v in values)
    mean = sums / channels
    var = squares / channels - mean * mean
    scale = lax.rsqrt(var + 1e-05)
    total = None
    for off, v, gain_ref in zip(offsets, values, gain_refs):
        normal = ((v - mean) * scale * gain_ref[4:5, 0:depth]).astype(BF16)
        w = w_ref[pl.ds(pl.multiple_of((idx_ref[0] ^ off) * depth, 16), depth), :]
        part = jnp.dot(normal, w, preferred_element_type=F32)
        total = part if total is None else total + part
    out_ref[...] = total.astype(BF16)


def call(kernel, out, scratch, mib, idx, *arrays):
    vmem = pl.BlockSpec(memory_space=pltpu.VMEM)
    return pl.pallas_call(
        kernel,
        out_shape=out,
        in_specs=[pl.BlockSpec(memory_space=pltpu.SMEM)] + [vmem] * len(arrays),
        out_specs=jax.tree.map(lambda _: vmem, out),
        scratch_shapes=scratch,
        compiler_params=pltpu.CompilerParams(vmem_limit_bytes=mib * 1024 * 1024),
    )(idx, *arrays)


def after(value, *others):
    return lax.optimization_barrier((value, *others))[0]


def write_kernel(each, end_ref, *refs):
    *part_refs, out_ref = refs
    count = len(part_refs) // each
    pieces = count // out_ref.shape[0]
    rows = part_refs[0].shape[0]
    for i in range(count):
        tap, r = i // pieces, i % pieces
        if each == 1:
            out_ref[tap, r * rows : (r + 1) * rows, :] = part_refs[i][...].astype(F32)
            continue
        for ref, here in ((part_refs[2 * i], end_ref[0] > 0), (part_refs[2 * i + 1], end_ref[0] == 0)):

            @pl.when(here)
            def _(ref=ref, tap=tap, r=r):
                out_ref[tap, r * rows : (r + 1) * rows, :] = ref[...].astype(F32)


def written(parts, taps, at, buffer, shape):
    me = lax.axis_index("dp")
    end = jnp.logical_or(me == 0, me == lax.axis_size("dp") - 1).astype(jnp.int32).reshape(1)
    each = len(parts[0])
    parts = [v for part in parts for v in part]
    rows, width = parts[0].shape
    extra = [] if buffer is None else [buffer]
    kernel = functools.partial(write_kernel, each)
    if buffer is not None:
        kernel = lambda end, b, *refs: write_kernel(each, end, *refs)
    return pl.pallas_call(
        kernel,
        out_shape=jax.ShapeDtypeStruct(shape, F32),
        grid=(1,),
        in_specs=[pl.BlockSpec(memory_space=pltpu.SMEM)]
        + [pl.BlockSpec(memory_space=pl.ANY)] * len(extra)
        + [pl.BlockSpec((rows, width), lambda i: (0, 0))] * len(parts),
        out_specs=pl.BlockSpec((taps, shape[1], width), lambda i: (at // taps, 0, 0)),
        input_output_aliases={1: 0} if extra else {},
        compiler_params=pltpu.CompilerParams(vmem_limit_bytes=16 * 1024 * 1024),
    )(end, *extra, *parts)


def edge_kernel(head_ref, tail_ref, out_ref):
    depth = head_ref.shape[0]
    extra = jnp.zeros((out_ref.shape[1] - depth, LANES), F32)
    head = jnp.concatenate([head_ref[...].astype(F32), extra], axis=0).T
    tail = jnp.concatenate([tail_ref[...].astype(F32), extra], axis=0).T
    out_ref[...] = jnp.zeros_like(out_ref)
    out_ref[0:2, :] = head[0:2]
    out_ref[2:4, :] = tail[LANES - 2 : LANES]


def edge_rows(x, width):
    peers = lax.axis_size("seq")
    me = lax.axis_index("seq")
    depth, length = x.shape
    ends = pl.pallas_call(
        edge_kernel,
        out_shape=jax.ShapeDtypeStruct((8, width), F32),
        grid=(1,),
        in_specs=[
            pl.BlockSpec((depth, LANES), lambda i: (0, 0)),
            pl.BlockSpec((depth, LANES), lambda i: (0, length // LANES - 1)),
        ],
        out_specs=pl.BlockSpec((8, width), lambda i: (0, 0)),
        compiler_params=pltpu.CompilerParams(vmem_limit_bytes=2 * 1024 * 1024),
    )(x, x)
    if peers == 2:
        before = behind = swap(ends, "seq", 1)
    else:
        up = [(i, (i + 1) % peers) for i in range(peers - 1)]
        down = [(j, i) for i, j in up]
        before, behind = lax.ppermute(ends, "seq", up), lax.ppermute(ends, "seq", down)
    before = jnp.where(me == 0, 0.0, before[2:4])
    behind = jnp.where(me == peers - 1, 0.0, behind[0:2])
    return jnp.concatenate([before, behind], axis=0)


def added(a, b):
    return (a.astype(F32) + b.astype(F32)).astype(BF16)


def chain_sums(count, part, sent, idle):
    me = lax.axis_index("dp")
    end = jnp.logical_or(me == 0, me == 3)
    outer_pairs = [(0, 1), (1, 0), (2, 3), (3, 2)]
    middle_pairs = [(1, 2), (2, 1)]
    last = None
    h, p, s, outer, middle, sums = {}, {}, {}, {}, {}, {}
    for r in range(count + 5):
        if r < count:
            h[r] = part(r, last)
        if r < count + 3:
            value = h.get(r, s.get(r - 3))
            if r in h and r - 3 in s:
                value = jnp.where(end, h[r], s[r - 3])
            last = value = lax.optimization_barrier(value)
            outer[r] = lax.ppermute(value, "dp", outer_pairs)
            last = sent(r, last, sums)
        if r - 1 in outer:
            got = after(outer.pop(r - 1), last)
            if r - 1 < count:
                last = p[r - 1] = lax.optimization_barrier(added(h[r - 1], got))
                middle[r - 1] = lax.ppermute(last, "dp", middle_pairs)
            if r >= 4:
                sums[r - 4] = (got, s[r - 4])
                if r - 1 >= count:
                    last = got
            last = idle(r - 1, last, sums)
        if r - 2 in middle:
            got = after(middle.pop(r - 2), last)
            last = s[r - 2] = lax.optimization_barrier(added(p[r - 2], got))
    return [sums[c] for c in range(count)]


def on_device(block_input, conv_weight, norm_gain, qkv_weight, encoder_grad):
    x = jnp.swapaxes(block_input[0], 0, 1)
    depth, length = x.shape
    taps, _, width = conv_weight.shape
    peers, shards = lax.axis_size("mp"), lax.axis_size("seq")
    bits = [1 << b for b in reversed(range(peers.bit_length() - 1))]
    idx = jnp.stack([lax.axis_index("mp"), lax.axis_index("seq")]).astype(jnp.int32)

    offsets = [0]
    for bit in bits:
        offsets = offsets + [o ^ bit for o in offsets]
    near = [j for j, o in enumerate(offsets) if o < 2]
    far = [j for j, o in enumerate(offsets) if o >= 2]
    half = length // 2
    pick = lambda items, at: [items[j] for j in at]
    scratch = lambda at: [
        pltpu.VMEM((length + 16, len(at) * depth), BF16),
        pltpu.VMEM((taps * width // LANES, length + 2 * EDGE, LANES), F32),
    ]

    blocks = [x]
    for bit in bits[:-1]:
        blocks = blocks + [swap(b, "mp", bit) for b in blocks]
    own = swap(x, "mp", bits[-1])
    edges = edge_rows(x, width)
    payload = jnp.concatenate([edges, norm_gain.reshape(1, -1), jnp.zeros((3, width), F32)], axis=0)
    payloads = [payload] + [swap(payload, "mp", o) for o in offsets[1:]]

    part = jax.ShapeDtypeStruct((half, width), F32)
    even, odd = call(
        functools.partial(first_kernel, pick(offsets, near)),
        (part, part),
        scratch(near),
        24,
        idx, x, own, *pick(payloads, near), conv_weight,
    )
    hold = [even] + pick(payloads, far)
    blocks = blocks + [own] + [swap(after(b, *hold), "mp", bits[-1]) for b in blocks[1:]]
    pair = shards == 2 and peers % shards == 0 and lax.axis_size("dp") == 4
    per = peers // shards if pair else 0
    piece = jax.ShapeDtypeStruct((depth, width), BF16)
    encoded, pre_grad, joined, *first = call(
        functools.partial(second_kernel, offsets, far, per),
        (
            jax.ShapeDtypeStruct((half, width), BF16),
            jax.ShapeDtypeStruct((length + 2 * EDGE, width), F32),
            jax.ShapeDtypeStruct((peers * depth, length + LANES), BF16),
            *([piece] if pair else []),
        ),
        scratch(far)
        + [
            pltpu.VMEM((width // LANES, length, LANES), F32),
            pltpu.VMEM((LANES, width), F32),
        ],
        26,
        idx, *blocks, *payloads, conv_weight, even, odd, encoder_grad[0],
    )
    encs = [encoded]
    for bit in bits[:-1]:
        encs = encs + [swap(e, "mp", bit) for e in encs]

    everything = tuple(range(per))
    pieces_of = lambda k: everything[1:] if k == 0 else (everything if k == 1 else ())

    def gradient(group, hold):
        pieces = [pieces_of(k) for k in group]
        outs = []
        for q in pieces:
            if not pair:
                outs.append([jax.ShapeDtypeStruct((peers * depth, width), BF16)])
                continue
            whole = jax.ShapeDtypeStruct((per * depth, width), BF16)
            outs.append([whole] + ([piece] * len(q) if q else [whole]))
        flat = call(
            functools.partial(grad_kernel, group, depth, per, pieces),
            tuple(o for tap in outs for o in tap),
            [pltpu.VMEM((LANES, width * min(len(group), 2)), F32)],
            24 if len(group) > 2 else 16,
            after(idx, *hold) if hold else idx, joined, pre_grad,
        )
        flat = list(flat)
        taken = [[flat.pop(0) for _ in tap] for tap in outs]
        return [t[0] for t in taken], [t[1:] for t in taken]

    qkv_call = lambda idx, encs: call(
        functools.partial(qkv_kernel, offsets),
        jax.ShapeDtypeStruct((half, qkv_weight.shape[1]), BF16),
        [],
        8,
        idx, *encs, *payloads, qkv_weight,
    )
    if not pair:
        sums = [gradient((k,), [])[0][0] for k in range(taps)]
        sums = [lax.psum_scatter(v, "seq", scatter_dimension=0, tiled=True) for v in sums]
        sums = [lax.psum(v, "dp").astype(F32) for v in sums]
        encs = encs + [swap(e, "mp", bits[-1]) for e in encs]
        return (qkv_call(idx, encs)[None], jnp.stack(sums, axis=1))

    chunks = taps * per
    keep, send, got, relays, done = [], [], {}, [], {}

    def work(group, hold):
        if not group:
            return
        mine, other = gradient(group, hold)
        keep.extend(mine)
        send.extend(other if send else [list(first) + other[0]] + other[1:])

    def launch(tap, hold):
        if tap < taps:
            got[tap] = [swap(after(v, *hold) if hold else v, "seq", 1) for v in send[tap]]

    work((0,), [])
    launch(0, [])
    work(tuple(range(1, min(3, taps))), [keep[-1]])
    launch(1, [])

    def share(c, last):
        tap, row = c // per, c % per
        rows = slice(row * depth, (row + 1) * depth)
        value = got[tap][row] if len(got[tap]) > 1 else got[tap][0][rows]
        return added(keep[tap][rows], value if last is None else after(value, last))

    starts = {(k - 1) * per - 1 - (k == 3): k for k in range(2, taps)}

    def sent(r, last, sums):
        if r < chunks and r in starts:
            launch(starts[r], [last])
        if r == chunks + 2:
            early = len(sums) // per
            parts = [sums[i] for i in range(early * per)]
            parts[0] = (after(parts[0][0], last), parts[0][1])
            last = done["early"] = written(parts, early, 0, None, (taps, per * depth, width))
            done["at"] = early
        return last

    def idle(c, last, sums):
        if c == per + 5:
            held = encs[1:]
            relays.extend([swap(after(e, last, *held), "mp", bits[-1]) for e in encs])
        if c == 0:
            work(tuple(range(3, taps)), [last] + encs[1:])
            last = keep[-1]
        if c == chunks:
            last = done["qkv"] = qkv_call(after(idx, last, *relays), encs + relays)
        return last

    sums = chain_sums(chunks, share, sent, idle)
    shape = (taps, per * depth, width)
    conv_grad, early = done["early"], done["at"]
    me = lax.axis_index("dp")
    end = jnp.logical_or(me == 0, me == lax.axis_size("dp") - 1)
    for k in range(early, taps):
        parts = [(jnp.where(end, got, own),) for got, own in sums[k * per : (k + 1) * per]]
        conv_grad = written(parts, 1, k, conv_grad, shape)
    return (done["qkv"][None], jnp.swapaxes(conv_grad, 0, 1))


def solution(mesh):
    return jax.shard_map(
        on_device,
        mesh=mesh,
        in_specs=(
            P("dp", "seq", "mp"),
            P(None, None, "mp"),
            P("mp"),
            P(None, "mp"),
            P("dp", "seq", "mp"),
        ),
        out_specs=(P("dp", "seq", "mp"), P("seq", None, "mp")),
        check_vma=False,
    )
```
